32 devices in a mesh: seq: 16 (over z, y, x), fsdp: 2 (over core).
Axes of the slice: x: 2, y: 2, z: 4, core: 2. Of those that a mesh axis runs over, the one named last changes fastest.
Arguments:
- tokens: bfloat16 [2, 4096, 2048], P('fsdp', 'seq'), may hold values from -6 to 6
- cotangent: bfloat16 [2, 4096, 2048], P('fsdp', 'seq'), may hold values from -6 to 6
- norm_gain: bfloat16 [2048], P('fsdp'), may hold values from 0.5 to 1.5
- in_weight: bfloat16 [2048, 8192], P('fsdp'), may hold values from -0.125 to 0.125
- conv_weight: bfloat16 [4096, 4], P('fsdp'), may hold values from -3 to 3
- conv_bias: bfloat16 [4096], P('fsdp'), may hold values from -3 to 3
- select_weight: bfloat16 [4096, 160], P('fsdp'), may hold values from -0.09375 to 0.09375
- beta_weight: bfloat16 [4096, 128], P('fsdp'), may hold values from -0.5 to 0.5
- beta_bias: bfloat16 [4096], P('fsdp'), may hold values from -14 to 0
- skip_gain: bfloat16 [4096], P('fsdp'), may hold values from 0.5 to 1.5
- out_weight: bfloat16 [4096, 2048], P('fsdp'), may hold values from -0.25 to 0.25
Outputs:
- layer_out: bfloat16 [2, 4096, 2048], P('fsdp', 'seq')
- token_grad: float32 [2, 4096, 2048], P('fsdp', 'seq')
- gain_grad: float32 [2048], P(('seq', 'fsdp'))
- in_grad: float32 [2048, 8192], P(('seq', 'fsdp'))
- conv_weight_grad: float32 [4096, 4], P(('seq', 'fsdp'))
- conv_bias_grad: float32 [4096], P(('seq', 'fsdp'))
- select_grad: float32 [4096, 160], P(('seq', 'fsdp'))
- beta_weight_grad: float32 [4096, 128], P(('seq', 'fsdp'))
- beta_bias_grad: float32 [4096], P(('seq', 'fsdp'))
- skip_grad: float32 [4096], P(('seq', 'fsdp'))
- out_grad: float32 [4096, 2048], P(('seq', 'fsdp'))
The draws below stay inside these ranges and needn't reach their ends.
All inputs are finite; a program needn't handle non-finite values.
Results may differ from the reference program's by a relative error of at most 0.012.
Values may be sent and summed in bfloat16 or wider, within the bound.
No kernel may reach another device: no remote copies, remote signals or barrier semaphores. Data moves between devices by JAX's collectives and lax.ppermute only.
A program may use at most 320 MiB of HBM per device.

```python
import jax
import jax.numpy as jnp
from jax import lax

D = 2048
INNER = 4096
STATE = 16
CONV = 4
RANK = 128
LENGTH = 4096
SEQ_ALL = 2


def shard_levels(rng, dims, split, smallest, largest):
    factor_of = 1.0
    for dim, blocks in split:
        draws = jax.random.uniform(jax.random.fold_in(jax.random.fold_in(rng, 6), dim), (blocks,), jnp.float32, smallest / len(split), largest / len(split))
        factor_of = factor_of * jnp.repeat(jnp.exp(draws), dims[dim] // blocks).reshape((-1,) + (1,) * (len(dims) - 1 - dim))
    return factor_of


def normal_values(key, extent, width, most, split=(), dtype=jnp.bfloat16):
    result = jax.random.normal(key, extent, jnp.float32) * width
    if len(split) > 0:
        result = shard_levels(key, extent, split, -0.22, 0.18) * result
    return jnp.clip(result, min=-most, max=most).astype(dtype)


def setup_inputs(seed: int = 0) -> dict:
    streams_of = jax.random.split(jax.random.key(seed), 12)
    return {
        "tokens": normal_values(streams_of[0], (SEQ_ALL, LENGTH, D), 1.0, 6.0, ((0, 2), (1, 16))),
        "cotangent": normal_values(streams_of[1], (SEQ_ALL, LENGTH, D), 1.0, 6.0, ((0, 2), (1, 16))),
        "norm_gain": jnp.clip(1.0 + 0.1 * jax.random.normal(streams_of[2], (D,), jnp.float32), 0.5, 1.5).astype(jnp.bfloat16),
        "in_weight": normal_values(streams_of[3], (D, 2 * INNER), D ** -0.5, 0.125, ((0, 2),)),
        "conv_weight": normal_values(streams_of[4], (INNER, CONV), CONV ** -0.5, 3.0, ((0, 2),)),
        "conv_bias": normal_values(streams_of[5], (INNER,), 0.5, 3.0, ((0, 2),)),
        "select_weight": normal_values(streams_of[6], (INNER, RANK + 2 * STATE), INNER ** -0.5, 0.09375, ((0, 2),)),
        "beta_weight": normal_values(streams_of[7], (INNER, RANK), RANK ** -0.5, 0.5, ((0, 2),)),
        "beta_bias": jnp.clip(-14.0 + 14.0 * jax.random.uniform(streams_of[8], (INNER,), jnp.float32) ** shard_levels(streams_of[8], (INNER,), ((0, 2),), -0.2, 0.2), -14.0, 0.0).astype(jnp.bfloat16),
        "skip_gain": jnp.clip(0.5 + 1.0 * jax.random.uniform(streams_of[9], (INNER,), jnp.float32) ** shard_levels(streams_of[9], (INNER,), ((0, 2),), -0.2, 0.2), 0.5, 1.5).astype(jnp.bfloat16),
        "out_weight": normal_values(streams_of[10], (INNER, D), (INNER // 8) ** -0.5, 0.25, ((0, 2),)),
    }


@jax.custom_vjp
def low(v):
    return lax.optimization_barrier(v.astype(jnp.bfloat16)).astype(jnp.float32)

@jax.custom_vjp
def low_back(v):
    return v

def low_keep(v):
    return (low(v), None)

def low_pass(kept, grad):
    return (grad,)

def back_keep(v):
    return (v, None)

def back_low(kept, grad):
    return (low(grad),)
low.defvjp(low_keep, low_pass)
low_back.defvjp(back_keep, back_low)
epsilon = 1e-05
highest = lax.Precision.HIGHEST

def product_of(left, right):
    return jnp.dot(left, right, precision=highest, preferred_element_type=jnp.float32)

def one_step(current, portion):
    rate_now, value_now, key_now, query_now = portion
    fading = 1.0 - key_now[:, None] * key_now[:, None] * rate_now[None, :]
    current = fading * current + key_now[:, None] * (rate_now * value_now)[None, :]
    return (current, lax.optimization_barrier(jnp.sum(current * query_now[:, None], axis=0)))

def recur_block(current, portion):
    return lax.scan(one_step, current, portion)

def sequence_forward(params, sequence):
    norm_gain, in_weight, conv_weight, conv_bias, select_weight, beta_weight, beta_bias, skip_gain, out_weight = params
    variance = lax.optimization_barrier(jnp.mean(sequence * sequence, axis=1, keepdims=True))
    normal = sequence * lax.rsqrt(variance + epsilon)
    normed = low(normal * norm_gain)
    projected = low(low_back(product_of(normed, in_weight)))
    inner_pre = projected[:, :INNER]
    gate_pre = projected[:, INNER:]
    padded = jnp.concatenate([jnp.zeros((CONV - 1, INNER), jnp.float32), inner_pre], axis=0)
    conv_sum = conv_bias + sum((conv_weight[:, tap_index] * padded[tap_index:tap_index + LENGTH] for tap_index in range(CONV)))
    inner_act = low(jax.nn.silu(conv_sum))
    selected = low_back(product_of(inner_act, select_weight))
    low_rank = low(selected[:, :RANK])
    key_vecs = selected[:, RANK:RANK + STATE]
    queries = selected[:, RANK + STATE:]
    logits = low_back(product_of(low_rank, beta_weight.T) + beta_bias)
    beta_gate = jax.nn.sigmoid(logits)
    step_rates = beta_gate / (1.0 + beta_gate * lax.optimization_barrier(jnp.sum(key_vecs * key_vecs, axis=1, keepdims=True)))
    block_count = LENGTH // 64
    portions = (step_rates.reshape(block_count, 64, INNER), inner_act.reshape(block_count, 64, INNER), key_vecs.reshape(block_count, 64, STATE), queries.reshape(block_count, 64, STATE))
    last_state, recurrent = lax.scan(jax.checkpoint(recur_block), jnp.zeros((STATE, INNER), jnp.float32), portions)
    recurrent = recurrent.reshape(LENGTH, INNER)
    branch = low((recurrent + skip_gain * inner_act) * jax.nn.silu(gate_pre))
    return sequence + product_of(branch, out_weight)

def reference(tokens, cotangent, norm_gain, in_weight, conv_weight, conv_bias, select_weight, beta_weight, beta_bias, skip_gain, out_weight):
    params = tuple((weight.astype(jnp.float32) for weight in (norm_gain, in_weight, conv_weight, conv_bias, select_weight, beta_weight, beta_bias, skip_gain, out_weight)))
    inputs_wide = tokens.astype(jnp.float32)

    def whole(weights, sequences):

        def one_sequence(sequence):
            return jax.checkpoint(sequence_forward)(weights, sequence)
        return lax.map(one_sequence, sequences)
    output, pullback = jax.vjp(whole, params, inputs_wide)
    weight_grads, token_grad = pullback(cotangent.astype(jnp.float32))
    return (output.astype(jnp.bfloat16), token_grad, weight_grads[0], weight_grads[1], weight_grads[2], weight_grads[3], weight_grads[4], weight_grads[5], weight_grads[6], weight_grads[7], weight_grads[8])
```

```python
import functools

import jax
import jax.numpy as jnp
from jax import lax
from jax.experimental import pallas as pl
from jax.experimental.pallas import tpu as pltpu
from jax.sharding import PartitionSpec as P

f32 = jnp.float32
bf16 = jnp.bfloat16
epsilon = 1e-05
lanes = 128
group = 4
block_len = 32
both = ("seq", "fsdp")


def matmul(left, right):
    return jnp.dot(left, right, preferred_element_type=f32)


def matmul_nt(left, right):
    return lax.dot_general(left, right, (((1,), (1,)), ((), ())), preferred_element_type=f32)


def matmul_tn(left, right):
    return lax.dot_general(left, right, (((0,), (0,)), ((), ())), preferred_element_type=f32)


def swish_slope(value):
    logistic = jax.nn.sigmoid(value)
    return logistic * (1.0 + value * (1.0 - logistic))


def swap(value):
    return lax.ppermute(value, "fsdp", [(0, 1), (1, 0)])


def at(stacked, index):
    return lax.dynamic_index_in_dim(stacked, index, 0, keepdims=False)


def spread(ref, position, state):
    return jnp.broadcast_to(ref[0, position, pl.ds(state, 1), :], (8, lanes))


def summary_kernel(r_ref, v_ref, d_ref, k_ref, q_ref, k2_ref, p_ref, s_ref, g_ref):
    length, tiles = r_ref.shape[1], r_ref.shape[2]
    states = k_ref.shape[2]
    zero = jnp.zeros((8, lanes), f32)
    one = jnp.ones((8, lanes), f32)
    for tile in range(0, tiles, 8):
        cut = pl.ds(tile, 8)

        def body(position, carry):
            product, current, grads = (list(part) for part in carry)
            rate = r_ref[0, position, cut, :]
            fed = rate * v_ref[0, position, cut, :]
            grad = d_ref[0, position, cut, :]
            for i in range(states):
                fading = 1.0 - spread(k2_ref, position, i) * rate
                current[i] = fading * current[i] + spread(k_ref, position, i) * fed
                product[i] = product[i] * fading
                grads[i] = grads[i] + product[i] * (spread(q_ref, position, i) * grad)
            return (tuple(product), tuple(current), tuple(grads))

        product, current, grads = lax.fori_loop(
            0, length, body, ((one,) * states, (zero,) * states, (zero,) * states), unroll=4
        )
        for i in range(states):
            p_ref[0, i, cut, :] = product[i].astype(p_ref.dtype)
            s_ref[0, i, cut, :] = current[i].astype(s_ref.dtype)
            g_ref[0, i, cut, :] = grads[i].astype(g_ref.dtype)


def forward_kernel(r_ref, v_ref, k_ref, q_ref, k2_ref, init_ref, out_ref, start_ref):
    length, tiles = r_ref.shape[1], r_ref.shape[2]
    states = k_ref.shape[2]
    blocks = start_ref.shape[1]
    span = length // blocks
    for tile in range(0, tiles, 8):
        cut = pl.ds(tile, 8)

        def block(index, current):
            for i in range(states):
                start_ref[0, index, i, cut, :] = current[i]

            def body(step, current):
                current = list(current)
                position = index * span + step
                rate = r_ref[0, position, cut, :]
                fed = rate * v_ref[0, position, cut, :]
                total = None
                for i in range(states):
                    fading = 1.0 - spread(k2_ref, position, i) * rate
                    current[i] = fading * current[i] + spread(k_ref, position, i) * fed
                    term = spread(q_ref, position, i) * current[i]
                    total = term if total is None else total + term
                out_ref[0, position, cut, :] = total
                return tuple(current)

            return lax.fori_loop(0, span, body, current, unroll=4)

        initial = tuple(init_ref[0, i, cut, :] for i in range(states))
        lax.fori_loop(0, blocks, block, initial)


def backward_kernel(
    r_ref,
    v_ref,
    d_ref,
    k_ref,
    q_ref,
    k2_ref,
    start_ref,
    last_ref,
    dr_ref,
    dv_ref,
    dk_ref,
    dq_ref,
    hist,
):
    length, tiles = r_ref.shape[1], r_ref.shape[2]
    states = k_ref.shape[2]
    blocks = start_ref.shape[1]
    span = length // blocks
    cuts = [pl.ds(tile, 8) for tile in range(0, tiles, 8)]

    def block(lap, grads):
        index = blocks - 1 - lap
        base = index * span
        for cut in cuts:

            def ahead(step, current):
                current = list(current)
                position = base + step
                rate = r_ref[0, position, cut, :]
                fed = rate * v_ref[0, position, cut, :]
                for i in range(states):
                    fading = 1.0 - spread(k2_ref, position, i) * rate
                    current[i] = fading * current[i] + spread(k_ref, position, i) * fed
                    hist[step + 1, i, cut, :] = current[i]
                return tuple(current)

            initial = tuple(start_ref[0, index, i, cut, :] for i in range(states))
            for i in range(states):
                hist[0, i, cut, :] = initial[i]
            lax.fori_loop(0, span, ahead, initial, unroll=4)

        def back(lap_step, grads):
            grads = [list(part) for part in grads]
            step = span - 1 - lap_step
            position = base + step
            rates = [r_ref[0, position, cut, :] for cut in cuts]
            values = [v_ref[0, position, cut, :] for cut in cuts]
            outs = [d_ref[0, position, cut, :] for cut in cuts]
            d_rates = [None] * len(cuts)
            d_fed = [None] * len(cuts)
            for i in range(states):
                key = spread(k_ref, position, i)
                query = spread(q_ref, position, i)
                square = spread(k2_ref, position, i)
                key_term = None
                query_term = None
                for n, cut in enumerate(cuts):
                    grad = query * outs[n] + grads[n][i]
                    keyed = key * grad
                    held = key * hist[step, i, cut, :]
                    left = values[n] - held
                    rated = grad * rates[n]
                    part = keyed * left
                    d_rates[n] = part if i == 0 else d_rates[n] + part
                    d_fed[n] = keyed if i == 0 else d_fed[n] + keyed
                    part = rated * (left - held)
                    key_term = part if n == 0 else key_term + part
                    part = outs[n] * hist[step + 1, i, cut, :]
                    query_term = part if n == 0 else query_term + part
                    grads[n][i] = grad - square * rated
                dk_ref[0, position, pl.ds(i, 1), :] = jnp.sum(key_term, axis=0, keepdims=True)
                dq_ref[0, position, pl.ds(i, 1), :] = jnp.sum(query_term, axis=0, keepdims=True)
            for n, cut in enumerate(cuts):
                dr_ref[0, position, cut, :] = d_rates[n]
                dv_ref[0, position, cut, :] = rates[n] * d_fed[n]
            return tuple(tuple(part) for part in grads)

        return lax.fori_loop(0, span, back, grads)

    first = tuple(tuple(last_ref[0, i, cut, :] for i in range(states)) for cut in cuts)
    lax.fori_loop(0, blocks, block, first)


def per_sequence(kernel, name, operands, results, scratch, flops):
    sequences = operands[0].shape[0]

    def spec(array):
        rest = array.shape[1:]
        return pl.BlockSpec((1,) + rest, lambda n: (n,) + (0,) * len(rest))

    moved = sum(a.size * a.dtype.itemsize for a in (*operands, *results))
    return pl.pallas_call(
        kernel,
        grid=(sequences,),
        in_specs=[spec(a) for a in operands],
        out_specs=[spec(a) for a in results],
        out_shape=list(results),
        scratch_shapes=scratch,
        compiler_params=pltpu.CompilerParams(vmem_limit_bytes=56 * 2**20),
        cost_estimate=pl.CostEstimate(flops=flops, bytes_accessed=moved, transcendentals=0),
        name=name,
    )(*operands)


def exchange_states(product, last_state, summary):
    count = lax.axis_size("seq")
    shape = product.shape
    rows = product.size // lanes // count
    packed = jnp.stack([a.reshape(count, rows, lanes) for a in (product, last_state, summary)], 1)
    pieces = lax.all_to_all(packed, "seq", 0, 0).astype(f32)
    state = jnp.zeros((rows, lanes), f32)
    grad = jnp.zeros((rows, lanes), f32)
    states, grads = [], []
    for piece in range(count):
        states.append(state)
        state = pieces[piece, 0] * state + pieces[piece, 1]
        grads.append(grad)
        later = count - 1 - piece
        grad = pieces[later, 0] * grad + pieces[later, 2]
    sent = jnp.stack(
        [jnp.stack([a, b]) for a, b in zip(states, reversed(grads))]
    ).astype(bf16)
    got = lax.all_to_all(sent, "seq", 0, 0).astype(f32)
    return got[:, 0].reshape(shape), got[:, 1].reshape(shape)


def plane_gather(value):
    count = lax.axis_size("seq")
    return [value] + [
        lax.ppermute(value, "seq", [(s, s ^ d) for s in range(count)]) for d in range(1, group)
    ]


def plane_trade(chunk_for):
    count = lax.axis_size("seq")
    mine = lax.axis_index("seq") % group
    return [chunk_for(mine)] + [
        lax.ppermute(
            chunk_for(jnp.bitwise_xor(mine, d)), "seq", [(s, s ^ d) for s in range(count)]
        )
        for d in range(1, group)
    ]


def line_reduce(chunk_for, wanted):
    count = lax.axis_size("seq") // group
    mine = lax.axis_index("seq") // group

    def pairs(step, sign):
        found = []
        for o in range(count):
            target = o + sign * (count - 1 - step)
            if not (0 <= target < count):
                continue
            for p in range(group):
                for c in range(2):
                    if wanted(target, c):
                        source = (o * group + p) * 2 + c
                        found.append((source, source + sign * group * 2))
        return found

    total = chunk_for(mine)
    for sign in (1, -1):
        received = None
        for step in range(count - 1):
            links = pairs(step, sign)
            if not links:
                continue
            target = jnp.clip(mine + sign * (count - 1 - step), 0, count - 1)
            part = chunk_for(target)
            if received is not None:
                part = part + received.astype(f32)
            received = lax.ppermute(part.astype(bf16), both, links)
        total = total + received.astype(f32)
    return total


def owner_reduce(partial):
    half, rows, width = partial.shape
    core = lax.axis_index("fsdp")
    outer = lax.axis_index("seq") // group
    total = line_reduce(
        lambda target: at(partial, jnp.clip(target - core * half, 0, half - 1)),
        lambda target, c: target // half == c,
    )
    pieces = total.reshape(2, rows // 2, width)
    other = swap(at(pieces, 1 - core))
    return jnp.where(outer // half == core, at(pieces, core), other)


def local(
    tokens,
    cotangent,
    norm_gain,
    in_weight,
    conv_weight,
    conv_bias,
    select_weight,
    beta_weight,
    beta_bias,
    skip_gain,
    out_weight,
):
    core = lax.axis_index("fsdp")
    place = lax.axis_index("seq")
    count = lax.axis_size("seq")
    outer_count = count // group
    member = place % group
    length, model = tokens.shape[1], tokens.shape[2]
    half_model = in_weight.shape[0]
    half, taps = conv_weight.shape
    inner = 2 * half
    rank = beta_weight.shape[1]
    states = (select_weight.shape[1] - rank) // 2
    tiles = half // lanes
    rows = 2 * length
    reach = taps - 1

    own_tokens = tokens[0]
    other_tokens = swap(own_tokens)
    own_cot = cotangent[0]
    other_cot = swap(own_cot)
    gain_other = swap(norm_gain)
    low = jnp.where(core == 0, norm_gain, gain_other)
    high = jnp.where(core == 0, gain_other, norm_gain)
    gain_full = jnp.concatenate([low, high]).astype(f32)

    def columns(start):
        return lax.dynamic_slice(in_weight, (0, start), (half_model, half))

    inner_own = columns(core * half)
    gate_own = columns(inner + core * half)
    inner_got = swap(columns((1 - core) * half))
    gate_got = swap(columns(inner + (1 - core) * half))

    def normalise(values):
        wide = values.astype(f32)
        inverse = lax.rsqrt(jnp.mean(wide * wide, axis=1, keepdims=True) + epsilon)
        normal = wide * inverse
        return normal, inverse, (normal * gain_full).astype(bf16)

    normal, inverse, own_normed = normalise(own_tokens)
    other_normed = normalise(other_tokens)[2]
    normed = jnp.concatenate([own_normed, other_normed])
    cot = jnp.concatenate([own_cot, other_cot])
    normed_own = lax.dynamic_slice(normed, (0, core * half_model), (rows, half_model))
    normed_got = lax.dynamic_slice(normed, (0, (1 - core) * half_model), (rows, half_model))

    inner_pre = (matmul(normed_own, inner_own) + matmul(normed_got, inner_got)).astype(bf16)
    inner_pre = inner_pre.reshape(2, length, half)
    edges = lax.ppermute(
        inner_pre[:, length - reach :], "seq", [(s, s + 1) for s in range(count - 1)]
    )
    gate = (matmul(normed_own, gate_own) + matmul(normed_got, gate_got)).astype(bf16).astype(f32)
    d_branch = matmul_nt(cot, out_weight)

    def gathered(own):
        got = [a for a in plane_gather(own)]
        swapped = swap(jnp.stack(got[1:]))
        return got, swapped

    normed_parts, normed_swapped = gathered(own_normed)
    cot_parts, cot_swapped = gathered(own_cot)

    def all_rows(parts, swapped, other):
        pieces = []
        for d in range(group):
            pieces += [parts[d], other if d == 0 else swapped[d - 1]]
        return jnp.concatenate(pieces)

    normed_all = all_rows(normed_parts, normed_swapped, other_normed)
    cot_all = all_rows(cot_parts, cot_swapped, other_cot)

    extended = jnp.concatenate([edges, inner_pre], axis=1)
    conv_wide = conv_weight.astype(f32)
    conv_sum = conv_bias.astype(f32)
    for tap in range(taps):
        conv_sum = conv_sum + conv_wide[:, tap] * extended[:, tap : tap + length].astype(f32)
    conv_sum = conv_sum.reshape(rows, half)
    inner_act = jax.nn.silu(conv_sum).astype(bf16)
    selected = matmul(inner_act, select_weight)
    selected = selected + swap(selected.reshape(2, length, -1)[::-1]).reshape(rows, -1)
    low_rank = selected[:, :rank].astype(bf16)
    keys = selected[:, rank : rank + states]
    queries = selected[:, rank + states :]
    beta_gate = jax.nn.sigmoid(matmul_nt(low_rank, beta_weight) + beta_bias.astype(f32))
    key_norm = jnp.sum(keys * keys, axis=1, keepdims=True)
    denominator = 1.0 + beta_gate * key_norm
    rates = beta_gate / denominator
    values = inner_act.astype(f32)
    swish = jax.nn.silu(gate)
    d_recurrent = d_branch * swish

    def tiled(array):
        return array.reshape(2, length, tiles, lanes)

    def wide(array):
        return jnp.broadcast_to(
            array.reshape(2, length, states, 1), (2, length, states, lanes)
        )

    rate_t, value_t, grad_t = tiled(rates), tiled(values), tiled(d_recurrent)
    key_t, query_t, square_t = wide(keys), wide(queries), wide(keys * keys)
    size = rows * states * half
    state_shape = (2, states, tiles, lanes)
    product, last_state, summary = per_sequence(
        summary_kernel,
        "summary",
        (rate_t, value_t, grad_t, key_t, query_t, square_t),
        [jax.ShapeDtypeStruct(state_shape, bf16)] * 3,
        [],
        9 * size,
    )
    first_state, last_grad = exchange_states(product, last_state, summary)
    blocks = length // block_len
    recurrent, starts = per_sequence(
        forward_kernel,
        "forward",
        (rate_t, value_t, key_t, query_t, square_t, first_state),
        [
            jax.ShapeDtypeStruct((2, length, tiles, lanes), f32),
            jax.ShapeDtypeStruct((2, blocks, states, tiles, lanes), f32),
        ],
        [],
        7 * size,
    )
    skip_wide = skip_gain.astype(f32)
    skip_sum = recurrent.reshape(rows, half) + skip_wide * values
    branch = (skip_sum * swish).astype(bf16)
    d_gate = (d_branch * skip_sum * swish_slope(gate)).astype(bf16)

    owner_rows = 2 * half // count
    branch_split = branch.reshape(rows, outer_count // 2, group, owner_rows)

    def branch_chunk(p):
        return lax.dynamic_index_in_dim(branch_split, p, 2, keepdims=False).reshape(rows, -1)

    branch_all = jnp.concatenate(plane_trade(branch_chunk))
    out_partial = matmul_tn(branch_all, cot_all).reshape(outer_count // 2, owner_rows, model)
    out_grad = owner_reduce(out_partial)

    out_sum = matmul(branch, out_weight)
    layer_out = own_tokens.astype(f32) + (out_sum[:length] + swap(out_sum[length:]))
    layer_out = layer_out.astype(bf16)[None]

    def in_weight_part(grad_half):
        width = half // group

        def chunk(p):
            return lax.dynamic_slice(grad_half, (0, p * width), (rows, width))

        grad_all = jnp.concatenate(plane_trade(chunk))
        partial = matmul_tn(normed_all, grad_all).reshape(outer_count, -1, width)
        total = line_reduce(lambda target: at(partial, target), lambda target, c: True)
        pieces = total.reshape(group, -1, width)
        got = jnp.stack(plane_trade(lambda p: at(pieces, p).astype(bf16)))
        got = got.reshape(group, 2, -1, width)
        mine = lax.dynamic_index_in_dim(got, core, 1, keepdims=False)
        other = swap(lax.dynamic_index_in_dim(got, 1 - core, 1, keepdims=False))
        quarters = []
        for source in (jnp.where(core == 0, mine, other), jnp.where(core == 0, other, mine)):
            quarters += [at(source, jnp.bitwise_xor(member, q)) for q in range(group)]
        return jnp.concatenate(quarters, axis=1).astype(f32)

    gate_grad = in_weight_part(d_gate)
    d_rates, d_values, d_keys, d_queries = per_sequence(
        backward_kernel,
        "backward",
        (rate_t, value_t, grad_t, key_t, query_t, square_t, starts, last_grad),
        [
            jax.ShapeDtypeStruct((2, length, tiles, lanes), f32),
            jax.ShapeDtypeStruct((2, length, tiles, lanes), f32),
            jax.ShapeDtypeStruct((2, length, states, lanes), f32),
            jax.ShapeDtypeStruct((2, length, states, lanes), f32),
        ],
        [pltpu.VMEM((block_len + 1, states, tiles, lanes), f32)],
        23 * size,
    )
    d_rates = d_rates.reshape(rows, half)
    d_values = d_values.reshape(rows, half)
    squared_den = denominator * denominator
    d_norm = jnp.sum(d_rates * (-(beta_gate * beta_gate) / squared_den), axis=1, keepdims=True)
    d_keys = jnp.sum(d_keys, axis=3).reshape(rows, states) + 2.0 * keys * d_norm
    d_queries = jnp.sum(d_queries, axis=3).reshape(rows, states)
    d_logits = (d_rates / squared_den * beta_gate * (1.0 - beta_gate)).astype(bf16)
    d_selected = jnp.concatenate([matmul(d_logits, beta_weight), d_keys, d_queries], axis=1)
    d_selected = d_selected + swap(d_selected.reshape(2, length, -1)[::-1]).reshape(rows, -1)
    d_selected = d_selected.astype(bf16)
    d_inner = d_recurrent * skip_wide + d_values + matmul_nt(d_selected, select_weight)
    d_conv = (d_inner * swish_slope(conv_sum)).reshape(2, length, half)
    later = lax.ppermute(d_conv[:, :reach], "seq", [(s + 1, s) for s in range(count - 1)])
    d_extended = jnp.concatenate([d_conv, later], axis=1)
    d_inner_pre = sum(
        conv_wide[:, tap] * d_extended[:, reach - tap : reach - tap + length]
        for tap in range(taps)
    )
    d_inner_pre = d_inner_pre.reshape(rows, half).astype(bf16)
    inner_grad = in_weight_part(d_inner_pre)
    in_grad = jnp.concatenate([inner_grad, gate_grad], axis=1)

    vectors = [
        jnp.sum(d_conv * extended[:, tap : tap + length].astype(f32), axis=(0, 1))
        for tap in range(taps)
    ]
    vectors += [
        jnp.sum(d_conv, axis=(0, 1)),
        jnp.sum(d_logits.astype(f32), axis=0),
        jnp.sum(d_recurrent * values, axis=0),
    ]
    tail = jnp.stack(vectors, axis=1)
    pack = jnp.concatenate(
        [
            matmul_tn(inner_act, d_selected),
            matmul_tn(d_logits, low_rank),
            tail,
        ],
        axis=1,
    )
    width = pack.shape[1]
    pack = jnp.pad(pack, ((0, 0), (0, -width % lanes)))
    pack = pack.reshape(outer_count // 2, group, owner_rows, -1)
    pack_parts = plane_trade(
        lambda p: lax.dynamic_index_in_dim(pack, p, 1, keepdims=False).astype(bf16)
    )
    pack_sum = sum(a.astype(f32) for a in pack_parts)
    pack_own = owner_reduce(pack_sum)
    edge = select_weight.shape[1]
    select_grad = pack_own[:, :edge]
    beta_weight_grad = pack_own[:, edge : edge + rank]
    edge += rank
    conv_weight_grad = pack_own[:, edge : edge + taps]
    conv_bias_grad = pack_own[:, edge + taps]
    beta_bias_grad = pack_own[:, edge + taps + 1]
    skip_grad = pack_own[:, edge + taps + 2]

    d_normed_own = matmul_nt(d_inner_pre, inner_own) + matmul_nt(d_gate, gate_own)
    d_normed_got = matmul_nt(d_inner_pre, inner_got) + matmul_nt(d_gate, gate_got)
    left = jnp.where(core == 0, d_normed_own, d_normed_got)
    right = jnp.where(core == 0, d_normed_got, d_normed_own)
    d_normed = jnp.concatenate([left, right], axis=1)
    d_normed = d_normed[:length] + swap(d_normed[length:])
    gain_term = jnp.sum(d_normed * normal, axis=0)
    gain_parts = lax.all_to_all(gain_term.reshape(count, 1, -1), "seq", 0, 0)
    gain_sum = jnp.sum(gain_parts, axis=(0, 1)).reshape(2, -1)
    gain_grad = at(gain_sum, core) + swap(at(gain_sum, 1 - core))
    d_normal = d_normed * gain_full
    token_grad = inverse * (
        d_normal - normal * jnp.mean(normal * d_normal, axis=1, keepdims=True)
    ) + own_cot.astype(f32)

    return (
        layer_out,
        token_grad[None],
        gain_grad,
        in_grad,
        conv_weight_grad,
        conv_bias_grad,
        select_grad,
        beta_weight_grad,
        beta_bias_grad,
        skip_grad,
        out_grad,
    )


def solution(mesh):
    in_specs = (
        P("fsdp", "seq", None),
        P("fsdp", "seq", None),
        P("fsdp"),
        P("fsdp", None),
        P("fsdp", None),
        P("fsdp"),
        P("fsdp", None),
        P("fsdp", None),
        P("fsdp"),
        P("fsdp"),
        P("fsdp", None),
    )
    out_specs = (
        P("fsdp", "seq", None),
        P("fsdp", "seq", None),
        P(("seq", "fsdp")),
        P(("seq", "fsdp"), None),
        P(("seq", "fsdp"), None),
        P(("seq", "fsdp")),
        P(("seq", "fsdp"), None),
        P(("seq", "fsdp"), None),
        P(("seq", "fsdp")),
        P(("seq", "fsdp")),
        P(("seq", "fsdp"), None),
    )
    return jax.shard_map(local, mesh=mesh, in_specs=in_specs, out_specs=out_specs, check_vma=False)
```

```python
import functools

import jax
import jax.numpy as jnp
from jax import lax
from jax.experimental import pallas as pl
from jax.experimental.pallas import tpu as pltpu
from jax.sharding import PartitionSpec as P

f32 = jnp.float32
bf16 = jnp.bfloat16
epsilon = 1e-05
lanes = 128
group = 4
span = 16
batch = 8
narrow = 2
seq = ("outer", "member")


def matmul(left, right):
    return jnp.dot(left, right, preferred_element_type=f32)


def matmul_nt(left, right):
    return lax.dot_general(left, right, (((1,), (1,)), ((), ())), preferred_element_type=f32)


def matmul_tn(left, right):
    return lax.dot_general(left, right, (((0,), (0,)), ((), ())), preferred_element_type=f32)


def swish_slope(value):
    logistic = jax.nn.sigmoid(value)
    return logistic * (1.0 + value * (1.0 - logistic))


def together(*values):
    return lax.optimization_barrier(values)


def swap(value):
    return lax.ppermute(value, "fsdp", [(0, 1), (1, 0)])


def at(stacked, index):
    return lax.dynamic_index_in_dim(stacked, index, 0, keepdims=False)


def column(j):
    return pl.ds(j * lanes, lanes)


def eights(ref):
    return ref.reshape(ref.shape[0] // 8, 8, ref.shape[1])


def tall(ref, base, step, j):
    return jnp.broadcast_to(ref[base + step // 8, pl.ds(step % 8, 1), column(j)], (8, lanes))


def spread_columns(sel_ref, first, states, targets):
    length = sel_ref.shape[1]
    for i in range(states):
        value = jnp.broadcast_to(sel_ref[0, :, first + i : first + i + 1], (length, lanes))
        for target, apply in targets:
            target.reshape(length * states, lanes)[pl.ds(i, length, stride=states), :] = apply(
                value
            )


def gate_of(low_rank, weight_ref, bias_ref, j):
    logits = matmul_nt(low_rank, weight_ref[pl.ds(j * lanes, lanes), :])
    return jax.nn.sigmoid(logits + bias_ref[:, column(j)])


def key_sum(sel_ref, rank, states):
    keys = sel_ref[0, :, rank : rank + states]
    return jnp.sum(keys * keys, axis=1, keepdims=True)


def halves(ref, position, states):
    return [ref[position, pl.ds(h, 8), :] for h in range(0, states, 8)]


def summary_kernel(
    sel_ref, act_ref, gate_ref, db_ref, bw_ref, bb_ref, r_ref, f_ref, d_ref, sum_ref, kb, k2b, qb
):
    length, half = act_ref.shape[1], act_ref.shape[2]
    states = kb.shape[1]
    rank = bw_ref.shape[1]
    tiles = half // lanes
    spread_columns(sel_ref, rank, states, [(kb, lambda v: v), (k2b, lambda v: v * v)])
    spread_columns(sel_ref, rank + states, states, [(qb, lambda v: v)])
    norm = key_sum(sel_ref, rank, states)
    low_rank = sel_ref[0, :, :rank].astype(bf16)
    for j in range(tiles):
        beta = gate_of(low_rank, bw_ref, bb_ref, j)
        rate = beta / (1.0 + beta * norm)
        r_ref[0, :, column(j)] = rate
        f_ref[0, :, column(j)] = rate * act_ref[0, :, column(j)].astype(f32)
        gate = gate_ref[0, :, column(j)].astype(f32)
        d_ref[0, :, column(j)] = db_ref[0, :, column(j)] * (gate * jax.nn.sigmoid(gate))
    zero = jnp.zeros((8, lanes), f32)
    one = jnp.ones((8, lanes), f32)
    group = range(states // 8)
    rates, feds, outs = (eights(ref.at[0]) for ref in (r_ref, f_ref, d_ref))
    for first in range(0, tiles, batch):
        places = [(h, j) for j in range(first, first + batch) for h in group]

        def body(lap, carry):
            product, current, grads = (list(part) for part in carry)
            for step in range(8):
                position = pl.multiple_of(lap * 8, 8) + step
                key, square, query = (halves(ref, position, states) for ref in (kb, k2b, qb))
                for n, (h, j) in enumerate(places):
                    fading = 1.0 - square[h] * tall(rates, lap, step, j)
                    current[n] = fading * current[n] + key[h] * tall(feds, lap, step, j)
                    product[n] = product[n] * fading
                    grads[n] = grads[n] + product[n] * (query[h] * tall(outs, lap, step, j))
            return (tuple(product), tuple(current), tuple(grads))

        size = len(places)
        product, current, grads = lax.fori_loop(
            0, length // 8, body, ((one,) * size, (zero,) * size, (zero,) * size)
        )
        for kind, parts in enumerate((product, current, grads)):
            for n in range(0, size, states // 8):
                whole = jnp.concatenate(parts[n : n + states // 8])
                sum_ref[places[n][1], kind] = whole.astype(sum_ref.dtype)


def advance(rates, feds, key, square, base, step, current, places):
    for n, (h, j) in enumerate(places):
        fading = 1.0 - square[h] * tall(rates, base, step, j)
        current[n] = fading * current[n] + key[h] * tall(feds, base, step, j)


def keep(ref, step, states, places, parts):
    by_tile = {}
    for (h, j), part in zip(places, parts):
        by_tile.setdefault(j, []).append(part)
    for j, both in by_tile.items():
        ref[pl.ds(step * states, states), column(j)] = jnp.concatenate(both).astype(bf16)


def forward_kernel(
    sel_ref,
    r_ref,
    f_ref,
    init_ref,
    act_ref,
    gate_ref,
    db_ref,
    qd_ref,
    skip_ref,
    gate_out,
    branch_out,
    branch_ref,
    start_ref,
    term_ref,
    kb,
    k2b,
    state,
    hist,
    held,
):
    length, half = act_ref.shape[1], act_ref.shape[2]
    states = init_ref.shape[2]
    tiles = half // lanes
    rank = sel_ref.shape[2] - 2 * states
    parts = range(states // 8)
    spread_columns(sel_ref, rank, states, [(kb, lambda v: v), (k2b, lambda v: v * v)])
    for j in range(tiles):
        state[:, column(j)] = init_ref[j, 0].astype(f32)
    rates, feds = (eights(ref.at[0]) for ref in (r_ref, f_ref))

    def block(index, carry):
        base = pl.multiple_of(index * span, span)
        start_ref[0, index] = state[...]
        for first in range(0, tiles, batch):
            places = [(h, j) for j in range(first, first + batch) for h in parts]
            current = [state[pl.ds(h * 8, 8), column(j)] for h, j in places]
            for step in range(span):
                key, square = (halves(ref, base + step, states) for ref in (kb, k2b))
                advance(rates, feds, key, square, index * (span // 8), step, current, places)
                keep(hist, step, states, places, current)
            for n, (h, j) in enumerate(places):
                state[pl.ds(h * 8, 8), column(j)] = current[n]
        held[pl.ds(base, span), :] = matmul(qd_ref[0, pl.ds(base, span), :], hist[...])
        return carry

    lax.fori_loop(0, length // span, block, 0)
    width = half // group
    outer_half = branch_out.shape[0] // 2
    owned = branch_out.shape[2] // group
    for j in range(tiles):
        value = act_ref[0, :, column(j)].astype(f32)
        skip_sum = held[:, column(j)] + skip_ref[:, column(j)] * value
        gate = gate_ref[0, :, column(j)].astype(f32)
        logistic = jax.nn.sigmoid(gate)
        swish = gate * logistic
        d_branch = db_ref[0, :, column(j)]
        branch = (skip_sum * swish).astype(bf16)
        d_gate = (d_branch * skip_sum * (logistic * (1.0 + gate * (1.0 - logistic)))).astype(bf16)
        term_ref[0, :, column(j)] = jnp.sum(d_branch * swish * value, axis=0, keepdims=True)
        branch_ref[0, :, column(j)] = branch
        member, offset = divmod(j * lanes, width)
        gate_out[member, :, pl.ds(offset, lanes)] = d_gate
        for inside in range(0, lanes, owned):
            owner = (j * lanes + inside) // owned
            outer = owner % 2 * outer_half + owner // (2 * group)
            offset = owner // 2 % group * owned
            branch_out[outer, :, offset : offset + owned] = branch[:, inside : inside + owned]


def backward_kernel(
    sel_ref,
    r_ref,
    f_ref,
    d_ref,
    act_ref,
    start_ref,
    last_ref,
    kd_ref,
    bw_ref,
    bb_ref,
    skip_ref,
    dlog_ref,
    dsel_ref,
    base_ref,
    bias_ref,
    kb,
    k2b,
    qb,
    v_s,
    before,
    s_hist,
    g_hist,
    w_hist,
    grad_s,
    dr_s,
    dk_s,
    dq_s,
):
    length, half = act_ref.shape[1], act_ref.shape[2]
    states = last_ref.shape[2]
    tiles = half // lanes
    rank = bw_ref.shape[1]
    group = range(states // 8)
    blocks = length // span
    spread_columns(sel_ref, rank, states, [(kb, lambda v: v), (k2b, lambda v: v * v)])
    spread_columns(sel_ref, rank + states, states, [(qb, lambda v: v)])
    v_s[...] = act_ref[0].astype(f32)
    rates, feds, outs, values = (eights(ref) for ref in (r_ref.at[0], f_ref.at[0], d_ref.at[0], v_s))
    for j in range(tiles):
        grad_s[:, column(j)] = last_ref[j, 0].astype(f32)
    wide = span * states
    own = lax.broadcasted_iota(jnp.int32, (span, wide), 1) // states == lax.broadcasted_iota(
        jnp.int32, (span, wide), 0
    )

    def block(lap, carry):
        index = blocks - 1 - lap
        base = pl.multiple_of(index * span, span)
        eight = index * (span // 8)
        rows = pl.ds(base, span)
        diagonal = kd_ref[0, rows, :]
        d_query, d_key = None, None
        for first in range(0, tiles, narrow):
            places = [(h, j) for j in range(first, first + narrow) for h in group]
            cols = pl.ds(first * lanes, narrow * lanes)
            current = [start_ref[0, index, pl.ds(h * 8, 8), column(j)] for h, j in places]
            for step in range(span):
                for n, (h, j) in enumerate(places):
                    before[step, pl.ds(h * 8, 8), column(j)] = current[n]
                key, square = (halves(ref, base + step, states) for ref in (kb, k2b))
                advance(rates, feds, key, square, eight, step, current, places)
                keep(s_hist, step, states, places, current)
            part = matmul_nt(s_hist[:, cols], d_ref[0, rows, cols].astype(bf16))
            d_query = part if d_query is None else d_query + part
        for first in range(0, tiles, narrow):
            places = [(h, j) for j in range(first, first + narrow) for h in group]
            cols = pl.ds(first * lanes, narrow * lanes)
            grads = [grad_s[pl.ds(h * 8, 8), column(j)] for h, j in places]
            for step in reversed(range(span)):
                key, square, query = (halves(ref, base + step, states) for ref in (kb, k2b, qb))
                full, left = [], []
                for n, (h, j) in enumerate(places):
                    grad = grads[n] + query[h] * tall(outs, eight, step, j)
                    kept = key[h] * before[step, pl.ds(h * 8, 8), column(j)]
                    full.append(grad)
                    left.append(grad * (tall(values, eight, step, j) - kept))
                    grads[n] = grad * (1.0 - square[h] * tall(rates, eight, step, j))
                keep(g_hist, step, states, places, full)
                keep(w_hist, step, states, places, left)
            for n, (h, j) in enumerate(places):
                grad_s[pl.ds(h * 8, 8), column(j)] = grads[n]
            block_rates = r_ref[0, rows, cols]
            dr_s[rows, cols] = matmul(diagonal, w_hist[:, cols])
            base_ref[0, rows, cols] = block_rates * matmul(diagonal, g_hist[:, cols])
            part = matmul_nt(w_hist[:, cols], (2.0 * block_rates).astype(bf16)) - matmul_nt(
                g_hist[:, cols], f_ref[0, rows, cols].astype(bf16)
            )
            d_key = part if d_key is None else d_key + part
        dq_s[rows, :] = jnp.where(own, d_query.T, 0.0)
        dk_s[rows, :] = jnp.where(own, d_key.T, 0.0)
        return carry

    lax.fori_loop(0, blocks, block, 0)

    norm = key_sum(sel_ref, rank, states)
    low_rank = sel_ref[0, :, :rank].astype(bf16)
    d_norm = jnp.zeros((length, lanes), f32)
    for j in range(tiles):
        beta = gate_of(low_rank, bw_ref, bb_ref, j)
        inverse = 1.0 / (1.0 + beta * norm)
        rate = beta * inverse
        d_rate = dr_s[:, column(j)]
        d_norm = d_norm - d_rate * (rate * rate)
        d_logits = (d_rate * (inverse * inverse) * (beta * (1.0 - beta))).astype(bf16)
        dlog_ref[0, :, column(j)] = d_logits
        bias_ref[0, :, column(j)] = jnp.sum(d_logits.astype(f32), axis=0, keepdims=True)
        base_ref[0, :, column(j)] += d_ref[0, :, column(j)] * skip_ref[:, column(j)]
    d_norm = 2.0 * jnp.sum(d_norm, axis=1, keepdims=True)
    dsel_ref[0, :, :rank] = matmul(dlog_ref[0], bw_ref[...])

    def folded(ref):
        total = ref[:, :lanes]
        for first in range(lanes, wide, lanes):
            total = total + ref[:, first : first + lanes]
        size = lanes // 2
        while size >= states:
            total = total + pltpu.roll(total, size, 1)
            size //= 2
        return total[:, : 2 * states]

    place = lax.broadcasted_iota(jnp.int32, (length, 2 * states), 1)
    keys = sel_ref[0, :, rank:]
    dsel_ref[0, :, rank:] = jnp.where(place < states, folded(dk_s) + keys * d_norm, folded(dq_s))


def correlate_kernel(taps, split, d_ref, later_ref, w_ref, out_ref, held):
    length, half = d_ref.shape[1], d_ref.shape[2]
    width = half // split
    for j in range(half // lanes):
        held[:length, :] = d_ref[0, :, column(j)]
        held[length:, :] = later_ref[0, :, column(j)]
        total = None
        for tap in range(taps):
            part = w_ref[tap : tap + 1, column(j)] * held[pl.ds(taps - 1 - tap, length), :]
            total = part if total is None else total + part
        member, offset = divmod(j * lanes, width)
        out_ref[member, :, pl.ds(offset, lanes)] = total.astype(bf16)


def copy_kernel(core_ref, in_ref, out_ref):
    out_ref[...] = in_ref[...]


def other_columns(core, in_weight, gate):
    half_model, half = in_weight.shape[0], in_weight.shape[1] // 4
    wide = half // group
    first = 2 * group if gate else 0
    return pl.pallas_call(
        copy_kernel,
        grid_spec=pltpu.PrefetchScalarGridSpec(
            num_scalar_prefetch=1,
            grid=(group,),
            in_specs=[
                pl.BlockSpec(
                    (half_model, wide), lambda n, core: (0, first + group * (1 - core[0]) + n)
                )
            ],
            out_specs=pl.BlockSpec((half_model, wide), lambda n, core: (0, n)),
        ),
        out_shape=shape(half_model, half, dtype=bf16),
        name="columns",
    )(core, in_weight)


def whole_kernel(transposed, left_ref, right_ref, out_ref):
    product = matmul_nt if transposed else matmul
    out_ref[...] = product(left_ref[...], right_ref[...])


def run_product(left, right, transposed, micros):
    rows, depth = left.shape
    columns = right.shape[0 if transposed else 1]
    wide = 4 * lanes
    right_spec = (
        pl.BlockSpec((wide, depth), lambda n: (n, 0))
        if transposed
        else pl.BlockSpec((depth, wide), lambda n: (0, n))
    )
    return pl.pallas_call(
        functools.partial(whole_kernel, transposed),
        grid=(columns // wide,),
        in_specs=[pl.BlockSpec((rows, depth), lambda n: (0, 0)), right_spec],
        out_specs=pl.BlockSpec((rows, wide), lambda n: (0, n)),
        out_shape=shape(rows, columns),
        compiler_params=pltpu.CompilerParams(vmem_limit_bytes=40 * 2**20),
        cost_estimate=pl.CostEstimate(
            flops=int(micros * 1.15e9), bytes_accessed=1 << 20, transcendentals=0
        ),
        name="product",
    )(left, right)


def project_kernel(core_ref, x_ref, own_ref, got_ref, out_ref):
    size = own_ref.shape[0]
    mine = pl.multiple_of(core_ref[0] * size, size)
    other = pl.multiple_of((1 - core_ref[0]) * size, size)
    out_ref[...] = (
        matmul(x_ref[:, pl.ds(mine, size)], own_ref[...])
        + matmul(x_ref[:, pl.ds(other, size)], got_ref[...])
    ).astype(out_ref.dtype)


def run_project(core, normed, in_weight, got, gate, micros):
    rows, model = normed.shape
    half_model, half = got.shape
    wide = half // group
    first = 2 * group if gate else 0
    return pl.pallas_call(
        project_kernel,
        grid_spec=pltpu.PrefetchScalarGridSpec(
            num_scalar_prefetch=1,
            grid=(group,),
            in_specs=[
                pl.BlockSpec((rows, model), lambda n, core: (0, 0)),
                pl.BlockSpec((half_model, wide), lambda n, core: (0, first + group * core[0] + n)),
                pl.BlockSpec((half_model, wide), lambda n, core: (0, n)),
            ],
            out_specs=pl.BlockSpec((rows, wide), lambda n, core: (0, n)),
        ),
        out_shape=shape(rows, half, dtype=bf16),
        compiler_params=pltpu.CompilerParams(vmem_limit_bytes=40 * 2**20),
        cost_estimate=pl.CostEstimate(
            flops=int(micros * 1.15e9), bytes_accessed=2 * half_model * half * 2, transcendentals=0
        ),
        name="project",
    )(core, normed, in_weight, got)


def normed_kernel(
    core_ref,
    inner_ref,
    gate_ref,
    inner_own,
    gate_own,
    inner_got,
    gate_got,
    kept_ref,
    sent_ref,
    inner_flat,
    gate_flat,
    total,
):
    lap = pl.program_id(0)
    length = kept_ref.shape[0]
    wide = inner_ref.shape[2]

    @pl.when(lap == 0)
    def _():
        for n in range(group):
            inner_flat[:, pl.ds(n * wide, wide)] = inner_ref[n]
            gate_flat[:, pl.ds(n * wide, wide)] = gate_ref[n]

    @pl.when(lap < group)
    def _():
        total[...] = matmul_nt(inner_flat[...], inner_own[...]) + matmul_nt(
            gate_flat[...], gate_own[...]
        )

    @pl.when(lap >= group)
    def _():
        total[...] = matmul_nt(inner_flat[...], inner_got[...]) + matmul_nt(
            gate_flat[...], gate_got[...]
        )

    kept_ref[...] = total[pl.ds(pl.multiple_of(core_ref[0] * length, length), length), :]
    sent_ref[...] = total[pl.ds(pl.multiple_of((1 - core_ref[0]) * length, length), length), :]


def run_normed(core, inner_split, gate_split, in_weight, inner_got, gate_got, micros):
    _, rows, wide = inner_split.shape
    half_model, half = inner_got.shape
    high = half_model // group
    result = shape(rows // 2, 2 * half_model)
    whole = pl.BlockSpec((group, rows, wide), lambda n, core: (0, 0, 0))

    def own(offset):
        return pl.BlockSpec(
            (high, half), lambda n, core: (jnp.minimum(n, group - 1), offset + core[0])
        )

    got = pl.BlockSpec((high, half), lambda n, core: (jnp.maximum(n - group, 0), 0))
    out = pl.BlockSpec(
        (rows // 2, high),
        lambda n, core: (0, jnp.where(n < group, n + group * core[0], n - group * core[0])),
    )
    return pl.pallas_call(
        normed_kernel,
        grid_spec=pltpu.PrefetchScalarGridSpec(
            num_scalar_prefetch=1,
            grid=(2 * group,),
            in_specs=[whole, whole, own(0), own(2), got, got],
            out_specs=[out] * 2,
            scratch_shapes=[
                pltpu.VMEM((rows, half), bf16),
                pltpu.VMEM((rows, half), bf16),
                pltpu.VMEM((rows, high), f32),
            ],
        ),
        out_shape=[result] * 2,
        compiler_params=pltpu.CompilerParams(vmem_limit_bytes=50 * 2**20),
        cost_estimate=pl.CostEstimate(
            flops=int(micros * 1.15e9), bytes_accessed=1 << 20, transcendentals=0
        ),
        name="normed",
    )(core, inner_split, gate_split, in_weight, in_weight, inner_got, gate_got)


def pack_kernel(sel_ref, low_ref, act_ref, log_ref, vec_ref, out_ref):
    half = act_ref.shape[1]
    rows = out_ref.shape[3]
    first, second = sel_ref.shape[0], low_ref.shape[0]
    step = 2 * lanes
    tail = out_ref.shape[2] - first - second
    for start in range(0, half, step):
        cols = pl.ds(start, step)
        parts = (
            matmul(sel_ref[...], act_ref[:, cols]).astype(bf16),
            matmul(low_ref[...], log_ref[:, cols]).astype(bf16),
            vec_ref[:tail, cols].astype(bf16),
        )
        size = min(rows, step)
        for inside in range(0, step, size):
            outer, rest = divmod(start + inside, group * rows)
            member, offset = divmod(rest, rows)
            row = 0
            for part in parts:
                out_ref[member, outer, row : row + part.shape[0], offset : offset + size] = part[
                    :, inside : inside + size
                ]
                row += part.shape[0]


def run_pack(selected, low_rank, act, logits, vectors, outer_half, rows, micros):
    height = selected.shape[0] + low_rank.shape[0] + vectors.shape[0]
    operands = (selected, low_rank, act, logits, vectors)
    return pl.pallas_call(
        pack_kernel,
        out_shape=shape(group, outer_half, height, rows, dtype=bf16),
        in_specs=[pl.BlockSpec(memory_space=pltpu.VMEM)] * 5,
        out_specs=pl.BlockSpec(memory_space=pltpu.VMEM),
        compiler_params=pltpu.CompilerParams(vmem_limit_bytes=40 * 2**20),
        cost_estimate=pl.CostEstimate(
            flops=int(micros * 1.15e9), bytes_accessed=1 << 20, transcendentals=0
        ),
        name="pack",
    )(*operands)


def sequence_spec(array):
    rest = array.shape[1:]
    return pl.BlockSpec((1,) + rest, lambda n: (n,) + (0,) * len(rest))


def whole_spec(array):
    zeros = (0,) * array.ndim
    return pl.BlockSpec(array.shape, lambda n: zeros)


def per_sequence(
    kernel, name, operands, shared, results, scratch, micros, out_specs=None, in_specs=None
):
    sequences = operands[0].shape[0]
    moved = sum(a.size * a.dtype.itemsize for a in (*operands, *shared, *results))
    return pl.pallas_call(
        kernel,
        grid=(sequences,),
        in_specs=[(in_specs or {}).get(i, sequence_spec(a)) for i, a in enumerate(operands)]
        + [whole_spec(a) for a in shared],
        out_specs=out_specs or [sequence_spec(a) for a in results],
        out_shape=list(results),
        scratch_shapes=scratch,
        compiler_params=pltpu.CompilerParams(vmem_limit_bytes=58 * 2**20),
        cost_estimate=pl.CostEstimate(
            flops=int(micros * 1.15e9), bytes_accessed=moved, transcendentals=0
        ),
        name=name,
    )(*operands, *shared)


def shape(*dims, dtype=f32):
    return jax.ShapeDtypeStruct(dims, dtype)


def block_diagonal(array):
    length, states = array.shape[1], array.shape[2]
    wide = span * states
    own = jnp.arange(wide)[None, :] // states == jnp.arange(length)[:, None] % span
    return jnp.where(own, jnp.tile(array, (1, 1, span)), 0.0).astype(bf16)


def run_summary(selected, inner_act, gate, d_branch, beta_weight, beta_bias, states):
    count, length, half = inner_act.shape
    natural = shape(count, length, half)
    tiles = half // lanes
    results = [natural] * 3 + [shape(tiles, 3, count * states, lanes, dtype=bf16)]
    specs = [sequence_spec(a) for a in results]
    specs[3] = pl.BlockSpec((tiles, 3, states, lanes), lambda n: (0, 0, n, 0))
    kept = pltpu.VMEM((length, states, lanes), f32)
    return per_sequence(
        summary_kernel,
        "summary",
        (selected, inner_act, gate, d_branch),
        (beta_weight, beta_bias),
        results,
        [kept] * 3,
        25,
        specs,
    )


def run_forward(selected, rates, fed, chain, act, gate, d_branch, skip, outer_count):
    count, length, half = rates.shape
    states = chain.shape[2] // count
    queries = selected[:, :, selected.shape[2] - states :]
    kept = pltpu.VMEM((length, states, lanes), f32)
    results = [
        shape(group, count * length, half // group, dtype=bf16),
        shape(outer_count, count * length, half // outer_count, dtype=bf16),
        shape(count, length, half, dtype=bf16),
        shape(count, length // span, states, half),
        shape(count, 1, half),
    ]
    specs = [sequence_spec(a) for a in results]
    specs[0] = pl.BlockSpec((group, length, half // group), lambda n: (0, n, 0))
    specs[1] = pl.BlockSpec((outer_count, length, half // outer_count), lambda n: (0, n, 0))
    return per_sequence(
        forward_kernel,
        "forward",
        (selected, rates, fed, chain, act, gate, d_branch, block_diagonal(queries)),
        (skip,),
        results,
        [kept] * 2
        + [
            pltpu.VMEM((states, half), f32),
            pltpu.VMEM((span * states, half), bf16),
            pltpu.VMEM((length, half), f32),
        ],
        20,
        specs,
        {3: pl.BlockSpec((half // lanes, 1, states, lanes), lambda n: (0, 0, n, 0))},
    )


def run_backward(
    sequence, into, selected, rates, fed, grads, act, starts, chain, beta_weight, beta_bias, skip
):
    count, length, half = rates.shape
    states = chain.shape[2] // count
    rank = beta_weight.shape[1]
    keys = selected[:, :, rank : rank + states]
    kept = pltpu.VMEM((length, states, lanes), f32)
    natural = pltpu.VMEM((length, half), f32)
    hist = pltpu.VMEM((span * states, half), bf16)
    folded = pltpu.VMEM((length, span * states), f32)
    operands = (selected, rates, fed, grads, act, starts, chain, block_diagonal(keys))
    shared = (beta_weight, beta_bias, skip)
    results = [
        shape(count, length, half, dtype=bf16),
        shape(count, length, selected.shape[2]),
        shape(count, length, half),
        shape(count, 1, half),
    ]

    def spec(array):
        rest = array.shape[1:]
        return pl.BlockSpec((1,) + rest, lambda n: (sequence,) + (0,) * len(rest))

    def kernel(*refs):
        backward_kernel(*refs[len(into) :])

    moved = sum(a.size * a.dtype.itemsize for a in (*operands, *results)) // count
    return pl.pallas_call(
        kernel,
        grid=(1,),
        in_specs=[pl.BlockSpec(memory_space=pl.ANY) for _ in into]
        + [spec(a) for a in operands[:6]]
        + [pl.BlockSpec((half // lanes, 1, states, lanes), lambda n: (0, 1, sequence, 0))]
        + [spec(a) for a in operands[7:]]
        + [whole_spec(a) for a in shared],
        out_specs=[spec(a) for a in results],
        out_shape=results,
        scratch_shapes=[kept] * 3
        + [natural, pltpu.VMEM((span, states, half), f32)]
        + [hist] * 3
        + [pltpu.VMEM((states, half), f32), natural]
        + [folded] * 2,
        input_output_aliases={n: n for n in range(len(into))},
        compiler_params=pltpu.CompilerParams(vmem_limit_bytes=58 * 2**20),
        cost_estimate=pl.CostEstimate(
            flops=int(34 * 1.15e9), bytes_accessed=moved, transcendentals=0
        ),
        name="backward",
    )(*into, *operands, *shared)


def run_correlate(d_conv, later, weights, taps):
    count, length, half = d_conv.shape
    results = [shape(group, count * length, half // group, dtype=bf16)]
    specs = [pl.BlockSpec((group, length, half // group), lambda n: (0, n, 0))]
    later = jnp.pad(later, ((0, 0), (0, 8 - later.shape[1]), (0, 0)))
    return per_sequence(
        functools.partial(correlate_kernel, taps, group),
        "correlate",
        (d_conv, later),
        (weights,),
        results,
        [pltpu.VMEM((length + 8, lanes), f32)],
        4,
        specs,
    )[0]


def chain_kernel(pieces_ref, out_ref):
    count = pieces_ref.shape[0]
    state = jnp.zeros(pieces_ref.shape[2:], f32)
    grad = jnp.zeros(pieces_ref.shape[2:], f32)
    for piece in range(count):
        later = count - 1 - piece
        out_ref[piece, 0] = state.astype(bf16)
        out_ref[later, 1] = grad.astype(bf16)
        state = pieces_ref[piece, 0].astype(f32) * state + pieces_ref[piece, 1].astype(f32)
        grad = pieces_ref[later, 0].astype(f32) * grad + pieces_ref[later, 2].astype(f32)


def exchange_states(sums):
    count = lax.axis_size(seq)
    tiles, kinds, rows, _ = sums.shape
    share = tiles * rows // count
    if share < rows:
        sums = sums.reshape(tiles, kinds, rows // share, share, lanes).swapaxes(1, 2)
    pieces = lax.all_to_all(sums.reshape(count, kinds, share, lanes), seq, 0, 0)
    vmem = pl.BlockSpec(memory_space=pltpu.VMEM)
    sent = pl.pallas_call(
        chain_kernel,
        out_shape=shape(count, 2, share, lanes, dtype=bf16),
        in_specs=[vmem],
        out_specs=vmem,
        name="chain",
    )(pieces)
    got = lax.all_to_all(sent, seq, 0, 0)
    if share < rows:
        got = got.reshape(tiles, rows // share, 2, share, lanes).swapaxes(1, 2)
    return got.reshape(tiles, 2, rows, lanes)


def shifted(value, steps):
    count = lax.axis_size(seq)
    pairs = [(s, s + steps) for s in range(count) if 0 <= s + steps < count]
    return lax.ppermute(value, seq, pairs)


def plane_trade(chunks):
    mine = lax.axis_index("member")
    got = [at(chunks, mine)]
    for d in range(1, group):
        pairs = [(m, m ^ d) for m in range(group)]
        got.append(lax.ppermute(at(chunks, jnp.bitwise_xor(mine, d)), "member", pairs))
    return got


def line_step(partial, bit, axis="outer"):
    count = lax.axis_size(axis)
    mine = (lax.axis_index(axis) // bit) % 2
    split = partial.reshape((-1, 2) + partial.shape[1:])
    sent = lax.dynamic_index_in_dim(split, 1 - mine, 1, keepdims=False).astype(bf16)
    kept = lax.dynamic_index_in_dim(split, mine, 1, keepdims=False)
    got = lax.ppermute(sent, axis, [(o, o ^ bit) for o in range(count)])
    return kept + got.astype(f32)


def line_reduce(partial, bit, axis="outer"):
    while partial.shape[0] > 1:
        partial = line_step(partial, bit, axis)
        bit *= 2
    return partial[0]


def to_owner(rows):
    half = lax.axis_size("outer") // 2
    core = lax.axis_index("fsdp")
    pairs = []
    for o in range(2 * half):
        c = 1 - o // half
        pairs.append((o * 2 + c, (o ^ half) * 2 + 1 - c))
    got = lax.ppermute(rows.astype(bf16), ("outer", "fsdp"), pairs).astype(f32)
    return jnp.where(lax.axis_index("outer") // half == core, rows, got)


def owner_sum(partial):
    partial = line_reduce(partial, 1)
    half = lax.axis_size("outer") // 2
    pairs = []
    for o in range(2 * half):
        c = 1 - o // half
        pairs.append((o * 2 + c, (o ^ half) * 2 + c))
    return partial + lax.ppermute(partial.astype(bf16), ("outer", "fsdp"), pairs).astype(f32)


def owner_part(total, axis):
    core = lax.axis_index("fsdp")
    outer = lax.axis_index("outer")
    half = lax.axis_size("outer") // 2
    size = total.shape[axis] // 2
    mine = lax.dynamic_slice_in_dim(total, core * size, size, axis)
    other = swap(lax.dynamic_slice_in_dim(total, (1 - core) * size, size, axis))
    return jnp.where(outer // half == core, mine, other)


def local(
    tokens,
    cotangent,
    norm_gain,
    in_weight,
    conv_weight,
    conv_bias,
    select_weight,
    beta_weight,
    beta_bias,
    skip_gain,
    out_weight,
):
    core = lax.axis_index("fsdp")
    count = lax.axis_size(seq)
    outer_count = lax.axis_size("outer")
    member = lax.axis_index("member")
    length, model = tokens.shape[1], tokens.shape[2]
    half_model = in_weight.shape[0]
    half, taps = conv_weight.shape
    inner = 2 * half
    rank = beta_weight.shape[1]
    states = (select_weight.shape[1] - rank) // 2
    rows = 2 * length
    reach = taps - 1

    def ordered(mine, other):
        return jnp.where(core == 0, mine, other), jnp.where(core == 0, other, mine)

    own_tokens = tokens[0]
    own_cot = cotangent[0]
    x = jnp.concatenate(ordered(own_tokens, swap(own_tokens)))
    cot = jnp.concatenate(ordered(own_cot, swap(own_cot)))
    gain_full = jnp.concatenate(ordered(norm_gain, swap(norm_gain))).astype(f32)

    core_index = core.astype(jnp.int32).reshape(1)
    inner_got = swap(other_columns(core_index, in_weight, False))
    gate_got = swap(other_columns(core_index, in_weight, True))

    def normalise(values):
        wide = values.astype(f32)
        inverse = lax.rsqrt(jnp.mean(wide * wide, axis=1, keepdims=True) + epsilon)
        normal = wide * inverse
        return normal, inverse, (normal * gain_full).astype(bf16)

    normal, inverse, own_normed = normalise(own_tokens)
    normed = normalise(x)[2]
    normed_all = lax.all_gather(own_normed, ("member", "fsdp"), tiled=True)
    cot_all = lax.all_gather(own_cot, ("outer", "fsdp"), tiled=True)
    d_branch = run_product(cot, out_weight, True, 5)
    inner_pre = run_project(core_index, normed, in_weight, inner_got, False, 5)
    inner_pre = inner_pre.reshape(2, length, half)
    edges = shifted(inner_pre[:, length - reach :], 1)
    gate = run_project(core_index, normed, in_weight, gate_got, True, 5).reshape(2, length, half)
    extended = jnp.concatenate([edges, inner_pre], axis=1)
    conv_wide = conv_weight.astype(f32)
    conv_sum = conv_bias.astype(f32)
    for tap in range(taps):
        conv_sum = conv_sum + conv_wide[:, tap] * extended[:, tap : tap + length].astype(f32)
    conv_sum = conv_sum.reshape(rows, half)
    inner_act = jax.nn.silu(conv_sum).astype(bf16)
    selected = matmul(inner_act, select_weight)
    selected = selected + swap(selected)
    low_rank = selected[:, :rank].astype(bf16)
    beta_shift = beta_bias.astype(f32)[None]
    skip_wide = skip_gain.astype(f32)[None]
    width = half // group
    owner_rows = 2 * half // count
    selected = selected.reshape(2, length, -1)
    act_rows = inner_act.reshape(2, length, half)
    d_branch = d_branch.reshape(2, length, half)
    rates, fed, d_recurrent, sums = run_summary(
        selected, act_rows, gate, d_branch, beta_weight, beta_shift, states
    )
    chain = exchange_states(sums)
    early, branch_split, branch, starts, skip_term = run_forward(
        selected, rates, fed, chain, act_rows, gate, d_branch, skip_wide, outer_count
    )
    early, branch_split, normed_all, cot_all = together(
        early, branch_split, normed_all, cot_all
    )
    branch = branch.reshape(rows, half)

    traded = plane_trade(early)
    branch_all = lax.all_to_all(branch_split, "outer", 0, 0).reshape(outer_count * rows, -1)
    def ordered_members(pieces):
        stacked = jnp.stack(pieces)
        return jnp.concatenate([at(stacked, jnp.bitwise_xor(member, m)) for m in range(group)])

    def in_weight_partial(grad_all):
        return matmul_tn(normed_all, grad_all).reshape(outer_count, -1, width)

    def in_weight_rows(inner_part, gate_part):
        pieces = jnp.concatenate([inner_part, gate_part], axis=1).reshape(group, -1, 2 * width)
        got = lax.all_to_all(pieces, "member", 0, 0).reshape(group, 2, -1, 2 * width)
        mine = lax.dynamic_index_in_dim(got, core, 1, keepdims=False)
        other = swap(lax.dynamic_index_in_dim(got, 1 - core, 1, keepdims=False))
        low, high = ordered(mine, other)
        found = [source[q, :, :width] for source in (low, high) for q in range(group)]
        found += [source[q, :, width:] for source in (low, high) for q in range(group)]
        return jnp.concatenate(found, axis=1).astype(f32)

    operands = (
        selected,
        rates,
        fed,
        d_recurrent,
        act_rows,
        starts,
        chain,
        beta_weight,
        beta_shift,
        skip_wide,
    )
    first_part = list(run_backward(0, (), *operands))
    *traded, first_part[1] = together(*traded, first_part[1])
    early_all = ordered_members(traded)
    gate_partial, *first_part = together(in_weight_partial(early_all), *first_part)
    gate_mid = line_step(gate_partial, 1)
    d_logits, d_selected, d_base, bias_term = run_backward(1, tuple(first_part), *operands)
    d_selected, branch_all, gate_mid = together(d_selected, branch_all, gate_mid)
    d_logits = d_logits.reshape(rows, half)
    d_selected = d_selected.reshape(rows, -1)
    d_selected = d_selected + swap(d_selected)
    d_selected = d_selected.astype(bf16)
    d_inner = d_base.reshape(rows, half) + matmul_nt(d_selected, select_weight)
    d_conv = (d_inner * swish_slope(conv_sum)).reshape(2, length, half)
    later = shifted(d_conv[:, :reach], -1)
    split = run_correlate(d_conv, later, conv_wide.T, taps)
    split, early, branch = together(split, early, branch)
    inner_all = lax.all_to_all(split, "member", 0, 0).reshape(group * rows, width)
    kept, sent = run_normed(core_index, split, early, in_weight, inner_got, gate_got, 10)
    gate_part = line_reduce(gate_mid, 2)
    inner_all, gate_part, kept, sent, branch_all = together(
        inner_all, gate_part, kept, sent, branch_all
    )
    inner_partial = in_weight_partial(inner_all)
    out_partial = matmul_tn(branch_all, cot_all).reshape(group, -1, model)

    out_sum = run_product(branch, out_weight, False, 5)
    out_sum = out_sum.reshape(2, length, model)
    layer_out = own_tokens.astype(f32) + (at(out_sum, core) + swap(at(out_sum, 1 - core)))
    layer_out = layer_out.astype(bf16)[None]

    d_normed = kept + swap(sent)
    gain_term = jnp.sum(d_normed * normal, axis=0)
    gain_term = gain_term.reshape(2, -1)
    gain_term = at(gain_term, core) + swap(at(gain_term, 1 - core))
    d_normal = d_normed * gain_full
    token_grad = inverse * (
        d_normal - normal * jnp.mean(normal * d_normal, axis=1, keepdims=True)
    ) + own_cot.astype(f32)

    vectors = [
        jnp.sum(d_conv * extended[:, tap : tap + length].astype(f32), axis=(0, 1))
        for tap in range(taps)
    ]
    owned = half // count
    vectors += [
        jnp.sum(d_conv, axis=(0, 1)),
        jnp.sum(bias_term, axis=(0, 1)),
        jnp.sum(skip_term, axis=(0, 1)),
        jnp.pad(gain_term.reshape(count, -1), ((0, 0), (0, owned - model // 2 // count))).reshape(-1),
    ]
    vectors = jnp.stack(vectors)
    vectors = jnp.pad(vectors, ((0, -vectors.shape[0] % 16), (0, 0)))
    pack = run_pack(
        d_selected.T, low_rank.T, inner_act, d_logits, vectors, outer_count // 2, owner_rows, 1
    )

    inner_mid = line_step(inner_partial, 1)
    pack_all = lax.all_to_all(pack, "member", 0, 0)
    out_total = line_reduce(out_partial, 1, "member")
    inner_mid, pack_all, out_total = together(inner_mid, pack_all, out_total)
    inner_part = line_reduce(inner_mid, 2)
    pack_own = owner_part(owner_sum(jnp.sum(pack_all.astype(f32), axis=0)), 1).T
    out_grad = to_owner(out_total)
    in_grad = in_weight_rows(inner_part.astype(bf16), gate_part.astype(bf16))
    edge = select_weight.shape[1]
    select_grad = pack_own[:, :edge]
    beta_weight_grad = pack_own[:, edge : edge + rank]
    edge += rank
    conv_weight_grad = pack_own[:, edge : edge + taps]
    conv_bias_grad = pack_own[:, edge + taps]
    beta_bias_grad = pack_own[:, edge + taps + 1]
    skip_grad = pack_own[:, edge + taps + 2]
    gain_grad = pack_own[: model // 2 // count, edge + taps + 3]

    return (
        layer_out,
        token_grad[None],
        gain_grad,
        in_grad,
        conv_weight_grad,
        conv_bias_grad,
        select_grad,
        beta_weight_grad,
        beta_bias_grad,
        skip_grad,
        out_grad,
    )


def solution(mesh):
    devices = mesh.devices
    parts = jax.sharding.Mesh(
        devices.reshape(devices.shape[0] // group, group, devices.shape[1]),
        ("outer", "member", "fsdp"),
    )
    everything = ("outer", "member", "fsdp")
    tokens = P("fsdp", seq, None)
    vector, matrix = P("fsdp"), P("fsdp", None)
    owned, owned_rows = P(everything), P(everything, None)
    in_specs = (
        tokens,
        tokens,
        vector,
        matrix,
        matrix,
        vector,
        matrix,
        matrix,
        vector,
        vector,
        matrix,
    )
    out_specs = (
        tokens,
        tokens,
        owned,
        owned_rows,
        owned_rows,
        owned,
        owned_rows,
        owned_rows,
        owned,
        owned,
        owned_rows,
    )
    return jax.shard_map(
        local, mesh=parts, in_specs=in_specs, out_specs=out_specs, check_vma=False
    )
```

```python
import functools

import jax
import jax.numpy as jnp
from jax import lax
from jax.experimental import pallas as pl
from jax.experimental.pallas import tpu as pltpu
from jax.sharding import PartitionSpec as P

f32 = jnp.float32
bf16 = jnp.bfloat16
epsilon = 1e-05
lanes = 128
group = 4
span = 16
batch = 8
narrow = 2
seq = ("outer", "member")


def matmul(left, right):
    return jnp.dot(left, right, preferred_element_type=f32)


def matmul_nt(left, right):
    return lax.dot_general(left, right, (((1,), (1,)), ((), ())), preferred_element_type=f32)


def matmul_tn(left, right):
    return lax.dot_general(left, right, (((0,), (0,)), ((), ())), preferred_element_type=f32)


def swish_slope(value):
    logistic = jax.nn.sigmoid(value)
    return logistic * (1.0 + value * (1.0 - logistic))


def together(*values):
    return lax.optimization_barrier(values)


def swap(value):
    return lax.ppermute(value, "fsdp", [(0, 1), (1, 0)])


def at(stacked, index):
    return lax.dynamic_index_in_dim(stacked, index, 0, keepdims=False)


def column(j):
    return pl.ds(j * lanes, lanes)


def eights(ref):
    return ref.reshape(ref.shape[0] // 8, 8, ref.shape[1])


def tall(ref, base, step, j):
    return jnp.broadcast_to(ref[base + step // 8, pl.ds(step % 8, 1), column(j)], (8, lanes))


def spread_columns(sel_ref, first, states, targets):
    length = sel_ref.shape[1]
    for i in range(states):
        value = jnp.broadcast_to(sel_ref[0, :, first + i : first + i + 1], (length, lanes))
        for target, apply in targets:
            target.reshape(length * states, lanes)[pl.ds(i, length, stride=states), :] = apply(
                value
            )


def gate_of(low_rank, weight_ref, bias_ref, j):
    logits = matmul_nt(low_rank, weight_ref[pl.ds(j * lanes, lanes), :])
    return jax.nn.sigmoid(logits + bias_ref[:, column(j)])


def key_sum(sel_ref, rank, states):
    keys = sel_ref[0, :, rank : rank + states]
    return jnp.sum(keys * keys, axis=1, keepdims=True)


def halves(ref, position, states):
    return [ref[position, pl.ds(h, 8), :] for h in range(0, states, 8)]


def summary_kernel(
    sel_ref, act_ref, gate_ref, db_ref, bw_ref, bb_ref, r_ref, f_ref, d_ref, sum_ref, kb, k2b, qb
):
    length, half = act_ref.shape[1], act_ref.shape[2]
    states = kb.shape[1]
    rank = bw_ref.shape[1]
    tiles = half // lanes
    spread_columns(sel_ref, rank, states, [(kb, lambda v: v), (k2b, lambda v: v * v)])
    spread_columns(sel_ref, rank + states, states, [(qb, lambda v: v)])
    norm = key_sum(sel_ref, rank, states)
    low_rank = sel_ref[0, :, :rank].astype(bf16)
    for j in range(tiles):
        beta = gate_of(low_rank, bw_ref, bb_ref, j)
        rate = beta / (1.0 + beta * norm)
        r_ref[0, :, column(j)] = rate
        f_ref[0, :, column(j)] = rate * act_ref[0, :, column(j)].astype(f32)
        gate = gate_ref[0, :, column(j)].astype(f32)
        d_ref[0, :, column(j)] = db_ref[0, :, column(j)] * (gate * jax.nn.sigmoid(gate))
    zero = jnp.zeros((8, lanes), f32)
    one = jnp.ones((8, lanes), f32)
    group = range(states // 8)
    rates, feds, outs = (eights(ref.at[0]) for ref in (r_ref, f_ref, d_ref))
    for first in range(0, tiles, batch):
        places = [(h, j) for j in range(first, first + batch) for h in group]

        def body(lap, carry):
            product, current, grads = (list(part) for part in carry)
            for step in range(8):
                position = pl.multiple_of(lap * 8, 8) + step
                key, square, query = (halves(ref, position, states) for ref in (kb, k2b, qb))
                for n, (h, j) in enumerate(places):
                    fading = 1.0 - square[h] * tall(rates, lap, step, j)
                    current[n] = fading * current[n] + key[h] * tall(feds, lap, step, j)
                    product[n] = product[n] * fading
                    grads[n] = grads[n] + product[n] * (query[h] * tall(outs, lap, step, j))
            return (tuple(product), tuple(current), tuple(grads))

        size = len(places)
        product, current, grads = lax.fori_loop(
            0, length // 8, body, ((one,) * size, (zero,) * size, (zero,) * size)
        )
        for kind, parts in enumerate((product, current, grads)):
            for n in range(0, size, states // 8):
                whole = jnp.concatenate(parts[n : n + states // 8])
                sum_ref[places[n][1], kind] = whole.astype(sum_ref.dtype)


def advance(rates, feds, key, square, base, step, current, places):
    for n, (h, j) in enumerate(places):
        fading = 1.0 - square[h] * tall(rates, base, step, j)
        current[n] = fading * current[n] + key[h] * tall(feds, base, step, j)


def keep(ref, step, states, places, parts):
    by_tile = {}
    for (h, j), part in zip(places, parts):
        by_tile.setdefault(j, []).append(part)
    for j, both in by_tile.items():
        ref[pl.ds(step * states, states), column(j)] = jnp.concatenate(both).astype(bf16)


def forward_kernel(
    sel_ref,
    r_ref,
    f_ref,
    init_ref,
    act_ref,
    gate_ref,
    db_ref,
    qd_ref,
    skip_ref,
    gate_out,
    branch_out,
    branch_ref,
    start_ref,
    term_ref,
    kb,
    k2b,
    state,
    hist,
    held,
):
    length, half = act_ref.shape[1], act_ref.shape[2]
    states = init_ref.shape[2]
    tiles = half // lanes
    rank = sel_ref.shape[2] - 2 * states
    parts = range(states // 8)
    spread_columns(sel_ref, rank, states, [(kb, lambda v: v), (k2b, lambda v: v * v)])
    for j in range(tiles):
        state[:, column(j)] = init_ref[j, 0].astype(f32)
    rates, feds = (eights(ref.at[0]) for ref in (r_ref, f_ref))

    def block(index, carry):
        base = pl.multiple_of(index * span, span)
        start_ref[0, index] = state[...]
        for first in range(0, tiles, batch):
            places = [(h, j) for j in range(first, first + batch) for h in parts]
            current = [state[pl.ds(h * 8, 8), column(j)] for h, j in places]
            for step in range(span):
                key, square = (halves(ref, base + step, states) for ref in (kb, k2b))
                advance(rates, feds, key, square, index * (span // 8), step, current, places)
                keep(hist, step, states, places, current)
            for n, (h, j) in enumerate(places):
                state[pl.ds(h * 8, 8), column(j)] = current[n]
        held[pl.ds(base, span), :] = matmul(qd_ref[0, pl.ds(base, span), :], hist[...])
        return carry

    lax.fori_loop(0, length // span, block, 0)
    width = half // group
    outer_half = branch_out.shape[0] // 2
    owned = branch_out.shape[2] // group
    for j in range(tiles):
        value = act_ref[0, :, column(j)].astype(f32)
        skip_sum = held[:, column(j)] + skip_ref[:, column(j)] * value
        gate = gate_ref[0, :, column(j)].astype(f32)
        logistic = jax.nn.sigmoid(gate)
        swish = gate * logistic
        d_branch = db_ref[0, :, column(j)]
        branch = (skip_sum * swish).astype(bf16)
        d_gate = (d_branch * skip_sum * (logistic * (1.0 + gate * (1.0 - logistic)))).astype(bf16)
        term_ref[0, :, column(j)] = jnp.sum(d_branch * swish * value, axis=0, keepdims=True)
        branch_ref[0, :, column(j)] = branch
        member, offset = divmod(j * lanes, width)
        gate_out[member, :, pl.ds(offset, lanes)] = d_gate
        for inside in range(0, lanes, owned):
            owner = (j * lanes + inside) // owned
            outer = owner % 2 * outer_half + owner // (2 * group)
            offset = owner // 2 % group * owned
            branch_out[outer, :, offset : offset + owned] = branch[:, inside : inside + owned]


def backward_kernel(
    sel_ref,
    r_ref,
    f_ref,
    d_ref,
    act_ref,
    start_ref,
    last_ref,
    kd_ref,
    bw_ref,
    bb_ref,
    skip_ref,
    dlog_ref,
    dsel_ref,
    base_ref,
    bias_ref,
    kb,
    k2b,
    qb,
    v_s,
    before,
    s_hist,
    g_hist,
    w_hist,
    grad_s,
    dr_s,
    dk_s,
    dq_s,
):
    length, half = act_ref.shape[1], act_ref.shape[2]
    states = last_ref.shape[2]
    tiles = half // lanes
    rank = bw_ref.shape[1]
    group = range(states // 8)
    blocks = length // span
    spread_columns(sel_ref, rank, states, [(kb, lambda v: v), (k2b, lambda v: v * v)])
    spread_columns(sel_ref, rank + states, states, [(qb, lambda v: v)])
    v_s[...] = act_ref[0].astype(f32)
    rates, feds, outs, values = (eights(ref) for ref in (r_ref.at[0], f_ref.at[0], d_ref.at[0], v_s))
    for j in range(tiles):
        grad_s[:, column(j)] = last_ref[j, 0].astype(f32)
    wide = span * states
    own = lax.broadcasted_iota(jnp.int32, (span, wide), 1) // states == lax.broadcasted_iota(
        jnp.int32, (span, wide), 0
    )

    def block(lap, carry):
        index = blocks - 1 - lap
        base = pl.multiple_of(index * span, span)
        eight = index * (span // 8)
        rows = pl.ds(base, span)
        diagonal = kd_ref[0, rows, :]
        d_query, d_key = None, None
        for first in range(0, tiles, narrow):
            places = [(h, j) for j in range(first, first + narrow) for h in group]
            cols = pl.ds(first * lanes, narrow * lanes)
            current = [start_ref[0, index, pl.ds(h * 8, 8), column(j)] for h, j in places]
            for step in range(span):
                for n, (h, j) in enumerate(places):
                    before[step, pl.ds(h * 8, 8), column(j)] = current[n]
                key, square = (halves(ref, base + step, states) for ref in (kb, k2b))
                advance(rates, feds, key, square, eight, step, current, places)
                keep(s_hist, step, states, places, current)
            part = matmul_nt(s_hist[:, cols], d_ref[0, rows, cols].astype(bf16))
            d_query = part if d_query is None else d_query + part
        for first in range(0, tiles, narrow):
            places = [(h, j) for j in range(first, first + narrow) for h in group]
            cols = pl.ds(first * lanes, narrow * lanes)
            grads = [grad_s[pl.ds(h * 8, 8), column(j)] for h, j in places]
            for step in reversed(range(span)):
                key, square, query = (halves(ref, base + step, states) for ref in (kb, k2b, qb))
                full, left = [], []
                for n, (h, j) in enumerate(places):
                    grad = grads[n] + query[h] * tall(outs, eight, step, j)
                    kept = key[h] * before[step, pl.ds(h * 8, 8), column(j)]
                    full.append(grad)
                    left.append(grad * (tall(values, eight, step, j) - kept))
                    grads[n] = grad * (1.0 - square[h] * tall(rates, eight, step, j))
                keep(g_hist, step, states, places, full)
                keep(w_hist, step, states, places, left)
            for n, (h, j) in enumerate(places):
                grad_s[pl.ds(h * 8, 8), column(j)] = grads[n]
            block_rates = r_ref[0, rows, cols]
            dr_s[rows, cols] = matmul(diagonal, w_hist[:, cols])
            base_ref[0, rows, cols] = block_rates * matmul(diagonal, g_hist[:, cols])
            part = matmul_nt(w_hist[:, cols], (2.0 * block_rates).astype(bf16)) - matmul_nt(
                g_hist[:, cols], f_ref[0, rows, cols].astype(bf16)
            )
            d_key = part if d_key is None else d_key + part
        dq_s[rows, :] = jnp.where(own, d_query.T, 0.0)
        dk_s[rows, :] = jnp.where(own, d_key.T, 0.0)
        return carry

    lax.fori_loop(0, blocks, block, 0)

    norm = key_sum(sel_ref, rank, states)
    low_rank = sel_ref[0, :, :rank].astype(bf16)
    d_norm = jnp.zeros((length, lanes), f32)
    for j in range(tiles):
        beta = gate_of(low_rank, bw_ref, bb_ref, j)
        inverse = 1.0 / (1.0 + beta * norm)
        rate = beta * inverse
        d_rate = dr_s[:, column(j)]
        d_norm = d_norm - d_rate * (rate * rate)
        d_logits = (d_rate * (inverse * inverse) * (beta * (1.0 - beta))).astype(bf16)
        dlog_ref[0, :, column(j)] = d_logits
        bias_ref[0, :, column(j)] = jnp.sum(d_logits.astype(f32), axis=0, keepdims=True)
        base_ref[0, :, column(j)] += d_ref[0, :, column(j)] * skip_ref[:, column(j)]
    d_norm = 2.0 * jnp.sum(d_norm, axis=1, keepdims=True)
    dsel_ref[0, :, :rank] = matmul(dlog_ref[0], bw_ref[...])

    def folded(ref):
        total = ref[:, :lanes]
        for first in range(lanes, wide, lanes):
            total = total + ref[:, first : first + lanes]
        size = lanes // 2
        while size >= states:
            total = total + pltpu.roll(total, size, 1)
            size //= 2
        return total[:, : 2 * states]

    place = lax.broadcasted_iota(jnp.int32, (length, 2 * states), 1)
    keys = sel_ref[0, :, rank:]
    dsel_ref[0, :, rank:] = jnp.where(place < states, folded(dk_s) + keys * d_norm, folded(dq_s))


def correlate_kernel(taps, split, d_ref, later_ref, w_ref, out_ref, held):
    length, half = d_ref.shape[1], d_ref.shape[2]
    width = half // split
    for j in range(half // lanes):
        held[:length, :] = d_ref[0, :, column(j)]
        held[length:, :] = later_ref[0, :, column(j)]
        total = None
        for tap in range(taps):
            part = w_ref[tap : tap + 1, column(j)] * held[pl.ds(taps - 1 - tap, length), :]
            total = part if total is None else total + part
        member, offset = divmod(j * lanes, width)
        out_ref[member, :, pl.ds(offset, lanes)] = total.astype(bf16)


def copy_kernel(core_ref, in_ref, out_ref):
    out_ref[...] = in_ref[...]


def other_columns(core, in_weight, gate):
    half_model, half = in_weight.shape[0], in_weight.shape[1] // 4
    wide = half // group
    first = 2 * group if gate else 0
    return pl.pallas_call(
        copy_kernel,
        grid_spec=pltpu.PrefetchScalarGridSpec(
            num_scalar_prefetch=1,
            grid=(group,),
            in_specs=[
                pl.BlockSpec(
                    (half_model, wide), lambda n, core: (0, first + group * (1 - core[0]) + n)
                )
            ],
            out_specs=pl.BlockSpec((half_model, wide), lambda n, core: (0, n)),
        ),
        out_shape=shape(half_model, half, dtype=bf16),
        name="columns",
    )(core, in_weight)


def whole_kernel(transposed, left_ref, right_ref, out_ref):
    product = matmul_nt if transposed else matmul
    out_ref[...] = product(left_ref[...], right_ref[...])


def run_product(left, right, transposed, micros):
    rows, depth = left.shape
    columns = right.shape[0 if transposed else 1]
    wide = 4 * lanes
    right_spec = (
        pl.BlockSpec((wide, depth), lambda n: (n, 0))
        if transposed
        else pl.BlockSpec((depth, wide), lambda n: (0, n))
    )
    return pl.pallas_call(
        functools.partial(whole_kernel, transposed),
        grid=(columns // wide,),
        in_specs=[pl.BlockSpec((rows, depth), lambda n: (0, 0)), right_spec],
        out_specs=pl.BlockSpec((rows, wide), lambda n: (0, n)),
        out_shape=shape(rows, columns),
        compiler_params=pltpu.CompilerParams(vmem_limit_bytes=40 * 2**20),
        cost_estimate=pl.CostEstimate(
            flops=int(micros * 1.15e9), bytes_accessed=1 << 20, transcendentals=0
        ),
        name="product",
    )(left, right)


def project_kernel(core_ref, x_ref, own_ref, got_ref, out_ref):
    size = own_ref.shape[0]
    mine = pl.multiple_of(core_ref[0] * size, size)
    other = pl.multiple_of((1 - core_ref[0]) * size, size)
    out_ref[...] = (
        matmul(x_ref[:, pl.ds(mine, size)], own_ref[...])
        + matmul(x_ref[:, pl.ds(other, size)], got_ref[...])
    ).astype(out_ref.dtype)


def run_project(core, normed, in_weight, got, gate, micros):
    rows, model = normed.shape
    half_model, half = got.shape
    wide = half // group
    first = 2 * group if gate else 0
    return pl.pallas_call(
        project_kernel,
        grid_spec=pltpu.PrefetchScalarGridSpec(
            num_scalar_prefetch=1,
            grid=(group,),
            in_specs=[
                pl.BlockSpec((rows, model), lambda n, core: (0, 0)),
                pl.BlockSpec((half_model, wide), lambda n, core: (0, first + group * core[0] + n)),
                pl.BlockSpec((half_model, wide), lambda n, core: (0, n)),
            ],
            out_specs=pl.BlockSpec((rows, wide), lambda n, core: (0, n)),
        ),
        out_shape=shape(rows, half, dtype=bf16),
        compiler_params=pltpu.CompilerParams(vmem_limit_bytes=40 * 2**20),
        cost_estimate=pl.CostEstimate(
            flops=int(micros * 1.15e9), bytes_accessed=2 * half_model * half * 2, transcendentals=0
        ),
        name="project",
    )(core, normed, in_weight, got)


def normed_kernel(
    core_ref,
    inner_ref,
    gate_ref,
    inner_own,
    gate_own,
    inner_got,
    gate_got,
    kept_ref,
    sent_ref,
    inner_flat,
    gate_flat,
    total,
):
    lap = pl.program_id(0)
    length = kept_ref.shape[0]
    wide = inner_ref.shape[2]

    @pl.when(lap == 0)
    def _():
        for n in range(group):
            inner_flat[:, pl.ds(n * wide, wide)] = inner_ref[n]
            gate_flat[:, pl.ds(n * wide, wide)] = gate_ref[n]

    @pl.when(lap < group)
    def _():
        total[...] = matmul_nt(inner_flat[...], inner_own[...]) + matmul_nt(
            gate_flat[...], gate_own[...]
        )

    @pl.when(lap >= group)
    def _():
        total[...] = matmul_nt(inner_flat[...], inner_got[...]) + matmul_nt(
            gate_flat[...], gate_got[...]
        )

    kept_ref[...] = total[pl.ds(pl.multiple_of(core_ref[0] * length, length), length), :]
    sent_ref[...] = total[pl.ds(pl.multiple_of((1 - core_ref[0]) * length, length), length), :]


def run_normed(core, inner_split, gate_split, in_weight, inner_got, gate_got, micros):
    _, rows, wide = inner_split.shape
    half_model, half = inner_got.shape
    high = half_model // group
    result = shape(rows // 2, 2 * half_model)
    whole = pl.BlockSpec((group, rows, wide), lambda n, core: (0, 0, 0))

    def own(offset):
        return pl.BlockSpec(
            (high, half), lambda n, core: (jnp.minimum(n, group - 1), offset + core[0])
        )

    got = pl.BlockSpec((high, half), lambda n, core: (jnp.maximum(n - group, 0), 0))
    out = pl.BlockSpec(
        (rows // 2, high),
        lambda n, core: (0, jnp.where(n < group, n + group * core[0], n - group * core[0])),
    )
    return pl.pallas_call(
        normed_kernel,
        grid_spec=pltpu.PrefetchScalarGridSpec(
            num_scalar_prefetch=1,
            grid=(2 * group,),
            in_specs=[whole, whole, own(0), own(2), got, got],
            out_specs=[out] * 2,
            scratch_shapes=[
                pltpu.VMEM((rows, half), bf16),
                pltpu.VMEM((rows, half), bf16),
                pltpu.VMEM((rows, high), f32),
            ],
        ),
        out_shape=[result] * 2,
        compiler_params=pltpu.CompilerParams(vmem_limit_bytes=50 * 2**20),
        cost_estimate=pl.CostEstimate(
            flops=int(micros * 1.15e9), bytes_accessed=1 << 20, transcendentals=0
        ),
        name="normed",
    )(core, inner_split, gate_split, in_weight, in_weight, inner_got, gate_got)


def pack_kernel(sel_ref, low_ref, act_ref, log_ref, vec_ref, out_ref):
    half = act_ref.shape[1]
    rows = out_ref.shape[3]
    first, second = sel_ref.shape[0], low_ref.shape[0]
    step = 2 * lanes
    tail = out_ref.shape[2] - first - second
    for start in range(0, half, step):
        cols = pl.ds(start, step)
        parts = (
            matmul(sel_ref[...], act_ref[:, cols]).astype(bf16),
            matmul(low_ref[...], log_ref[:, cols]).astype(bf16),
            vec_ref[:tail, cols].astype(bf16),
        )
        size = min(rows, step)
        for inside in range(0, step, size):
            outer, rest = divmod(start + inside, group * rows)
            member, offset = divmod(rest, rows)
            row = 0
            for part in parts:
                out_ref[member, outer, row : row + part.shape[0], offset : offset + size] = part[
                    :, inside : inside + size
                ]
                row += part.shape[0]


def run_pack(selected, low_rank, act, logits, vectors, outer_half, rows, micros):
    height = selected.shape[0] + low_rank.shape[0] + vectors.shape[0]
    operands = (selected, low_rank, act, logits, vectors)
    return pl.pallas_call(
        pack_kernel,
        out_shape=shape(group, outer_half, height, rows, dtype=bf16),
        in_specs=[pl.BlockSpec(memory_space=pltpu.VMEM)] * 5,
        out_specs=pl.BlockSpec(memory_space=pltpu.VMEM),
        compiler_params=pltpu.CompilerParams(vmem_limit_bytes=40 * 2**20),
        cost_estimate=pl.CostEstimate(
            flops=int(micros * 1.15e9), bytes_accessed=1 << 20, transcendentals=0
        ),
        name="pack",
    )(*operands)


def sequence_spec(array):
    rest = array.shape[1:]
    return pl.BlockSpec((1,) + rest, lambda n: (n,) + (0,) * len(rest))


def whole_spec(array):
    zeros = (0,) * array.ndim
    return pl.BlockSpec(array.shape, lambda n: zeros)


def per_sequence(
    kernel, name, operands, shared, results, scratch, micros, out_specs=None, in_specs=None
):
    sequences = operands[0].shape[0]
    moved = sum(a.size * a.dtype.itemsize for a in (*operands, *shared, *results))
    return pl.pallas_call(
        kernel,
        grid=(sequences,),
        in_specs=[(in_specs or {}).get(i, sequence_spec(a)) for i, a in enumerate(operands)]
        + [whole_spec(a) for a in shared],
        out_specs=out_specs or [sequence_spec(a) for a in results],
        out_shape=list(results),
        scratch_shapes=scratch,
        compiler_params=pltpu.CompilerParams(vmem_limit_bytes=58 * 2**20),
        cost_estimate=pl.CostEstimate(
            flops=int(micros * 1.15e9), bytes_accessed=moved, transcendentals=0
        ),
        name=name,
    )(*operands, *shared)


def shape(*dims, dtype=f32):
    return jax.ShapeDtypeStruct(dims, dtype)


def block_diagonal(array):
    length, states = array.shape[1], array.shape[2]
    wide = span * states
    own = jnp.arange(wide)[None, :] // states == jnp.arange(length)[:, None] % span
    return jnp.where(own, jnp.tile(array, (1, 1, span)), 0.0).astype(bf16)


def run_summary(selected, inner_act, gate, d_branch, beta_weight, beta_bias, states):
    count, length, half = inner_act.shape
    natural = shape(count, length, half)
    tiles = half // lanes
    results = [natural] * 3 + [shape(tiles, 3, count * states, lanes, dtype=bf16)]
    specs = [sequence_spec(a) for a in results]
    specs[3] = pl.BlockSpec((tiles, 3, states, lanes), lambda n: (0, 0, n, 0))
    kept = pltpu.VMEM((length, states, lanes), f32)
    return per_sequence(
        summary_kernel,
        "summary",
        (selected, inner_act, gate, d_branch),
        (beta_weight, beta_bias),
        results,
        [kept] * 3,
        25,
        specs,
    )


def run_forward(selected, rates, fed, chain, act, gate, d_branch, skip, outer_count):
    count, length, half = rates.shape
    states = chain.shape[2] // count
    queries = selected[:, :, selected.shape[2] - states :]
    kept = pltpu.VMEM((length, states, lanes), f32)
    results = [
        shape(group, count * length, half // group, dtype=bf16),
        shape(outer_count, count * length, half // outer_count, dtype=bf16),
        shape(count, length, half, dtype=bf16),
        shape(count, length // span, states, half),
        shape(count, 1, half),
    ]
    specs = [sequence_spec(a) for a in results]
    specs[0] = pl.BlockSpec((group, length, half // group), lambda n: (0, n, 0))
    specs[1] = pl.BlockSpec((outer_count, length, half // outer_count), lambda n: (0, n, 0))
    return per_sequence(
        forward_kernel,
        "forward",
        (selected, rates, fed, chain, act, gate, d_branch, block_diagonal(queries)),
        (skip,),
        results,
        [kept] * 2
        + [
            pltpu.VMEM((states, half), f32),
            pltpu.VMEM((span * states, half), bf16),
            pltpu.VMEM((length, half), f32),
        ],
        20,
        specs,
        {3: pl.BlockSpec((half // lanes, 1, states, lanes), lambda n: (0, 0, n, 0))},
    )


def run_backward(
    sequence, into, selected, rates, fed, grads, act, starts, chain, beta_weight, beta_bias, skip
):
    count, length, half = rates.shape
    states = chain.shape[2] // count
    rank = beta_weight.shape[1]
    keys = selected[:, :, rank : rank + states]
    kept = pltpu.VMEM((length, states, lanes), f32)
    natural = pltpu.VMEM((length, half), f32)
    hist = pltpu.VMEM((span * states, half), bf16)
    folded = pltpu.VMEM((length, span * states), f32)
    operands = (selected, rates, fed, grads, act, starts, chain, block_diagonal(keys))
    shared = (beta_weight, beta_bias, skip)
    results = [
        shape(count, length, half, dtype=bf16),
        shape(count, length, selected.shape[2]),
        shape(count, length, half),
        shape(count, 1, half),
    ]

    def spec(array):
        rest = array.shape[1:]
        return pl.BlockSpec((1,) + rest, lambda n: (sequence,) + (0,) * len(rest))

    def kernel(*refs):
        backward_kernel(*refs[len(into) :])

    moved = sum(a.size * a.dtype.itemsize for a in (*operands, *results)) // count
    return pl.pallas_call(
        kernel,
        grid=(1,),
        in_specs=[pl.BlockSpec(memory_space=pl.ANY) for _ in into]
        + [spec(a) for a in operands[:6]]
        + [pl.BlockSpec((half // lanes, 1, states, lanes), lambda n: (0, 1, sequence, 0))]
        + [spec(a) for a in operands[7:]]
        + [whole_spec(a) for a in shared],
        out_specs=[spec(a) for a in results],
        out_shape=results,
        scratch_shapes=[kept] * 3
        + [natural, pltpu.VMEM((span, states, half), f32)]
        + [hist] * 3
        + [pltpu.VMEM((states, half), f32), natural]
        + [folded] * 2,
        input_output_aliases={n: n for n in range(len(into))},
        compiler_params=pltpu.CompilerParams(vmem_limit_bytes=58 * 2**20),
        cost_estimate=pl.CostEstimate(
            flops=int(34 * 1.15e9), bytes_accessed=moved, transcendentals=0
        ),
        name="backward",
    )(*into, *operands, *shared)


def run_correlate(d_conv, later, weights, taps):
    count, length, half = d_conv.shape
    results = [shape(group, count * length, half // group, dtype=bf16)]
    specs = [pl.BlockSpec((group, length, half // group), lambda n: (0, n, 0))]
    later = jnp.pad(later, ((0, 0), (0, 8 - later.shape[1]), (0, 0)))
    return per_sequence(
        functools.partial(correlate_kernel, taps, group),
        "correlate",
        (d_conv, later),
        (weights,),
        results,
        [pltpu.VMEM((length + 8, lanes), f32)],
        4,
        specs,
    )[0]


def chain_kernel(pieces_ref, out_ref):
    count = pieces_ref.shape[0]
    state = jnp.zeros(pieces_ref.shape[2:], f32)
    grad = jnp.zeros(pieces_ref.shape[2:], f32)
    for piece in range(count):
        later = count - 1 - piece
        out_ref[piece, 0] = state.astype(bf16)
        out_ref[later, 1] = grad.astype(bf16)
        state = pieces_ref[piece, 0].astype(f32) * state + pieces_ref[piece, 1].astype(f32)
        grad = pieces_ref[later, 0].astype(f32) * grad + pieces_ref[later, 2].astype(f32)


def exchange_states(sums):
    count = lax.axis_size(seq)
    tiles, kinds, rows, _ = sums.shape
    share = tiles * rows // count
    if share < rows:
        sums = sums.reshape(tiles, kinds, rows // share, share, lanes).swapaxes(1, 2)
    pieces = lax.all_to_all(sums.reshape(count, kinds, share, lanes), seq, 0, 0)
    vmem = pl.BlockSpec(memory_space=pltpu.VMEM)
    sent = pl.pallas_call(
        chain_kernel,
        out_shape=shape(count, 2, share, lanes, dtype=bf16),
        in_specs=[vmem],
        out_specs=vmem,
        name="chain",
    )(pieces)
    got = lax.all_to_all(sent, seq, 0, 0)
    if share < rows:
        got = got.reshape(tiles, rows // share, 2, share, lanes).swapaxes(1, 2)
    return got.reshape(tiles, 2, rows, lanes)


def shifted(value, steps):
    count = lax.axis_size(seq)
    pairs = [(s, s + steps) for s in range(count) if 0 <= s + steps < count]
    return lax.ppermute(value, seq, pairs)


def plane_trade(chunks):
    mine = lax.axis_index("member")
    got = [at(chunks, mine)]
    for d in range(1, group):
        pairs = [(m, m ^ d) for m in range(group)]
        got.append(lax.ppermute(at(chunks, jnp.bitwise_xor(mine, d)), "member", pairs))
    return got


def line_step(partial, bit, axis="outer"):
    count = lax.axis_size(axis)
    mine = (lax.axis_index(axis) // bit) % 2
    split = partial.reshape((-1, 2) + partial.shape[1:])
    sent = lax.dynamic_index_in_dim(split, 1 - mine, 1, keepdims=False).astype(bf16)
    kept = lax.dynamic_index_in_dim(split, mine, 1, keepdims=False)
    got = lax.ppermute(sent, axis, [(o, o ^ bit) for o in range(count)])
    return kept + got.astype(f32)


def line_reduce(partial, bit, axis="outer"):
    while partial.shape[0] > 1:
        partial = line_step(partial, bit, axis)
        bit *= 2
    return partial[0]


def to_owner(rows):
    half = lax.axis_size("outer") // 2
    core = lax.axis_index("fsdp")
    pairs = []
    for o in range(2 * half):
        c = 1 - o // half
        pairs.append((o * 2 + c, (o ^ half) * 2 + 1 - c))
    got = lax.ppermute(rows.astype(bf16), ("outer", "fsdp"), pairs).astype(f32)
    return jnp.where(lax.axis_index("outer") // half == core, rows, got)


def owner_sum(partial):
    partial = line_reduce(partial, 1)
    half = lax.axis_size("outer") // 2
    pairs = []
    for o in range(2 * half):
        c = 1 - o // half
        pairs.append((o * 2 + c, (o ^ half) * 2 + c))
    return partial + lax.ppermute(partial.astype(bf16), ("outer", "fsdp"), pairs).astype(f32)


def owner_part(total, axis):
    core = lax.axis_index("fsdp")
    outer = lax.axis_index("outer")
    half = lax.axis_size("outer") // 2
    size = total.shape[axis] // 2
    mine = lax.dynamic_slice_in_dim(total, core * size, size, axis)
    other = swap(lax.dynamic_slice_in_dim(total, (1 - core) * size, size, axis))
    return jnp.where(outer // half == core, mine, other)


def local(
    tokens,
    cotangent,
    norm_gain,
    in_weight,
    conv_weight,
    conv_bias,
    select_weight,
    beta_weight,
    beta_bias,
    skip_gain,
    out_weight,
):
    core = lax.axis_index("fsdp")
    count = lax.axis_size(seq)
    outer_count = lax.axis_size("outer")
    member = lax.axis_index("member")
    length, model = tokens.shape[1], tokens.shape[2]
    half_model = in_weight.shape[0]
    half, taps = conv_weight.shape
    inner = 2 * half
    rank = beta_weight.shape[1]
    states = (select_weight.shape[1] - rank) // 2
    rows = 2 * length
    reach = taps - 1

    def ordered(mine, other):
        return jnp.where(core == 0, mine, other), jnp.where(core == 0, other, mine)

    own_tokens = tokens[0]
    own_cot = cotangent[0]
    x = jnp.concatenate(ordered(own_tokens, swap(own_tokens)))
    cot = jnp.concatenate(ordered(own_cot, swap(own_cot)))
    gain_full = jnp.concatenate(ordered(norm_gain, swap(norm_gain))).astype(f32)

    core_index = core.astype(jnp.int32).reshape(1)
    inner_got = swap(other_columns(core_index, in_weight, False))
    gate_got = swap(other_columns(core_index, in_weight, True))

    def normalise(values):
        wide = values.astype(f32)
        inverse = lax.rsqrt(jnp.mean(wide * wide, axis=1, keepdims=True) + epsilon)
        normal = wide * inverse
        return normal, inverse, (normal * gain_full).astype(bf16)

    normal, inverse, own_normed = normalise(own_tokens)
    normed = normalise(x)[2]
    normed_all = lax.all_gather(own_normed, ("member", "fsdp"), tiled=True)
    cot_all = lax.all_gather(own_cot, ("outer", "fsdp"), tiled=True)
    d_branch = run_product(cot, out_weight, True, 5)
    inner_pre = run_project(core_index, normed, in_weight, inner_got, False, 5)
    inner_pre = inner_pre.reshape(2, length, half)
    edges = shifted(inner_pre[:, length - reach :], 1)
    gate = run_project(core_index, normed, in_weight, gate_got, True, 5).reshape(2, length, half)
    extended = jnp.concatenate([edges, inner_pre], axis=1)
    conv_wide = conv_weight.astype(f32)
    conv_sum = conv_bias.astype(f32)
    for tap in range(taps):
        conv_sum = conv_sum + conv_wide[:, tap] * extended[:, tap : tap + length].astype(f32)
    conv_sum = conv_sum.reshape(rows, half)
    inner_act = jax.nn.silu(conv_sum).astype(bf16)
    selected = matmul(inner_act, select_weight)
    selected = selected + swap(selected)
    low_rank = selected[:, :rank].astype(bf16)
    beta_shift = beta_bias.astype(f32)[None]
    skip_wide = skip_gain.astype(f32)[None]
    width = half // group
    owner_rows = 2 * half // count
    selected = selected.reshape(2, length, -1)
    act_rows = inner_act.reshape(2, length, half)
    d_branch = d_branch.reshape(2, length, half)
    rates, fed, d_recurrent, sums = run_summary(
        selected, act_rows, gate, d_branch, beta_weight, beta_shift, states
    )
    chain = exchange_states(sums)
    early, branch_split, branch, starts, skip_term = run_forward(
        selected, rates, fed, chain, act_rows, gate, d_branch, skip_wide, outer_count
    )
    early, branch_split, normed_all, cot_all = together(
        early, branch_split, normed_all, cot_all
    )
    branch = branch.reshape(rows, half)

    traded = plane_trade(early)
    branch_all = lax.all_to_all(branch_split, "outer", 0, 0).reshape(outer_count * rows, -1)
    def ordered_members(pieces):
        stacked = jnp.stack(pieces)
        return jnp.concatenate([at(stacked, jnp.bitwise_xor(member, m)) for m in range(group)])

    def in_weight_partial(grad_all):
        return matmul_tn(normed_all, grad_all).reshape(outer_count, -1, width)

    def in_weight_rows(inner_part, gate_part):
        pieces = jnp.concatenate([inner_part, gate_part], axis=1).reshape(group, -1, 2 * width)
        got = lax.all_to_all(pieces, "member", 0, 0).reshape(group, 2, -1, 2 * width)
        mine = lax.dynamic_index_in_dim(got, core, 1, keepdims=False)
        other = swap(lax.dynamic_index_in_dim(got, 1 - core, 1, keepdims=False))
        low, high = ordered(mine, other)
        found = [source[q, :, :width] for source in (low, high) for q in range(group)]
        found += [source[q, :, width:] for source in (low, high) for q in range(group)]
        return jnp.concatenate(found, axis=1).astype(f32)

    operands = (
        selected,
        rates,
        fed,
        d_recurrent,
        act_rows,
        starts,
        chain,
        beta_weight,
        beta_shift,
        skip_wide,
    )
    first_part = list(run_backward(0, (), *operands))
    *traded, first_part[1] = together(*traded, first_part[1])
    early_all = ordered_members(traded)
    gate_partial, branch_all, *first_part = together(
        in_weight_partial(early_all), branch_all, *first_part
    )
    gate_mid = line_step(gate_partial, 1)
    d_logits, d_selected, d_base, bias_term = run_backward(1, tuple(first_part), *operands)
    d_selected, gate_mid = together(d_selected, gate_mid)
    d_logits = d_logits.reshape(rows, half)
    d_selected = d_selected.reshape(rows, -1)
    d_selected = d_selected + swap(d_selected)
    d_selected = d_selected.astype(bf16)
    d_inner = d_base.reshape(rows, half) + matmul_nt(d_selected, select_weight)
    d_conv = (d_inner * swish_slope(conv_sum)).reshape(2, length, half)
    later = shifted(d_conv[:, :reach], -1)
    split = run_correlate(d_conv, later, conv_wide.T, taps)
    split, early = together(split, early)
    inner_all = lax.all_to_all(split, "member", 0, 0).reshape(group * rows, width)
    kept, sent = run_normed(core_index, split, early, in_weight, inner_got, gate_got, 10)
    gate_part = line_reduce(gate_mid, 2)
    inner_all, gate_part, kept, sent = together(inner_all, gate_part, kept, sent)
    inner_partial, branch_all, branch = together(in_weight_partial(inner_all), branch_all, branch)
    out_partial = matmul_tn(branch_all, cot_all).reshape(group, -1, model)

    out_sum = run_product(branch, out_weight, False, 5)
    out_sum = out_sum.reshape(2, length, model)
    layer_out = own_tokens.astype(f32) + (at(out_sum, core) + swap(at(out_sum, 1 - core)))
    layer_out = layer_out.astype(bf16)[None]

    d_normed = kept + swap(sent)
    gain_term = jnp.sum(d_normed * normal, axis=0)
    gain_term = gain_term.reshape(2, -1)
    gain_term = at(gain_term, core) + swap(at(gain_term, 1 - core))
    d_normal = d_normed * gain_full
    token_grad = inverse * (
        d_normal - normal * jnp.mean(normal * d_normal, axis=1, keepdims=True)
    ) + own_cot.astype(f32)

    vectors = [
        jnp.sum(d_conv * extended[:, tap : tap + length].astype(f32), axis=(0, 1))
        for tap in range(taps)
    ]
    owned = half // count
    vectors += [
        jnp.sum(d_conv, axis=(0, 1)),
        jnp.sum(bias_term, axis=(0, 1)),
        jnp.sum(skip_term, axis=(0, 1)),
        jnp.pad(gain_term.reshape(count, -1), ((0, 0), (0, owned - model // 2 // count))).reshape(-1),
    ]
    vectors = jnp.stack(vectors)
    vectors = jnp.pad(vectors, ((0, -vectors.shape[0] % 16), (0, 0)))
    pack = run_pack(
        d_selected.T, low_rank.T, inner_act, d_logits, vectors, outer_count // 2, owner_rows, 1
    )

    inner_mid = line_step(inner_partial, 1)
    pack_all = lax.all_to_all(pack, "member", 0, 0)
    out_mid = line_step(out_partial, 1, "member")
    inner_mid, out_mid = together(inner_mid, out_mid)
    inner_part = line_reduce(inner_mid, 2)
    out_total = line_reduce(out_mid, 2, "member")
    inner_part, out_total, pack_all = together(inner_part, out_total, pack_all)
    pack_own = owner_part(owner_sum(jnp.sum(pack_all.astype(f32), axis=0)), 1).T
    out_grad = to_owner(out_total)
    in_grad = in_weight_rows(inner_part.astype(bf16), gate_part.astype(bf16))
    edge = select_weight.shape[1]
    select_grad = pack_own[:, :edge]
    beta_weight_grad = pack_own[:, edge : edge + rank]
    edge += rank
    conv_weight_grad = pack_own[:, edge : edge + taps]
    conv_bias_grad = pack_own[:, edge + taps]
    beta_bias_grad = pack_own[:, edge + taps + 1]
    skip_grad = pack_own[:, edge + taps + 2]
    gain_grad = pack_own[: model // 2 // count, edge + taps + 3]

    return (
        layer_out,
        token_grad[None],
        gain_grad,
        in_grad,
        conv_weight_grad,
        conv_bias_grad,
        select_grad,
        beta_weight_grad,
        beta_bias_grad,
        skip_grad,
        out_grad,
    )


def solution(mesh):
    devices = mesh.devices
    parts = jax.sharding.Mesh(
        devices.reshape(devices.shape[0] // group, group, devices.shape[1]),
        ("outer", "member", "fsdp"),
    )
    everything = ("outer", "member", "fsdp")
    tokens = P("fsdp", seq, None)
    vector, matrix = P("fsdp"), P("fsdp", None)
    owned, owned_rows = P(everything), P(everything, None)
    in_specs = (
        tokens,
        tokens,
        vector,
        matrix,
        matrix,
        vector,
        matrix,
        matrix,
        vector,
        vector,
        matrix,
    )
    out_specs = (
        tokens,
        tokens,
        owned,
        owned_rows,
        owned_rows,
        owned,
        owned_rows,
        owned_rows,
        owned,
        owned,
        owned_rows,
    )
    return jax.shard_map(
        local, mesh=parts, in_specs=in_specs, out_specs=out_specs, check_vma=False
    )
```

```python
import functools

import jax
import jax.numpy as jnp
from jax import lax
from jax.experimental import pallas as pl
from jax.experimental.pallas import tpu as pltpu
from jax.sharding import PartitionSpec as P

f32 = jnp.float32
bf16 = jnp.bfloat16
epsilon = 1e-05
lanes = 128
group = 4
span = 16
batch = 8
narrow = 2
seq = ("outer", "member")


def matmul(left, right):
    return jnp.dot(left, right, preferred_element_type=f32)


def matmul_nt(left, right):
    return lax.dot_general(left, right, (((1,), (1,)), ((), ())), preferred_element_type=f32)


def matmul_tn(left, right):
    return lax.dot_general(left, right, (((0,), (0,)), ((), ())), preferred_element_type=f32)


def swish_slope(value):
    logistic = jax.nn.sigmoid(value)
    return logistic * (1.0 + value * (1.0 - logistic))


def together(*values):
    return lax.optimization_barrier(values)


def swap(value):
    return lax.ppermute(value, "fsdp", [(0, 1), (1, 0)])


def at(stacked, index):
    return lax.dynamic_index_in_dim(stacked, index, 0, keepdims=False)


def column(j):
    return pl.ds(j * lanes, lanes)


def eights(ref):
    return ref.reshape(ref.shape[0] // 8, 8, ref.shape[1])


def tall(ref, base, step, j):
    return jnp.broadcast_to(ref[base + step // 8, pl.ds(step % 8, 1), column(j)], (8, lanes))


def spread_columns(sel_ref, first, states, targets):
    length = sel_ref.shape[1]
    for i in range(states):
        value = jnp.broadcast_to(sel_ref[0, :, first + i : first + i + 1], (length, lanes))
        for target, apply in targets:
            target.reshape(length * states, lanes)[pl.ds(i, length, stride=states), :] = apply(
                value
            )


def gate_of(low_rank, weight_ref, bias_ref, j):
    logits = matmul_nt(low_rank, weight_ref[pl.ds(j * lanes, lanes), :])
    return jax.nn.sigmoid(logits + bias_ref[:, column(j)])


def key_sum(sel_ref, rank, states):
    keys = sel_ref[0, :, rank : rank + states]
    return jnp.sum(keys * keys, axis=1, keepdims=True)


def halves(ref, position, states):
    return [ref[position, pl.ds(h, 8), :] for h in range(0, states, 8)]


def summary_kernel(
    sel_ref, act_ref, gate_ref, db_ref, bw_ref, bb_ref, r_ref, f_ref, d_ref, sum_ref, kb, k2b, qb
):
    length, half = act_ref.shape[1], act_ref.shape[2]
    states = kb.shape[1]
    rank = bw_ref.shape[1]
    tiles = half // lanes
    spread_columns(sel_ref, rank, states, [(kb, lambda v: v), (k2b, lambda v: v * v)])
    spread_columns(sel_ref, rank + states, states, [(qb, lambda v: v)])
    norm = key_sum(sel_ref, rank, states)
    low_rank = sel_ref[0, :, :rank].astype(bf16)
    for j in range(tiles):
        beta = gate_of(low_rank, bw_ref, bb_ref, j)
        rate = beta / (1.0 + beta * norm)
        r_ref[0, :, column(j)] = rate
        f_ref[0, :, column(j)] = rate * act_ref[0, :, column(j)].astype(f32)
        gate = gate_ref[0, :, column(j)].astype(f32)
        d_ref[0, :, column(j)] = db_ref[0, :, column(j)] * (gate * jax.nn.sigmoid(gate))
    zero = jnp.zeros((8, lanes), f32)
    one = jnp.ones((8, lanes), f32)
    group = range(states // 8)
    rates, feds, outs = (eights(ref.at[0]) for ref in (r_ref, f_ref, d_ref))
    for first in range(0, tiles, batch):
        places = [(h, j) for j in range(first, first + batch) for h in group]

        def body(lap, carry):
            product, current, grads = (list(part) for part in carry)
            for step in range(8):
                position = pl.multiple_of(lap * 8, 8) + step
                key, square, query = (halves(ref, position, states) for ref in (kb, k2b, qb))
                for n, (h, j) in enumerate(places):
                    fading = 1.0 - square[h] * tall(rates, lap, step, j)
                    current[n] = fading * current[n] + key[h] * tall(feds, lap, step, j)
                    product[n] = product[n] * fading
                    grads[n] = grads[n] + product[n] * (query[h] * tall(outs, lap, step, j))
            return (tuple(product), tuple(current), tuple(grads))

        size = len(places)
        product, current, grads = lax.fori_loop(
            0, length // 8, body, ((one,) * size, (zero,) * size, (zero,) * size)
        )
        for kind, parts in enumerate((product, current, grads)):
            for n in range(0, size, states // 8):
                whole = jnp.concatenate(parts[n : n + states // 8])
                sum_ref[places[n][1], kind] = whole.astype(sum_ref.dtype)


def advance(rates, feds, key, square, base, step, current, places):
    for n, (h, j) in enumerate(places):
        fading = 1.0 - square[h] * tall(rates, base, step, j)
        current[n] = fading * current[n] + key[h] * tall(feds, base, step, j)


def keep(ref, step, states, places, parts):
    by_tile = {}
    for (h, j), part in zip(places, parts):
        by_tile.setdefault(j, []).append(part)
    for j, both in by_tile.items():
        ref[pl.ds(step * states, states), column(j)] = jnp.concatenate(both).astype(bf16)


def forward_kernel(
    sel_ref,
    r_ref,
    f_ref,
    init_ref,
    act_ref,
    gate_ref,
    db_ref,
    qd_ref,
    skip_ref,
    gate_out,
    branch_out,
    branch_ref,
    start_ref,
    term_ref,
    kb,
    k2b,
    state,
    hist,
    held,
):
    length, half = act_ref.shape[1], act_ref.shape[2]
    states = init_ref.shape[2]
    tiles = half // lanes
    rank = sel_ref.shape[2] - 2 * states
    parts = range(states // 8)
    spread_columns(sel_ref, rank, states, [(kb, lambda v: v), (k2b, lambda v: v * v)])
    for j in range(tiles):
        state[:, column(j)] = init_ref[j, 0].astype(f32)
    rates, feds = (eights(ref.at[0]) for ref in (r_ref, f_ref))

    def block(index, carry):
        base = pl.multiple_of(index * span, span)
        start_ref[0, index] = state[...]
        for first in range(0, tiles, batch):
            places = [(h, j) for j in range(first, first + batch) for h in parts]
            current = [state[pl.ds(h * 8, 8), column(j)] for h, j in places]
            for step in range(span):
                key, square = (halves(ref, base + step, states) for ref in (kb, k2b))
                advance(rates, feds, key, square, index * (span // 8), step, current, places)
                keep(hist, step, states, places, current)
            for n, (h, j) in enumerate(places):
                state[pl.ds(h * 8, 8), column(j)] = current[n]
        held[pl.ds(base, span), :] = matmul(qd_ref[0, pl.ds(base, span), :], hist[...])
        return carry

    lax.fori_loop(0, length // span, block, 0)
    width = half // group
    outer_half = branch_out.shape[0] // 2
    owned = branch_out.shape[2] // group
    for j in range(tiles):
        value = act_ref[0, :, column(j)].astype(f32)
        skip_sum = held[:, column(j)] + skip_ref[:, column(j)] * value
        gate = gate_ref[0, :, column(j)].astype(f32)
        logistic = jax.nn.sigmoid(gate)
        swish = gate * logistic
        d_branch = db_ref[0, :, column(j)]
        branch = (skip_sum * swish).astype(bf16)
        d_gate = (d_branch * skip_sum * (logistic * (1.0 + gate * (1.0 - logistic)))).astype(bf16)
        term_ref[0, :, column(j)] = jnp.sum(d_branch * swish * value, axis=0, keepdims=True)
        branch_ref[0, :, column(j)] = branch
        member, offset = divmod(j * lanes, width)
        gate_out[member, :, pl.ds(offset, lanes)] = d_gate
        for inside in range(0, lanes, owned):
            owner = (j * lanes + inside) // owned
            outer = owner % 2 * outer_half + owner // (2 * group)
            offset = owner // 2 % group * owned
            branch_out[outer, :, offset : offset + owned] = branch[:, inside : inside + owned]


def backward_kernel(
    sel_ref,
    r_ref,
    f_ref,
    d_ref,
    act_ref,
    start_ref,
    last_ref,
    kd_ref,
    bw_ref,
    bb_ref,
    skip_ref,
    dlog_ref,
    dsel_ref,
    base_ref,
    bias_ref,
    kb,
    k2b,
    qb,
    v_s,
    before,
    s_hist,
    g_hist,
    w_hist,
    grad_s,
    dr_s,
    dk_s,
    dq_s,
):
    length, half = act_ref.shape[1], act_ref.shape[2]
    states = last_ref.shape[2]
    tiles = half // lanes
    rank = bw_ref.shape[1]
    group = range(states // 8)
    blocks = length // span
    spread_columns(sel_ref, rank, states, [(kb, lambda v: v), (k2b, lambda v: v * v)])
    spread_columns(sel_ref, rank + states, states, [(qb, lambda v: v)])
    v_s[...] = act_ref[0].astype(f32)
    rates, feds, outs, values = (eights(ref) for ref in (r_ref.at[0], f_ref.at[0], d_ref.at[0], v_s))
    for j in range(tiles):
        grad_s[:, column(j)] = last_ref[j, 0].astype(f32)
    wide = span * states
    own = lax.broadcasted_iota(jnp.int32, (span, wide), 1) // states == lax.broadcasted_iota(
        jnp.int32, (span, wide), 0
    )

    def block(lap, carry):
        index = blocks - 1 - lap
        base = pl.multiple_of(index * span, span)
        eight = index * (span // 8)
        rows = pl.ds(base, span)
        diagonal = kd_ref[0, rows, :]
        d_query, d_key = None, None
        for first in range(0, tiles, narrow):
            places = [(h, j) for j in range(first, first + narrow) for h in group]
            cols = pl.ds(first * lanes, narrow * lanes)
            current = [start_ref[0, index, pl.ds(h * 8, 8), column(j)] for h, j in places]
            for step in range(span):
                for n, (h, j) in enumerate(places):
                    before[step, pl.ds(h * 8, 8), column(j)] = current[n]
                key, square = (halves(ref, base + step, states) for ref in (kb, k2b))
                advance(rates, feds, key, square, eight, step, current, places)
                keep(s_hist, step, states, places, current)
            part = matmul_nt(s_hist[:, cols], d_ref[0, rows, cols].astype(bf16))
            d_query = part if d_query is None else d_query + part
        for first in range(0, tiles, narrow):
            places = [(h, j) for j in range(first, first + narrow) for h in group]
            cols = pl.ds(first * lanes, narrow * lanes)
            grads = [grad_s[pl.ds(h * 8, 8), column(j)] for h, j in places]
            for step in reversed(range(span)):
                key, square, query = (halves(ref, base + step, states) for ref in (kb, k2b, qb))
                full, left = [], []
                for n, (h, j) in enumerate(places):
                    grad = grads[n] + query[h] * tall(outs, eight, step, j)
                    kept = key[h] * before[step, pl.ds(h * 8, 8), column(j)]
                    full.append(grad)
                    left.append(grad * (tall(values, eight, step, j) - kept))
                    grads[n] = grad * (1.0 - square[h] * tall(rates, eight, step, j))
                keep(g_hist, step, states, places, full)
                keep(w_hist, step, states, places, left)
            for n, (h, j) in enumerate(places):
                grad_s[pl.ds(h * 8, 8), column(j)] = grads[n]
            block_rates = r_ref[0, rows, cols]
            dr_s[rows, cols] = matmul(diagonal, w_hist[:, cols])
            base_ref[0, rows, cols] = block_rates * matmul(diagonal, g_hist[:, cols])
            part = matmul_nt(w_hist[:, cols], (2.0 * block_rates).astype(bf16)) - matmul_nt(
                g_hist[:, cols], f_ref[0, rows, cols].astype(bf16)
            )
            d_key = part if d_key is None else d_key + part
        dq_s[rows, :] = jnp.where(own, d_query.T, 0.0)
        dk_s[rows, :] = jnp.where(own, d_key.T, 0.0)
        return carry

    lax.fori_loop(0, blocks, block, 0)

    norm = key_sum(sel_ref, rank, states)
    low_rank = sel_ref[0, :, :rank].astype(bf16)
    d_norm = jnp.zeros((length, lanes), f32)
    for j in range(tiles):
        beta = gate_of(low_rank, bw_ref, bb_ref, j)
        inverse = 1.0 / (1.0 + beta * norm)
        rate = beta * inverse
        d_rate = dr_s[:, column(j)]
        d_norm = d_norm - d_rate * (rate * rate)
        d_logits = (d_rate * (inverse * inverse) * (beta * (1.0 - beta))).astype(bf16)
        dlog_ref[0, :, column(j)] = d_logits
        bias_ref[0, :, column(j)] = jnp.sum(d_logits.astype(f32), axis=0, keepdims=True)
        base_ref[0, :, column(j)] += d_ref[0, :, column(j)] * skip_ref[:, column(j)]
    d_norm = 2.0 * jnp.sum(d_norm, axis=1, keepdims=True)
    dsel_ref[0, :, :rank] = matmul(dlog_ref[0], bw_ref[...])

    def folded(ref):
        total = ref[:, :lanes]
        for first in range(lanes, wide, lanes):
            total = total + ref[:, first : first + lanes]
        size = lanes // 2
        while size >= states:
            total = total + pltpu.roll(total, size, 1)
            size //= 2
        return total[:, : 2 * states]

    place = lax.broadcasted_iota(jnp.int32, (length, 2 * states), 1)
    keys = sel_ref[0, :, rank:]
    dsel_ref[0, :, rank:] = jnp.where(place < states, folded(dk_s) + keys * d_norm, folded(dq_s))


def correlate_kernel(taps, split, d_ref, later_ref, w_ref, out_ref, held):
    length, half = d_ref.shape[1], d_ref.shape[2]
    width = half // split
    for j in range(half // lanes):
        held[:length, :] = d_ref[0, :, column(j)]
        held[length:, :] = later_ref[0, :, column(j)]
        total = None
        for tap in range(taps):
            part = w_ref[tap : tap + 1, column(j)] * held[pl.ds(taps - 1 - tap, length), :]
            total = part if total is None else total + part
        member, offset = divmod(j * lanes, width)
        out_ref[member, :, pl.ds(offset, lanes)] = total.astype(bf16)


def copy_kernel(core_ref, in_ref, out_ref):
    out_ref[...] = in_ref[...]


def other_columns(core, in_weight, gate):
    half_model, half = in_weight.shape[0], in_weight.shape[1] // 4
    wide = half // group
    first = 2 * group if gate else 0
    return pl.pallas_call(
        copy_kernel,
        grid_spec=pltpu.PrefetchScalarGridSpec(
            num_scalar_prefetch=1,
            grid=(group,),
            in_specs=[
                pl.BlockSpec(
                    (half_model, wide), lambda n, core: (0, first + group * (1 - core[0]) + n)
                )
            ],
            out_specs=pl.BlockSpec((half_model, wide), lambda n, core: (0, n)),
        ),
        out_shape=shape(half_model, half, dtype=bf16),
        cost_estimate=pl.CostEstimate(
            flops=int(5 * 1.15e9), bytes_accessed=4 * half_model * half, transcendentals=0
        ),
        name="columns",
    )(core, in_weight)


def whole_kernel(transposed, left_ref, right_ref, out_ref):
    product = matmul_nt if transposed else matmul
    out_ref[...] = product(left_ref[...], right_ref[...])


def run_product(left, right, transposed, micros):
    rows, depth = left.shape
    columns = right.shape[0 if transposed else 1]
    wide = 4 * lanes
    right_spec = (
        pl.BlockSpec((wide, depth), lambda n: (n, 0))
        if transposed
        else pl.BlockSpec((depth, wide), lambda n: (0, n))
    )
    return pl.pallas_call(
        functools.partial(whole_kernel, transposed),
        grid=(columns // wide,),
        in_specs=[pl.BlockSpec((rows, depth), lambda n: (0, 0)), right_spec],
        out_specs=pl.BlockSpec((rows, wide), lambda n: (0, n)),
        out_shape=shape(rows, columns),
        compiler_params=pltpu.CompilerParams(vmem_limit_bytes=40 * 2**20),
        cost_estimate=pl.CostEstimate(
            flops=int(micros * 1.15e9), bytes_accessed=1 << 20, transcendentals=0
        ),
        name="product",
    )(left, right)


def project_kernel(core_ref, x_ref, own_ref, got_ref, out_ref):
    size = own_ref.shape[0]
    mine = pl.multiple_of(core_ref[0] * size, size)
    other = pl.multiple_of((1 - core_ref[0]) * size, size)
    out_ref[...] = (
        matmul(x_ref[:, pl.ds(mine, size)], own_ref[...])
        + matmul(x_ref[:, pl.ds(other, size)], got_ref[...])
    ).astype(out_ref.dtype)


def run_project(core, normed, in_weight, got, gate, micros):
    rows, model = normed.shape
    half_model, half = got.shape
    wide = half // group
    first = 2 * group if gate else 0
    return pl.pallas_call(
        project_kernel,
        grid_spec=pltpu.PrefetchScalarGridSpec(
            num_scalar_prefetch=1,
            grid=(group,),
            in_specs=[
                pl.BlockSpec((rows, model), lambda n, core: (0, 0)),
                pl.BlockSpec((half_model, wide), lambda n, core: (0, first + group * core[0] + n)),
                pl.BlockSpec((half_model, wide), lambda n, core: (0, n)),
            ],
            out_specs=pl.BlockSpec((rows, wide), lambda n, core: (0, n)),
        ),
        out_shape=shape(rows, half, dtype=bf16),
        compiler_params=pltpu.CompilerParams(vmem_limit_bytes=40 * 2**20),
        cost_estimate=pl.CostEstimate(
            flops=int(micros * 1.15e9), bytes_accessed=2 * half_model * half * 2, transcendentals=0
        ),
        name="project",
    )(core, normed, in_weight, got)


def normed_kernel(
    core_ref,
    inner_ref,
    gate_ref,
    inner_own,
    gate_own,
    inner_got,
    gate_got,
    kept_ref,
    sent_ref,
    inner_flat,
    gate_flat,
    total,
):
    lap = pl.program_id(0)
    length = kept_ref.shape[0]
    wide = inner_ref.shape[2]

    @pl.when(lap == 0)
    def _():
        for n in range(group):
            inner_flat[:, pl.ds(n * wide, wide)] = inner_ref[n]
            gate_flat[:, pl.ds(n * wide, wide)] = gate_ref[n]

    @pl.when(lap < group)
    def _():
        total[...] = matmul_nt(inner_flat[...], inner_own[...]) + matmul_nt(
            gate_flat[...], gate_own[...]
        )

    @pl.when(lap >= group)
    def _():
        total[...] = matmul_nt(inner_flat[...], inner_got[...]) + matmul_nt(
            gate_flat[...], gate_got[...]
        )

    kept_ref[...] = total[pl.ds(pl.multiple_of(core_ref[0] * length, length), length), :]
    sent_ref[...] = total[pl.ds(pl.multiple_of((1 - core_ref[0]) * length, length), length), :]


def run_normed(core, inner_split, gate_split, in_weight, inner_got, gate_got, micros):
    _, rows, wide = inner_split.shape
    half_model, half = inner_got.shape
    high = half_model // group
    result = shape(rows // 2, 2 * half_model)
    whole = pl.BlockSpec((group, rows, wide), lambda n, core: (0, 0, 0))

    def own(offset):
        return pl.BlockSpec(
            (high, half), lambda n, core: (jnp.minimum(n, group - 1), offset + core[0])
        )

    got = pl.BlockSpec((high, half), lambda n, core: (jnp.maximum(n - group, 0), 0))
    out = pl.BlockSpec(
        (rows // 2, high),
        lambda n, core: (0, jnp.where(n < group, n + group * core[0], n - group * core[0])),
    )
    return pl.pallas_call(
        normed_kernel,
        grid_spec=pltpu.PrefetchScalarGridSpec(
            num_scalar_prefetch=1,
            grid=(2 * group,),
            in_specs=[whole, whole, own(0), own(2), got, got],
            out_specs=[out] * 2,
            scratch_shapes=[
                pltpu.VMEM((rows, half), bf16),
                pltpu.VMEM((rows, half), bf16),
                pltpu.VMEM((rows, high), f32),
            ],
        ),
        out_shape=[result] * 2,
        compiler_params=pltpu.CompilerParams(vmem_limit_bytes=50 * 2**20),
        cost_estimate=pl.CostEstimate(
            flops=int(micros * 1.15e9), bytes_accessed=1 << 20, transcendentals=0
        ),
        name="normed",
    )(core, inner_split, gate_split, in_weight, in_weight, inner_got, gate_got)


def pack_kernel(sel_ref, low_ref, act_ref, log_ref, vec_ref, out_ref):
    half = act_ref.shape[1]
    rows = out_ref.shape[3]
    first, second = sel_ref.shape[0], low_ref.shape[0]
    step = 2 * lanes
    tail = out_ref.shape[2] - first - second
    for start in range(0, half, step):
        cols = pl.ds(start, step)
        parts = (
            matmul(sel_ref[...], act_ref[:, cols]).astype(bf16),
            matmul(low_ref[...], log_ref[:, cols]).astype(bf16),
            vec_ref[:tail, cols].astype(bf16),
        )
        size = min(rows, step)
        for inside in range(0, step, size):
            outer, rest = divmod(start + inside, group * rows)
            member, offset = divmod(rest, rows)
            row = 0
            for part in parts:
                out_ref[member, outer, row : row + part.shape[0], offset : offset + size] = part[
                    :, inside : inside + size
                ]
                row += part.shape[0]


def run_pack(selected, low_rank, act, logits, vectors, outer_half, rows, micros):
    height = selected.shape[0] + low_rank.shape[0] + vectors.shape[0]
    operands = (selected, low_rank, act, logits, vectors)
    return pl.pallas_call(
        pack_kernel,
        out_shape=shape(group, outer_half, height, rows, dtype=bf16),
        in_specs=[pl.BlockSpec(memory_space=pltpu.VMEM)] * 5,
        out_specs=pl.BlockSpec(memory_space=pltpu.VMEM),
        compiler_params=pltpu.CompilerParams(vmem_limit_bytes=40 * 2**20),
        cost_estimate=pl.CostEstimate(
            flops=int(micros * 1.15e9), bytes_accessed=1 << 20, transcendentals=0
        ),
        name="pack",
    )(*operands)


def sequence_spec(array):
    rest = array.shape[1:]
    return pl.BlockSpec((1,) + rest, lambda n: (n,) + (0,) * len(rest))


def whole_spec(array):
    zeros = (0,) * array.ndim
    return pl.BlockSpec(array.shape, lambda n: zeros)


def per_sequence(
    kernel, name, operands, shared, results, scratch, micros, out_specs=None, in_specs=None
):
    sequences = operands[0].shape[0]
    moved = sum(a.size * a.dtype.itemsize for a in (*operands, *shared, *results))
    return pl.pallas_call(
        kernel,
        grid=(sequences,),
        in_specs=[(in_specs or {}).get(i, sequence_spec(a)) for i, a in enumerate(operands)]
        + [whole_spec(a) for a in shared],
        out_specs=out_specs or [sequence_spec(a) for a in results],
        out_shape=list(results),
        scratch_shapes=scratch,
        compiler_params=pltpu.CompilerParams(vmem_limit_bytes=58 * 2**20),
        cost_estimate=pl.CostEstimate(
            flops=int(micros * 1.15e9), bytes_accessed=moved, transcendentals=0
        ),
        name=name,
    )(*operands, *shared)


def shape(*dims, dtype=f32):
    return jax.ShapeDtypeStruct(dims, dtype)


def block_diagonal(array):
    length, states = array.shape[1], array.shape[2]
    wide = span * states
    own = jnp.arange(wide)[None, :] // states == jnp.arange(length)[:, None] % span
    return jnp.where(own, jnp.tile(array, (1, 1, span)), 0.0).astype(bf16)


def run_summary(selected, inner_act, gate, d_branch, beta_weight, beta_bias, states):
    count, length, half = inner_act.shape
    natural = shape(count, length, half)
    tiles = half // lanes
    results = [natural] * 3 + [shape(tiles, 3, count * states, lanes, dtype=bf16)]
    specs = [sequence_spec(a) for a in results]
    specs[3] = pl.BlockSpec((tiles, 3, states, lanes), lambda n: (0, 0, n, 0))
    kept = pltpu.VMEM((length, states, lanes), f32)
    return per_sequence(
        summary_kernel,
        "summary",
        (selected, inner_act, gate, d_branch),
        (beta_weight, beta_bias),
        results,
        [kept] * 3,
        25,
        specs,
    )


def run_forward(selected, rates, fed, chain, act, gate, d_branch, skip, outer_count):
    count, length, half = rates.shape
    states = chain.shape[2] // count
    queries = selected[:, :, selected.shape[2] - states :]
    kept = pltpu.VMEM((length, states, lanes), f32)
    results = [
        shape(group, count * length, half // group, dtype=bf16),
        shape(outer_count, count * length, half // outer_count, dtype=bf16),
        shape(count, length, half, dtype=bf16),
        shape(count, length // span, states, half),
        shape(count, 1, half),
    ]
    specs = [sequence_spec(a) for a in results]
    specs[0] = pl.BlockSpec((group, length, half // group), lambda n: (0, n, 0))
    specs[1] = pl.BlockSpec((outer_count, length, half // outer_count), lambda n: (0, n, 0))
    return per_sequence(
        forward_kernel,
        "forward",
        (selected, rates, fed, chain, act, gate, d_branch, block_diagonal(queries)),
        (skip,),
        results,
        [kept] * 2
        + [
            pltpu.VMEM((states, half), f32),
            pltpu.VMEM((span * states, half), bf16),
            pltpu.VMEM((length, half), f32),
        ],
        20,
        specs,
        {3: pl.BlockSpec((half // lanes, 1, states, lanes), lambda n: (0, 0, n, 0))},
    )


def run_backward(
    sequence, into, selected, rates, fed, grads, act, starts, chain, beta_weight, beta_bias, skip
):
    count, length, half = rates.shape
    states = chain.shape[2] // count
    rank = beta_weight.shape[1]
    keys = selected[:, :, rank : rank + states]
    kept = pltpu.VMEM((length, states, lanes), f32)
    natural = pltpu.VMEM((length, half), f32)
    hist = pltpu.VMEM((span * states, half), bf16)
    folded = pltpu.VMEM((length, span * states), f32)
    operands = (selected, rates, fed, grads, act, starts, chain, block_diagonal(keys))
    shared = (beta_weight, beta_bias, skip)
    results = [
        shape(count, length, half, dtype=bf16),
        shape(count, length, selected.shape[2]),
        shape(count, length, half),
        shape(count, 1, half),
    ]

    def spec(array):
        rest = array.shape[1:]
        return pl.BlockSpec((1,) + rest, lambda n: (sequence,) + (0,) * len(rest))

    def kernel(*refs):
        backward_kernel(*refs[len(into) :])

    moved = sum(a.size * a.dtype.itemsize for a in (*operands, *results)) // count
    return pl.pallas_call(
        kernel,
        grid=(1,),
        in_specs=[pl.BlockSpec(memory_space=pl.ANY) for _ in into]
        + [spec(a) for a in operands[:6]]
        + [pl.BlockSpec((half // lanes, 1, states, lanes), lambda n: (0, 1, sequence, 0))]
        + [spec(a) for a in operands[7:]]
        + [whole_spec(a) for a in shared],
        out_specs=[spec(a) for a in results],
        out_shape=results,
        scratch_shapes=[kept] * 3
        + [natural, pltpu.VMEM((span, states, half), f32)]
        + [hist] * 3
        + [pltpu.VMEM((states, half), f32), natural]
        + [folded] * 2,
        input_output_aliases={n: n for n in range(len(into))},
        compiler_params=pltpu.CompilerParams(vmem_limit_bytes=58 * 2**20),
        cost_estimate=pl.CostEstimate(
            flops=int(34 * 1.15e9), bytes_accessed=moved, transcendentals=0
        ),
        name="backward",
    )(*into, *operands, *shared)


def run_correlate(d_conv, later, weights, taps):
    count, length, half = d_conv.shape
    results = [shape(group, count * length, half // group, dtype=bf16)]
    specs = [pl.BlockSpec((group, length, half // group), lambda n: (0, n, 0))]
    later = jnp.pad(later, ((0, 0), (0, 8 - later.shape[1]), (0, 0)))
    return per_sequence(
        functools.partial(correlate_kernel, taps, group),
        "correlate",
        (d_conv, later),
        (weights,),
        results,
        [pltpu.VMEM((length + 8, lanes), f32)],
        4,
        specs,
    )[0]


def chain_kernel(pieces_ref, out_ref):
    count = pieces_ref.shape[0]
    state = jnp.zeros(pieces_ref.shape[2:], f32)
    grad = jnp.zeros(pieces_ref.shape[2:], f32)
    for piece in range(count):
        later = count - 1 - piece
        out_ref[piece, 0] = state.astype(bf16)
        out_ref[later, 1] = grad.astype(bf16)
        state = pieces_ref[piece, 0].astype(f32) * state + pieces_ref[piece, 1].astype(f32)
        grad = pieces_ref[later, 0].astype(f32) * grad + pieces_ref[later, 2].astype(f32)


def exchange_states(sums):
    count = lax.axis_size(seq)
    tiles, kinds, rows, _ = sums.shape
    share = tiles * rows // count
    if share < rows:
        sums = sums.reshape(tiles, kinds, rows // share, share, lanes).swapaxes(1, 2)
    pieces = lax.all_to_all(sums.reshape(count, kinds, share, lanes), seq, 0, 0)
    vmem = pl.BlockSpec(memory_space=pltpu.VMEM)
    sent = pl.pallas_call(
        chain_kernel,
        out_shape=shape(count, 2, share, lanes, dtype=bf16),
        in_specs=[vmem],
        out_specs=vmem,
        name="chain",
    )(pieces)
    got = lax.all_to_all(sent, seq, 0, 0)
    if share < rows:
        got = got.reshape(tiles, rows // share, 2, share, lanes).swapaxes(1, 2)
    return got.reshape(tiles, 2, rows, lanes)


def shifted(value, steps):
    count = lax.axis_size(seq)
    pairs = [(s, s + steps) for s in range(count) if 0 <= s + steps < count]
    return lax.ppermute(value, seq, pairs)


def plane_trade(chunks):
    mine = lax.axis_index("member")
    got = [at(chunks, mine)]
    for d in range(1, group):
        pairs = [(m, m ^ d) for m in range(group)]
        got.append(lax.ppermute(at(chunks, jnp.bitwise_xor(mine, d)), "member", pairs))
    return got


def line_trade(partial, bit, axis="outer"):
    count = lax.axis_size(axis)
    mine = (lax.axis_index(axis) // bit) % 2
    split = partial.reshape((-1, 2) + partial.shape[1:])
    sent = lax.dynamic_index_in_dim(split, 1 - mine, 1, keepdims=False).astype(bf16)
    kept = lax.dynamic_index_in_dim(split, mine, 1, keepdims=False)
    got = lax.ppermute(sent, axis, [(o, o ^ bit) for o in range(count)])
    return kept, got


def line_step(partial, bit, axis="outer"):
    kept, got = line_trade(partial, bit, axis)
    return kept + got.astype(f32)


def line_reduce(partial, bit, axis="outer"):
    while partial.shape[0] > 1:
        partial = line_step(partial, bit, axis)
        bit *= 2
    return partial[0]


def to_owner(rows):
    half = lax.axis_size("outer") // 2
    core = lax.axis_index("fsdp")
    pairs = []
    for o in range(2 * half):
        c = 1 - o // half
        pairs.append((o * 2 + c, (o ^ half) * 2 + 1 - c))
    got = lax.ppermute(rows.astype(bf16), ("outer", "fsdp"), pairs).astype(f32)
    return jnp.where(lax.axis_index("outer") // half == core, rows, got)


def owner_sum(partial):
    partial = line_reduce(partial, 1)
    half = lax.axis_size("outer") // 2
    pairs = []
    for o in range(2 * half):
        c = 1 - o // half
        pairs.append((o * 2 + c, (o ^ half) * 2 + c))
    return partial + lax.ppermute(partial.astype(bf16), ("outer", "fsdp"), pairs).astype(f32)


def owner_part(total, axis):
    core = lax.axis_index("fsdp")
    outer = lax.axis_index("outer")
    half = lax.axis_size("outer") // 2
    size = total.shape[axis] // 2
    mine = lax.dynamic_slice_in_dim(total, core * size, size, axis)
    other = swap(lax.dynamic_slice_in_dim(total, (1 - core) * size, size, axis))
    return jnp.where(outer // half == core, mine, other)


def local(
    tokens,
    cotangent,
    norm_gain,
    in_weight,
    conv_weight,
    conv_bias,
    select_weight,
    beta_weight,
    beta_bias,
    skip_gain,
    out_weight,
):
    core = lax.axis_index("fsdp")
    count = lax.axis_size(seq)
    outer_count = lax.axis_size("outer")
    member = lax.axis_index("member")
    length, model = tokens.shape[1], tokens.shape[2]
    half_model = in_weight.shape[0]
    half, taps = conv_weight.shape
    inner = 2 * half
    rank = beta_weight.shape[1]
    states = (select_weight.shape[1] - rank) // 2
    rows = 2 * length
    reach = taps - 1

    def ordered(mine, other):
        return jnp.where(core == 0, mine, other), jnp.where(core == 0, other, mine)

    own_tokens = tokens[0]
    own_cot = cotangent[0]
    x = jnp.concatenate(ordered(own_tokens, swap(own_tokens)))
    cot = jnp.concatenate(ordered(own_cot, swap(own_cot)))
    gain_full = jnp.concatenate(ordered(norm_gain, swap(norm_gain))).astype(f32)

    core_index = core.astype(jnp.int32).reshape(1)
    inner_got = swap(other_columns(core_index, in_weight, False))
    gate_got = swap(other_columns(core_index, in_weight, True))

    def normalise(values):
        wide = values.astype(f32)
        inverse = lax.rsqrt(jnp.mean(wide * wide, axis=1, keepdims=True) + epsilon)
        normal = wide * inverse
        return normal, inverse, (normal * gain_full).astype(bf16)

    normal, inverse, own_normed = normalise(own_tokens)
    normed = normalise(x)[2]
    normed_all = lax.all_gather(own_normed, ("member", "fsdp"), tiled=True)
    cot_all = lax.all_gather(own_cot, ("outer", "fsdp"), tiled=True)
    d_branch = run_product(cot, out_weight, True, 5)
    inner_pre = run_project(core_index, normed, in_weight, inner_got, False, 5)
    inner_pre = inner_pre.reshape(2, length, half)
    edges = shifted(inner_pre[:, length - reach :], 1)
    gate = run_project(core_index, normed, in_weight, gate_got, True, 5).reshape(2, length, half)
    extended = jnp.concatenate([edges, inner_pre], axis=1)
    conv_wide = conv_weight.astype(f32)
    conv_sum = conv_bias.astype(f32)
    for tap in range(taps):
        conv_sum = conv_sum + conv_wide[:, tap] * extended[:, tap : tap + length].astype(f32)
    conv_sum = conv_sum.reshape(rows, half)
    inner_act = jax.nn.silu(conv_sum).astype(bf16)
    selected = matmul(inner_act, select_weight)
    selected = selected + swap(selected)
    low_rank = selected[:, :rank].astype(bf16)
    beta_shift = beta_bias.astype(f32)[None]
    skip_wide = skip_gain.astype(f32)[None]
    width = half // group
    owner_rows = 2 * half // count
    selected = selected.reshape(2, length, -1)
    act_rows = inner_act.reshape(2, length, half)
    d_branch = d_branch.reshape(2, length, half)
    rates, fed, d_recurrent, sums = run_summary(
        selected, act_rows, gate, d_branch, beta_weight, beta_shift, states
    )
    chain = exchange_states(sums)
    early, branch_split, branch, starts, skip_term = run_forward(
        selected, rates, fed, chain, act_rows, gate, d_branch, skip_wide, outer_count
    )
    early, branch_split, normed_all, cot_all = together(
        early, branch_split, normed_all, cot_all
    )
    branch = branch.reshape(rows, half)

    traded = plane_trade(early)
    branch_all = lax.all_to_all(branch_split, "outer", 0, 0).reshape(outer_count * rows, -1)
    def ordered_members(pieces):
        stacked = jnp.stack(pieces)
        return jnp.concatenate([at(stacked, jnp.bitwise_xor(member, m)) for m in range(group)])

    def in_weight_partial(grad_all):
        return matmul_tn(normed_all, grad_all).reshape(outer_count, -1, width)

    def in_weight_rows(inner_part, gate_part):
        pieces = jnp.concatenate([inner_part, gate_part], axis=1).reshape(group, -1, 2 * width)
        got = lax.all_to_all(pieces, "member", 0, 0).reshape(group, 2, -1, 2 * width)
        mine = lax.dynamic_index_in_dim(got, core, 1, keepdims=False)
        other = swap(lax.dynamic_index_in_dim(got, 1 - core, 1, keepdims=False))
        low, high = ordered(mine, other)
        found = [source[q, :, :width] for source in (low, high) for q in range(group)]
        found += [source[q, :, width:] for source in (low, high) for q in range(group)]
        return jnp.concatenate(found, axis=1).astype(f32)

    operands = (
        selected,
        rates,
        fed,
        d_recurrent,
        act_rows,
        starts,
        chain,
        beta_weight,
        beta_shift,
        skip_wide,
    )
    first_part = list(run_backward(0, (), *operands))
    *traded, first_part[1] = together(*traded, first_part[1])
    early_all = ordered_members(traded)
    gate_partial, branch_all, *first_part = together(
        in_weight_partial(early_all), branch_all, *first_part
    )
    gate_kept, gate_got_sum = line_trade(gate_partial, 1)
    d_logits, d_selected, d_base, bias_term = run_backward(1, tuple(first_part), *operands)
    d_selected, gate_got_sum = together(d_selected, gate_got_sum)
    d_logits = d_logits.reshape(rows, half)
    d_selected = d_selected.reshape(rows, -1)
    d_selected = d_selected + swap(d_selected)
    d_selected = d_selected.astype(bf16)
    d_inner = d_base.reshape(rows, half) + matmul_nt(d_selected, select_weight)
    d_conv = (d_inner * swish_slope(conv_sum)).reshape(2, length, half)
    later = shifted(d_conv[:, :reach], -1)
    split = run_correlate(d_conv, later, conv_wide.T, taps)
    split, early = together(split, early)
    inner_all = lax.all_to_all(split, "member", 0, 0).reshape(group * rows, width)
    kept, sent = run_normed(core_index, split, early, in_weight, inner_got, gate_got, 10)
    split, gate_got_sum = together(split, gate_got_sum)
    gate_part = line_reduce(gate_kept + gate_got_sum.astype(f32), 2)
    inner_all, gate_part, kept, sent = together(inner_all, gate_part, kept, sent)
    inner_partial, branch_all, branch = together(in_weight_partial(inner_all), branch_all, branch)
    out_partial = matmul_tn(branch_all, cot_all).reshape(group, -1, model)

    out_sum = run_product(branch, out_weight, False, 5)
    out_sum = out_sum.reshape(2, length, model)
    layer_out = own_tokens.astype(f32) + (at(out_sum, core) + swap(at(out_sum, 1 - core)))
    layer_out = layer_out.astype(bf16)[None]

    d_normed = kept + swap(sent)
    gain_term = jnp.sum(d_normed * normal, axis=0)
    gain_term = gain_term.reshape(2, -1)
    gain_term = at(gain_term, core) + swap(at(gain_term, 1 - core))
    d_normal = d_normed * gain_full
    token_grad = inverse * (
        d_normal - normal * jnp.mean(normal * d_normal, axis=1, keepdims=True)
    ) + own_cot.astype(f32)

    vectors = [
        jnp.sum(d_conv * extended[:, tap : tap + length].astype(f32), axis=(0, 1))
        for tap in range(taps)
    ]
    owned = half // count
    vectors += [
        jnp.sum(d_conv, axis=(0, 1)),
        jnp.sum(bias_term, axis=(0, 1)),
        jnp.sum(skip_term, axis=(0, 1)),
        jnp.pad(gain_term.reshape(count, -1), ((0, 0), (0, owned - model // 2 // count))).reshape(-1),
    ]
    vectors = jnp.stack(vectors)
    vectors = jnp.pad(vectors, ((0, -vectors.shape[0] % 16), (0, 0)))
    pack = run_pack(
        d_selected.T, low_rank.T, inner_act, d_logits, vectors, outer_count // 2, owner_rows, 1
    )

    inner_mid = line_step(inner_partial, 1)
    out_kept, out_got = line_trade(out_partial, 1, "member")
    pack, out_got = together(pack, out_got)
    out_mid = out_kept + out_got.astype(f32)
    pack_all = lax.all_to_all(pack, "member", 0, 0)
    inner_part = line_reduce(inner_mid, 2)
    out_total = line_reduce(out_mid, 2, "member")
    inner_part, pack_all = together(inner_part, pack_all)
    pack_own = owner_part(owner_sum(jnp.sum(pack_all.astype(f32), axis=0)), 1).T
    out_grad = to_owner(out_total)
    in_grad = in_weight_rows(inner_part.astype(bf16), gate_part.astype(bf16))
    edge = select_weight.shape[1]
    select_grad = pack_own[:, :edge]
    beta_weight_grad = pack_own[:, edge : edge + rank]
    edge += rank
    conv_weight_grad = pack_own[:, edge : edge + taps]
    conv_bias_grad = pack_own[:, edge + taps]
    beta_bias_grad = pack_own[:, edge + taps + 1]
    skip_grad = pack_own[:, edge + taps + 2]
    gain_grad = pack_own[: model // 2 // count, edge + taps + 3]

    return (
        layer_out,
        token_grad[None],
        gain_grad,
        in_grad,
        conv_weight_grad,
        conv_bias_grad,
        select_grad,
        beta_weight_grad,
        beta_bias_grad,
        skip_grad,
        out_grad,
    )


def solution(mesh):
    devices = mesh.devices
    parts = jax.sharding.Mesh(
        devices.reshape(devices.shape[0] // group, group, devices.shape[1]),
        ("outer", "member", "fsdp"),
    )
    everything = ("outer", "member", "fsdp")
    tokens = P("fsdp", seq, None)
    vector, matrix = P("fsdp"), P("fsdp", None)
    owned, owned_rows = P(everything), P(everything, None)
    in_specs = (
        tokens,
        tokens,
        vector,
        matrix,
        matrix,
        vector,
        matrix,
        matrix,
        vector,
        vector,
        matrix,
    )
    out_specs = (
        tokens,
        tokens,
        owned,
        owned_rows,
        owned_rows,
        owned,
        owned_rows,
        owned_rows,
        owned,
        owned,
        owned_rows,
    )
    return jax.shard_map(
        local, mesh=parts, in_specs=in_specs, out_specs=out_specs, check_vma=False
    )
```

```python
import functools

import jax
import jax.numpy as jnp
from jax import lax
from jax.experimental import pallas as pl
from jax.experimental.pallas import tpu as pltpu
from jax.sharding import PartitionSpec as P

f32 = jnp.float32
bf16 = jnp.bfloat16
epsilon = 1e-05
lanes = 128
group = 4
span = 16
batch = 8
narrow = 2
seq = ("outer", "member")


def matmul(left, right):
    return jnp.dot(left, right, preferred_element_type=f32)


def matmul_nt(left, right):
    return lax.dot_general(left, right, (((1,), (1,)), ((), ())), preferred_element_type=f32)


def matmul_tn(left, right):
    return lax.dot_general(left, right, (((0,), (0,)), ((), ())), preferred_element_type=f32)


def swish_slope(value):
    logistic = jax.nn.sigmoid(value)
    return logistic * (1.0 + value * (1.0 - logistic))


def together(*values):
    return lax.optimization_barrier(values)


def swap(value):
    return lax.ppermute(value, "fsdp", [(0, 1), (1, 0)])


def at(stacked, index):
    return lax.dynamic_index_in_dim(stacked, index, 0, keepdims=False)


def column(j):
    return pl.ds(j * lanes, lanes)


def eights(ref):
    return ref.reshape(ref.shape[0] // 8, 8, ref.shape[1])


def tall(ref, base, step, j):
    return jnp.broadcast_to(ref[base + step // 8, pl.ds(step % 8, 1), column(j)], (8, lanes))


def spread_columns(sel_ref, first, states, targets):
    length = sel_ref.shape[1]
    for i in range(states):
        value = jnp.broadcast_to(sel_ref[0, :, first + i : first + i + 1], (length, lanes))
        for target, apply in targets:
            target.reshape(length * states, lanes)[pl.ds(i, length, stride=states), :] = apply(
                value
            )


def gate_of(low_rank, weight_ref, bias_ref, j):
    logits = matmul_nt(low_rank, weight_ref[pl.ds(j * lanes, lanes), :])
    return jax.nn.sigmoid(logits + bias_ref[:, column(j)])


def key_sum(sel_ref, rank, states):
    keys = sel_ref[0, :, rank : rank + states]
    return jnp.sum(keys * keys, axis=1, keepdims=True)


def halves(ref, position, states):
    return [ref[position, pl.ds(h, 8), :] for h in range(0, states, 8)]


def summary_kernel(
    sel_ref, act_ref, gate_ref, db_ref, bw_ref, bb_ref, r_ref, f_ref, d_ref, sum_ref, kb, k2b, qb
):
    length, half = act_ref.shape[1], act_ref.shape[2]
    states = kb.shape[1]
    rank = bw_ref.shape[1]
    tiles = half // lanes
    spread_columns(sel_ref, rank, states, [(kb, lambda v: v), (k2b, lambda v: v * v)])
    spread_columns(sel_ref, rank + states, states, [(qb, lambda v: v)])
    norm = key_sum(sel_ref, rank, states)
    low_rank = sel_ref[0, :, :rank].astype(bf16)
    for j in range(tiles):
        beta = gate_of(low_rank, bw_ref, bb_ref, j)
        rate = beta / (1.0 + beta * norm)
        r_ref[0, :, column(j)] = rate
        f_ref[0, :, column(j)] = rate * act_ref[0, :, column(j)].astype(f32)
        gate = gate_ref[0, :, column(j)].astype(f32)
        d_ref[0, :, column(j)] = db_ref[0, :, column(j)] * (gate * jax.nn.sigmoid(gate))
    zero = jnp.zeros((8, lanes), f32)
    one = jnp.ones((8, lanes), f32)
    group = range(states // 8)
    rates, feds, outs = (eights(ref.at[0]) for ref in (r_ref, f_ref, d_ref))
    for first in range(0, tiles, batch):
        places = [(h, j) for j in range(first, first + batch) for h in group]

        def body(lap, carry):
            product, current, grads = (list(part) for part in carry)
            for step in range(8):
                position = pl.multiple_of(lap * 8, 8) + step
                key, square, query = (halves(ref, position, states) for ref in (kb, k2b, qb))
                for n, (h, j) in enumerate(places):
                    fading = 1.0 - square[h] * tall(rates, lap, step, j)
                    current[n] = fading * current[n] + key[h] * tall(feds, lap, step, j)
                    product[n] = product[n] * fading
                    grads[n] = grads[n] + product[n] * (query[h] * tall(outs, lap, step, j))
            return (tuple(product), tuple(current), tuple(grads))

        size = len(places)
        product, current, grads = lax.fori_loop(
            0, length // 8, body, ((one,) * size, (zero,) * size, (zero,) * size)
        )
        for kind, parts in enumerate((product, current, grads)):
            for n in range(0, size, states // 8):
                whole = jnp.concatenate(parts[n : n + states // 8])
                sum_ref[places[n][1], kind] = whole.astype(sum_ref.dtype)


def advance(rates, feds, key, square, base, step, current, places):
    for n, (h, j) in enumerate(places):
        fading = 1.0 - square[h] * tall(rates, base, step, j)
        current[n] = fading * current[n] + key[h] * tall(feds, base, step, j)


def keep(ref, step, states, places, parts):
    by_tile = {}
    for (h, j), part in zip(places, parts):
        by_tile.setdefault(j, []).append(part)
    for j, both in by_tile.items():
        ref[pl.ds(step * states, states), column(j)] = jnp.concatenate(both).astype(bf16)


def forward_kernel(
    sel_ref,
    r_ref,
    f_ref,
    init_ref,
    act_ref,
    gate_ref,
    db_ref,
    qd_ref,
    skip_ref,
    gate_out,
    branch_out,
    branch_ref,
    start_ref,
    term_ref,
    kb,
    k2b,
    state,
    hist,
    held,
):
    length, half = act_ref.shape[1], act_ref.shape[2]
    states = init_ref.shape[2]
    tiles = half // lanes
    rank = sel_ref.shape[2] - 2 * states
    parts = range(states // 8)
    spread_columns(sel_ref, rank, states, [(kb, lambda v: v), (k2b, lambda v: v * v)])
    for j in range(tiles):
        state[:, column(j)] = init_ref[j, 0].astype(f32)
    rates, feds = (eights(ref.at[0]) for ref in (r_ref, f_ref))

    def block(index, carry):
        base = pl.multiple_of(index * span, span)
        start_ref[0, index] = state[...]
        for first in range(0, tiles, batch):
            places = [(h, j) for j in range(first, first + batch) for h in parts]
            current = [state[pl.ds(h * 8, 8), column(j)] for h, j in places]
            for step in range(span):
                key, square = (halves(ref, base + step, states) for ref in (kb, k2b))
                advance(rates, feds, key, square, index * (span // 8), step, current, places)
                keep(hist, step, states, places, current)
            for n, (h, j) in enumerate(places):
                state[pl.ds(h * 8, 8), column(j)] = current[n]
        held[pl.ds(base, span), :] = matmul(qd_ref[0, pl.ds(base, span), :], hist[...])
        return carry

    lax.fori_loop(0, length // span, block, 0)
    width = half // group
    outer_half = branch_out.shape[0] // 2
    owned = branch_out.shape[2] // group
    for j in range(tiles):
        value = act_ref[0, :, column(j)].astype(f32)
        skip_sum = held[:, column(j)] + skip_ref[:, column(j)] * value
        gate = gate_ref[0, :, column(j)].astype(f32)
        logistic = jax.nn.sigmoid(gate)
        swish = gate * logistic
        d_branch = db_ref[0, :, column(j)]
        branch = (skip_sum * swish).astype(bf16)
        d_gate = (d_branch * skip_sum * (logistic * (1.0 + gate * (1.0 - logistic)))).astype(bf16)
        term_ref[0, :, column(j)] = jnp.sum(d_branch * swish * value, axis=0, keepdims=True)
        branch_ref[0, :, column(j)] = branch
        member, offset = divmod(j * lanes, width)
        gate_out[member, :, pl.ds(offset, lanes)] = d_gate
        for inside in range(0, lanes, owned):
            owner = (j * lanes + inside) // owned
            outer = owner % 2 * outer_half + owner // (2 * group)
            offset = owner // 2 % group * owned
            branch_out[outer, :, offset : offset + owned] = branch[:, inside : inside + owned]


def backward_kernel(
    sel_ref,
    r_ref,
    f_ref,
    d_ref,
    act_ref,
    start_ref,
    last_ref,
    kd_ref,
    bw_ref,
    bb_ref,
    skip_ref,
    dlog_ref,
    dsel_ref,
    base_ref,
    bias_ref,
    kb,
    k2b,
    qb,
    v_s,
    before,
    s_hist,
    g_hist,
    w_hist,
    grad_s,
    dr_s,
    dk_s,
    dq_s,
):
    length, half = act_ref.shape[1], act_ref.shape[2]
    states = last_ref.shape[2]
    tiles = half // lanes
    rank = bw_ref.shape[1]
    group = range(states // 8)
    blocks = length // span
    spread_columns(sel_ref, rank, states, [(kb, lambda v: v), (k2b, lambda v: v * v)])
    spread_columns(sel_ref, rank + states, states, [(qb, lambda v: v)])
    v_s[...] = act_ref[0].astype(f32)
    rates, feds, outs, values = (eights(ref) for ref in (r_ref.at[0], f_ref.at[0], d_ref.at[0], v_s))
    for j in range(tiles):
        grad_s[:, column(j)] = last_ref[j, 0].astype(f32)
    wide = span * states
    own = lax.broadcasted_iota(jnp.int32, (span, wide), 1) // states == lax.broadcasted_iota(
        jnp.int32, (span, wide), 0
    )

    def block(lap, carry):
        index = blocks - 1 - lap
        base = pl.multiple_of(index * span, span)
        eight = index * (span // 8)
        rows = pl.ds(base, span)
        diagonal = kd_ref[0, rows, :]
        d_key = None
        for first in range(0, tiles, narrow):
            places = [(h, j) for j in range(first, first + narrow) for h in group]
            cols = pl.ds(first * lanes, narrow * lanes)
            current = [start_ref[0, index, pl.ds(h * 8, 8), column(j)] for h, j in places]
            for step in range(span):
                for n, (h, j) in enumerate(places):
                    before[step, pl.ds(h * 8, 8), column(j)] = current[n]
                key, square = (halves(ref, base + step, states) for ref in (kb, k2b))
                advance(rates, feds, key, square, eight, step, current, places)
                keep(s_hist, step, states, places, current)
        d_query = matmul_nt(s_hist[...], d_ref[0, rows, :].astype(bf16))
        for first in range(0, tiles, narrow):
            places = [(h, j) for j in range(first, first + narrow) for h in group]
            cols = pl.ds(first * lanes, narrow * lanes)
            grads = [grad_s[pl.ds(h * 8, 8), column(j)] for h, j in places]
            for step in reversed(range(span)):
                key, square, query = (halves(ref, base + step, states) for ref in (kb, k2b, qb))
                full, left = [], []
                for n, (h, j) in enumerate(places):
                    grad = grads[n] + query[h] * tall(outs, eight, step, j)
                    kept = key[h] * before[step, pl.ds(h * 8, 8), column(j)]
                    full.append(grad)
                    left.append(grad * (tall(values, eight, step, j) - kept))
                    grads[n] = grad * (1.0 - square[h] * tall(rates, eight, step, j))
                keep(g_hist, step, states, places, full)
                keep(w_hist, step, states, places, left)
            for n, (h, j) in enumerate(places):
                grad_s[pl.ds(h * 8, 8), column(j)] = grads[n]
            block_rates = r_ref[0, rows, cols]
            dr_s[rows, cols] = matmul(diagonal, w_hist[:, cols])
            base_ref[0, rows, cols] = block_rates * matmul(diagonal, g_hist[:, cols])
            part = matmul_nt(w_hist[:, cols], (2.0 * block_rates).astype(bf16)) - matmul_nt(
                g_hist[:, cols], f_ref[0, rows, cols].astype(bf16)
            )
            d_key = part if d_key is None else d_key + part
        dq_s[rows, :] = jnp.where(own, d_query.T, 0.0)
        dk_s[rows, :] = jnp.where(own, d_key.T, 0.0)
        return carry

    lax.fori_loop(0, blocks, block, 0)

    norm = key_sum(sel_ref, rank, states)
    low_rank = sel_ref[0, :, :rank].astype(bf16)
    d_norm = jnp.zeros((length, lanes), f32)
    for j in range(tiles):
        beta = gate_of(low_rank, bw_ref, bb_ref, j)
        inverse = 1.0 / (1.0 + beta * norm)
        rate = beta * inverse
        d_rate = dr_s[:, column(j)]
        d_norm = d_norm - d_rate * (rate * rate)
        d_logits = (d_rate * (inverse * inverse) * (beta * (1.0 - beta))).astype(bf16)
        dlog_ref[0, :, column(j)] = d_logits
        bias_ref[0, :, column(j)] = jnp.sum(d_logits.astype(f32), axis=0, keepdims=True)
        base_ref[0, :, column(j)] += d_ref[0, :, column(j)] * skip_ref[:, column(j)]
    d_norm = 2.0 * jnp.sum(d_norm, axis=1, keepdims=True)
    dsel_ref[0, :, :rank] = matmul(dlog_ref[0], bw_ref[...])

    def folded(ref):
        total = ref[:, :lanes]
        for first in range(lanes, wide, lanes):
            total = total + ref[:, first : first + lanes]
        size = lanes // 2
        while size >= states:
            total = total + pltpu.roll(total, size, 1)
            size //= 2
        return total[:, : 2 * states]

    place = lax.broadcasted_iota(jnp.int32, (length, 2 * states), 1)
    keys = sel_ref[0, :, rank:]
    dsel_ref[0, :, rank:] = jnp.where(place < states, folded(dk_s) + keys * d_norm, folded(dq_s))


def correlate_kernel(taps, split, d_ref, later_ref, w_ref, out_ref, held):
    length, half = d_ref.shape[1], d_ref.shape[2]
    width = half // split
    for j in range(half // lanes):
        held[:length, :] = d_ref[0, :, column(j)]
        held[length:, :] = later_ref[0, :, column(j)]
        total = None
        for tap in range(taps):
            part = w_ref[tap : tap + 1, column(j)] * held[pl.ds(taps - 1 - tap, length), :]
            total = part if total is None else total + part
        member, offset = divmod(j * lanes, width)
        out_ref[member, :, pl.ds(offset, lanes)] = total.astype(bf16)


def copy_kernel(core_ref, in_ref, out_ref):
    out_ref[...] = in_ref[...]


def other_columns(core, in_weight, gate):
    half_model, half = in_weight.shape[0], in_weight.shape[1] // 4
    wide = half // group
    first = 2 * group if gate else 0
    return pl.pallas_call(
        copy_kernel,
        grid_spec=pltpu.PrefetchScalarGridSpec(
            num_scalar_prefetch=1,
            grid=(group,),
            in_specs=[
                pl.BlockSpec(
                    (half_model, wide), lambda n, core: (0, first + group * (1 - core[0]) + n)
                )
            ],
            out_specs=pl.BlockSpec((half_model, wide), lambda n, core: (0, n)),
        ),
        out_shape=shape(half_model, half, dtype=bf16),
        cost_estimate=pl.CostEstimate(
            flops=int(5 * 1.15e9), bytes_accessed=4 * half_model * half, transcendentals=0
        ),
        name="columns",
    )(core, in_weight)


def whole_kernel(transposed, left_ref, right_ref, out_ref):
    product = matmul_nt if transposed else matmul
    out_ref[...] = product(left_ref[...], right_ref[...])


def run_product(left, right, transposed, micros):
    rows, depth = left.shape
    columns = right.shape[0 if transposed else 1]
    wide = 4 * lanes
    right_spec = (
        pl.BlockSpec((wide, depth), lambda n: (n, 0))
        if transposed
        else pl.BlockSpec((depth, wide), lambda n: (0, n))
    )
    return pl.pallas_call(
        functools.partial(whole_kernel, transposed),
        grid=(columns // wide,),
        in_specs=[pl.BlockSpec((rows, depth), lambda n: (0, 0)), right_spec],
        out_specs=pl.BlockSpec((rows, wide), lambda n: (0, n)),
        out_shape=shape(rows, columns),
        compiler_params=pltpu.CompilerParams(vmem_limit_bytes=40 * 2**20),
        cost_estimate=pl.CostEstimate(
            flops=int(micros * 1.15e9), bytes_accessed=1 << 20, transcendentals=0
        ),
        name="product",
    )(left, right)


def project_kernel(core_ref, x_ref, own_ref, got_ref, out_ref):
    size = own_ref.shape[0]
    mine = pl.multiple_of(core_ref[0] * size, size)
    other = pl.multiple_of((1 - core_ref[0]) * size, size)
    out_ref[...] = (
        matmul(x_ref[:, pl.ds(mine, size)], own_ref[...])
        + matmul(x_ref[:, pl.ds(other, size)], got_ref[...])
    ).astype(out_ref.dtype)


def run_project(core, normed, in_weight, got, gate, micros):
    rows, model = normed.shape
    half_model, half = got.shape
    wide = half // group
    first = 2 * group if gate else 0
    return pl.pallas_call(
        project_kernel,
        grid_spec=pltpu.PrefetchScalarGridSpec(
            num_scalar_prefetch=1,
            grid=(group,),
            in_specs=[
                pl.BlockSpec((rows, model), lambda n, core: (0, 0)),
                pl.BlockSpec((half_model, wide), lambda n, core: (0, first + group * core[0] + n)),
                pl.BlockSpec((half_model, wide), lambda n, core: (0, n)),
            ],
            out_specs=pl.BlockSpec((rows, wide), lambda n, core: (0, n)),
        ),
        out_shape=shape(rows, half, dtype=bf16),
        compiler_params=pltpu.CompilerParams(vmem_limit_bytes=40 * 2**20),
        cost_estimate=pl.CostEstimate(
            flops=int(micros * 1.15e9), bytes_accessed=2 * half_model * half * 2, transcendentals=0
        ),
        name="project",
    )(core, normed, in_weight, got)


def normed_kernel(
    core_ref,
    inner_ref,
    gate_ref,
    inner_own,
    gate_own,
    inner_got,
    gate_got,
    kept_ref,
    sent_ref,
    inner_flat,
    gate_flat,
    total,
):
    lap = pl.program_id(0)
    length = kept_ref.shape[0]
    wide = inner_ref.shape[2]

    @pl.when(lap == 0)
    def _():
        for n in range(group):
            inner_flat[:, pl.ds(n * wide, wide)] = inner_ref[n]
            gate_flat[:, pl.ds(n * wide, wide)] = gate_ref[n]

    @pl.when(lap < group)
    def _():
        total[...] = matmul_nt(inner_flat[...], inner_own[...]) + matmul_nt(
            gate_flat[...], gate_own[...]
        )

    @pl.when(lap >= group)
    def _():
        total[...] = matmul_nt(inner_flat[...], inner_got[...]) + matmul_nt(
            gate_flat[...], gate_got[...]
        )

    kept_ref[...] = total[pl.ds(pl.multiple_of(core_ref[0] * length, length), length), :]
    sent_ref[...] = total[pl.ds(pl.multiple_of((1 - core_ref[0]) * length, length), length), :]


def run_normed(core, inner_split, gate_split, in_weight, inner_got, gate_got, micros):
    _, rows, wide = inner_split.shape
    half_model, half = inner_got.shape
    high = half_model // group
    result = shape(rows // 2, 2 * half_model)
    whole = pl.BlockSpec((group, rows, wide), lambda n, core: (0, 0, 0))

    def own(offset):
        return pl.BlockSpec(
            (high, half), lambda n, core: (jnp.minimum(n, group - 1), offset + core[0])
        )

    got = pl.BlockSpec((high, half), lambda n, core: (jnp.maximum(n - group, 0), 0))
    out = pl.BlockSpec(
        (rows // 2, high),
        lambda n, core: (0, jnp.where(n < group, n + group * core[0], n - group * core[0])),
    )
    return pl.pallas_call(
        normed_kernel,
        grid_spec=pltpu.PrefetchScalarGridSpec(
            num_scalar_prefetch=1,
            grid=(2 * group,),
            in_specs=[whole, whole, own(0), own(2), got, got],
            out_specs=[out] * 2,
            scratch_shapes=[
                pltpu.VMEM((rows, half), bf16),
                pltpu.VMEM((rows, half), bf16),
                pltpu.VMEM((rows, high), f32),
            ],
        ),
        out_shape=[result] * 2,
        compiler_params=pltpu.CompilerParams(vmem_limit_bytes=50 * 2**20),
        cost_estimate=pl.CostEstimate(
            flops=int(micros * 1.15e9), bytes_accessed=1 << 20, transcendentals=0
        ),
        name="normed",
    )(core, inner_split, gate_split, in_weight, in_weight, inner_got, gate_got)


def pack_kernel(sel_ref, low_ref, act_ref, log_ref, vec_ref, out_ref):
    half = act_ref.shape[1]
    rows = out_ref.shape[3]
    first, second = sel_ref.shape[0], low_ref.shape[0]
    step = 2 * lanes
    tail = out_ref.shape[2] - first - second
    for start in range(0, half, step):
        cols = pl.ds(start, step)
        parts = (
            matmul(sel_ref[...], act_ref[:, cols]).astype(bf16),
            matmul(low_ref[...], log_ref[:, cols]).astype(bf16),
            vec_ref[:tail, cols].astype(bf16),
        )
        size = min(rows, step)
        for inside in range(0, step, size):
            outer, rest = divmod(start + inside, group * rows)
            member, offset = divmod(rest, rows)
            row = 0
            for part in parts:
                out_ref[member, outer, row : row + part.shape[0], offset : offset + size] = part[
                    :, inside : inside + size
                ]
                row += part.shape[0]


def run_pack(selected, low_rank, act, logits, vectors, outer_half, rows, micros):
    height = selected.shape[0] + low_rank.shape[0] + vectors.shape[0]
    operands = (selected, low_rank, act, logits, vectors)
    return pl.pallas_call(
        pack_kernel,
        out_shape=shape(group, outer_half, height, rows, dtype=bf16),
        in_specs=[pl.BlockSpec(memory_space=pltpu.VMEM)] * 5,
        out_specs=pl.BlockSpec(memory_space=pltpu.VMEM),
        compiler_params=pltpu.CompilerParams(vmem_limit_bytes=40 * 2**20),
        cost_estimate=pl.CostEstimate(
            flops=int(micros * 1.15e9), bytes_accessed=1 << 20, transcendentals=0
        ),
        name="pack",
    )(*operands)


def sequence_spec(array):
    rest = array.shape[1:]
    return pl.BlockSpec((1,) + rest, lambda n: (n,) + (0,) * len(rest))


def whole_spec(array):
    zeros = (0,) * array.ndim
    return pl.BlockSpec(array.shape, lambda n: zeros)


def per_sequence(
    kernel, name, operands, shared, results, scratch, micros, out_specs=None, in_specs=None
):
    sequences = operands[0].shape[0]
    moved = sum(a.size * a.dtype.itemsize for a in (*operands, *shared, *results))
    return pl.pallas_call(
        kernel,
        grid=(sequences,),
        in_specs=[(in_specs or {}).get(i, sequence_spec(a)) for i, a in enumerate(operands)]
        + [whole_spec(a) for a in shared],
        out_specs=out_specs or [sequence_spec(a) for a in results],
        out_shape=list(results),
        scratch_shapes=scratch,
        compiler_params=pltpu.CompilerParams(vmem_limit_bytes=58 * 2**20),
        cost_estimate=pl.CostEstimate(
            flops=int(micros * 1.15e9), bytes_accessed=moved, transcendentals=0
        ),
        name=name,
    )(*operands, *shared)


def shape(*dims, dtype=f32):
    return jax.ShapeDtypeStruct(dims, dtype)


def block_diagonal(array):
    length, states = array.shape[1], array.shape[2]
    wide = span * states
    own = jnp.arange(wide)[None, :] // states == jnp.arange(length)[:, None] % span
    return jnp.where(own, jnp.tile(array, (1, 1, span)), 0.0).astype(bf16)


def run_summary(selected, inner_act, gate, d_branch, beta_weight, beta_bias, states):
    count, length, half = inner_act.shape
    natural = shape(count, length, half)
    tiles = half // lanes
    results = [natural] * 3 + [shape(tiles, 3, count * states, lanes, dtype=bf16)]
    specs = [sequence_spec(a) for a in results]
    specs[3] = pl.BlockSpec((tiles, 3, states, lanes), lambda n: (0, 0, n, 0))
    kept = pltpu.VMEM((length, states, lanes), f32)
    return per_sequence(
        summary_kernel,
        "summary",
        (selected, inner_act, gate, d_branch),
        (beta_weight, beta_bias),
        results,
        [kept] * 3,
        25,
        specs,
    )


def run_forward(selected, rates, fed, chain, act, gate, d_branch, skip, outer_count):
    count, length, half = rates.shape
    states = chain.shape[2] // count
    queries = selected[:, :, selected.shape[2] - states :]
    kept = pltpu.VMEM((length, states, lanes), f32)
    results = [
        shape(group, count * length, half // group, dtype=bf16),
        shape(outer_count, count * length, half // outer_count, dtype=bf16),
        shape(count, length, half, dtype=bf16),
        shape(count, length // span, states, half),
        shape(count, 1, half),
    ]
    specs = [sequence_spec(a) for a in results]
    specs[0] = pl.BlockSpec((group, length, half // group), lambda n: (0, n, 0))
    specs[1] = pl.BlockSpec((outer_count, length, half // outer_count), lambda n: (0, n, 0))
    return per_sequence(
        forward_kernel,
        "forward",
        (selected, rates, fed, chain, act, gate, d_branch, block_diagonal(queries)),
        (skip,),
        results,
        [kept] * 2
        + [
            pltpu.VMEM((states, half), f32),
            pltpu.VMEM((span * states, half), bf16),
            pltpu.VMEM((length, half), f32),
        ],
        20,
        specs,
        {3: pl.BlockSpec((half // lanes, 1, states, lanes), lambda n: (0, 0, n, 0))},
    )


def run_backward(
    sequence, into, selected, rates, fed, grads, act, starts, chain, beta_weight, beta_bias, skip
):
    count, length, half = rates.shape
    states = chain.shape[2] // count
    rank = beta_weight.shape[1]
    keys = selected[:, :, rank : rank + states]
    kept = pltpu.VMEM((length, states, lanes), f32)
    natural = pltpu.VMEM((length, half), f32)
    hist = pltpu.VMEM((span * states, half), bf16)
    folded = pltpu.VMEM((length, span * states), f32)
    operands = (selected, rates, fed, grads, act, starts, chain, block_diagonal(keys))
    shared = (beta_weight, beta_bias, skip)
    results = [
        shape(count, length, half, dtype=bf16),
        shape(count, length, selected.shape[2]),
        shape(count, length, half),
        shape(count, 1, half),
    ]

    def spec(array):
        rest = array.shape[1:]
        return pl.BlockSpec((1,) + rest, lambda n: (sequence,) + (0,) * len(rest))

    def kernel(*refs):
        backward_kernel(*refs[len(into) :])

    moved = sum(a.size * a.dtype.itemsize for a in (*operands, *results)) // count
    return pl.pallas_call(
        kernel,
        grid=(1,),
        in_specs=[pl.BlockSpec(memory_space=pl.ANY) for _ in into]
        + [spec(a) for a in operands[:6]]
        + [pl.BlockSpec((half // lanes, 1, states, lanes), lambda n: (0, 1, sequence, 0))]
        + [spec(a) for a in operands[7:]]
        + [whole_spec(a) for a in shared],
        out_specs=[spec(a) for a in results],
        out_shape=results,
        scratch_shapes=[kept] * 3
        + [natural, pltpu.VMEM((span, states, half), f32)]
        + [hist] * 3
        + [pltpu.VMEM((states, half), f32), natural]
        + [folded] * 2,
        input_output_aliases={n: n for n in range(len(into))},
        compiler_params=pltpu.CompilerParams(vmem_limit_bytes=58 * 2**20),
        cost_estimate=pl.CostEstimate(
            flops=int(34 * 1.15e9), bytes_accessed=moved, transcendentals=0
        ),
        name="backward",
    )(*into, *operands, *shared)


def run_correlate(d_conv, later, weights, taps):
    count, length, half = d_conv.shape
    results = [shape(group, count * length, half // group, dtype=bf16)]
    specs = [pl.BlockSpec((group, length, half // group), lambda n: (0, n, 0))]
    later = jnp.pad(later, ((0, 0), (0, 8 - later.shape[1]), (0, 0)))
    return per_sequence(
        functools.partial(correlate_kernel, taps, group),
        "correlate",
        (d_conv, later),
        (weights,),
        results,
        [pltpu.VMEM((length + 8, lanes), f32)],
        4,
        specs,
    )[0]


def chain_kernel(pieces_ref, out_ref):
    count = pieces_ref.shape[0]
    state = jnp.zeros(pieces_ref.shape[2:], f32)
    grad = jnp.zeros(pieces_ref.shape[2:], f32)
    for piece in range(count):
        later = count - 1 - piece
        out_ref[piece, 0] = state.astype(bf16)
        out_ref[later, 1] = grad.astype(bf16)
        state = pieces_ref[piece, 0].astype(f32) * state + pieces_ref[piece, 1].astype(f32)
        grad = pieces_ref[later, 0].astype(f32) * grad + pieces_ref[later, 2].astype(f32)


def exchange_states(sums):
    count = lax.axis_size(seq)
    tiles, kinds, rows, _ = sums.shape
    share = tiles * rows // count
    if share < rows:
        sums = sums.reshape(tiles, kinds, rows // share, share, lanes).swapaxes(1, 2)
    pieces = lax.all_to_all(sums.reshape(count, kinds, share, lanes), seq, 0, 0)
    vmem = pl.BlockSpec(memory_space=pltpu.VMEM)
    sent = pl.pallas_call(
        chain_kernel,
        out_shape=shape(count, 2, share, lanes, dtype=bf16),
        in_specs=[vmem],
        out_specs=vmem,
        name="chain",
    )(pieces)
    got = lax.all_to_all(sent, seq, 0, 0)
    if share < rows:
        got = got.reshape(tiles, rows // share, 2, share, lanes).swapaxes(1, 2)
    return got.reshape(tiles, 2, rows, lanes)


def shifted(value, steps):
    count = lax.axis_size(seq)
    pairs = [(s, s + steps) for s in range(count) if 0 <= s + steps < count]
    return lax.ppermute(value, seq, pairs)


def plane_trade(chunks):
    mine = lax.axis_index("member")
    got = [at(chunks, mine)]
    for d in range(1, group):
        pairs = [(m, m ^ d) for m in range(group)]
        got.append(lax.ppermute(at(chunks, jnp.bitwise_xor(mine, d)), "member", pairs))
    return got


def line_trade(partial, bit, axis="outer"):
    count = lax.axis_size(axis)
    mine = (lax.axis_index(axis) // bit) % 2
    split = partial.reshape((-1, 2) + partial.shape[1:])
    sent = lax.dynamic_index_in_dim(split, 1 - mine, 1, keepdims=False).astype(bf16)
    kept = lax.dynamic_index_in_dim(split, mine, 1, keepdims=False)
    got = lax.ppermute(sent, axis, [(o, o ^ bit) for o in range(count)])
    return kept, got


def line_step(partial, bit, axis="outer"):
    kept, got = line_trade(partial, bit, axis)
    return kept + got.astype(f32)


def line_reduce(partial, bit, axis="outer"):
    while partial.shape[0] > 1:
        partial = line_step(partial, bit, axis)
        bit *= 2
    return partial[0]


def to_owner(rows):
    half = lax.axis_size("outer") // 2
    core = lax.axis_index("fsdp")
    pairs = []
    for o in range(2 * half):
        c = 1 - o // half
        pairs.append((o * 2 + c, (o ^ half) * 2 + 1 - c))
    got = lax.ppermute(rows.astype(bf16), ("outer", "fsdp"), pairs).astype(f32)
    return jnp.where(lax.axis_index("outer") // half == core, rows, got)


def owner_sum(partial):
    partial = line_reduce(partial, 1)
    half = lax.axis_size("outer") // 2
    pairs = []
    for o in range(2 * half):
        c = 1 - o // half
        pairs.append((o * 2 + c, (o ^ half) * 2 + c))
    return partial + lax.ppermute(partial.astype(bf16), ("outer", "fsdp"), pairs).astype(f32)


def owner_part(total, axis):
    core = lax.axis_index("fsdp")
    outer = lax.axis_index("outer")
    half = lax.axis_size("outer") // 2
    size = total.shape[axis] // 2
    mine = lax.dynamic_slice_in_dim(total, core * size, size, axis)
    other = swap(lax.dynamic_slice_in_dim(total, (1 - core) * size, size, axis))
    return jnp.where(outer // half == core, mine, other)


def local(
    tokens,
    cotangent,
    norm_gain,
    in_weight,
    conv_weight,
    conv_bias,
    select_weight,
    beta_weight,
    beta_bias,
    skip_gain,
    out_weight,
):
    core = lax.axis_index("fsdp")
    count = lax.axis_size(seq)
    outer_count = lax.axis_size("outer")
    member = lax.axis_index("member")
    length, model = tokens.shape[1], tokens.shape[2]
    half_model = in_weight.shape[0]
    half, taps = conv_weight.shape
    inner = 2 * half
    rank = beta_weight.shape[1]
    states = (select_weight.shape[1] - rank) // 2
    rows = 2 * length
    reach = taps - 1

    def ordered(mine, other):
        return jnp.where(core == 0, mine, other), jnp.where(core == 0, other, mine)

    own_tokens = tokens[0]
    own_cot = cotangent[0]
    x = jnp.concatenate(ordered(own_tokens, swap(own_tokens)))
    cot = jnp.concatenate(ordered(own_cot, swap(own_cot)))
    gain_full = jnp.concatenate(ordered(norm_gain, swap(norm_gain))).astype(f32)

    core_index = core.astype(jnp.int32).reshape(1)
    inner_got = swap(other_columns(core_index, in_weight, False))
    gate_got = swap(other_columns(core_index, in_weight, True))

    def normalise(values):
        wide = values.astype(f32)
        inverse = lax.rsqrt(jnp.mean(wide * wide, axis=1, keepdims=True) + epsilon)
        normal = wide * inverse
        return normal, inverse, (normal * gain_full).astype(bf16)

    normal, inverse, own_normed = normalise(own_tokens)
    normed = normalise(x)[2]
    normed_all = lax.all_gather(own_normed, ("member", "fsdp"), tiled=True)
    cot_all = lax.all_gather(own_cot, ("outer", "fsdp"), tiled=True)
    d_branch = run_product(cot, out_weight, True, 5)
    inner_pre = run_project(core_index, normed, in_weight, inner_got, False, 5)
    inner_pre = inner_pre.reshape(2, length, half)
    edges = shifted(inner_pre[:, length - reach :], 1)
    gate = run_project(core_index, normed, in_weight, gate_got, True, 5).reshape(2, length, half)
    extended = jnp.concatenate([edges, inner_pre], axis=1)
    conv_wide = conv_weight.astype(f32)
    conv_sum = conv_bias.astype(f32)
    for tap in range(taps):
        conv_sum = conv_sum + conv_wide[:, tap] * extended[:, tap : tap + length].astype(f32)
    conv_sum = conv_sum.reshape(rows, half)
    inner_act = jax.nn.silu(conv_sum).astype(bf16)
    selected = matmul(inner_act, select_weight)
    selected = selected + swap(selected)
    low_rank = selected[:, :rank].astype(bf16)
    beta_shift = beta_bias.astype(f32)[None]
    skip_wide = skip_gain.astype(f32)[None]
    width = half // group
    owner_rows = 2 * half // count
    selected = selected.reshape(2, length, -1)
    act_rows = inner_act.reshape(2, length, half)
    d_branch = d_branch.reshape(2, length, half)
    rates, fed, d_recurrent, sums = run_summary(
        selected, act_rows, gate, d_branch, beta_weight, beta_shift, states
    )
    chain = exchange_states(sums)
    early, branch_split, branch, starts, skip_term = run_forward(
        selected, rates, fed, chain, act_rows, gate, d_branch, skip_wide, outer_count
    )
    early, branch_split, normed_all, cot_all = together(
        early, branch_split, normed_all, cot_all
    )
    branch = branch.reshape(rows, half)

    traded = plane_trade(early)
    branch_all = lax.all_to_all(branch_split, "outer", 0, 0).reshape(outer_count * rows, -1)
    def ordered_members(pieces):
        stacked = jnp.stack(pieces)
        return jnp.concatenate([at(stacked, jnp.bitwise_xor(member, m)) for m in range(group)])

    def in_weight_partial(grad_all):
        return matmul_tn(normed_all, grad_all).reshape(outer_count, -1, width)

    def in_weight_rows(inner_part, gate_part):
        pieces = jnp.concatenate([inner_part, gate_part], axis=1).reshape(group, -1, 2 * width)
        got = lax.all_to_all(pieces, "member", 0, 0).reshape(group, 2, -1, 2 * width)
        mine = lax.dynamic_index_in_dim(got, core, 1, keepdims=False)
        other = swap(lax.dynamic_index_in_dim(got, 1 - core, 1, keepdims=False))
        low, high = ordered(mine, other)
        found = [source[q, :, :width] for source in (low, high) for q in range(group)]
        found += [source[q, :, width:] for source in (low, high) for q in range(group)]
        return jnp.concatenate(found, axis=1).astype(f32)

    operands = (
        selected,
        rates,
        fed,
        d_recurrent,
        act_rows,
        starts,
        chain,
        beta_weight,
        beta_shift,
        skip_wide,
    )
    first_part = list(run_backward(0, (), *operands))
    *traded, first_part[1] = together(*traded, first_part[1])
    early_all = ordered_members(traded)
    gate_partial, branch_all, *first_part = together(
        in_weight_partial(early_all), branch_all, *first_part
    )
    gate_kept, gate_got_sum = line_trade(gate_partial, 1)
    d_logits, d_selected, d_base, bias_term = run_backward(1, tuple(first_part), *operands)
    d_selected, gate_got_sum = together(d_selected, gate_got_sum)
    d_logits = d_logits.reshape(rows, half)
    d_selected = d_selected.reshape(rows, -1)
    d_selected = d_selected + swap(d_selected)
    d_selected = d_selected.astype(bf16)
    d_inner = d_base.reshape(rows, half) + matmul_nt(d_selected, select_weight)
    d_conv = (d_inner * swish_slope(conv_sum)).reshape(2, length, half)
    later = shifted(d_conv[:, :reach], -1)
    split = run_correlate(d_conv, later, conv_wide.T, taps)
    split, early = together(split, early)
    inner_all = lax.all_to_all(split, "member", 0, 0).reshape(group * rows, width)
    kept, sent = run_normed(core_index, split, early, in_weight, inner_got, gate_got, 10)
    split, gate_got_sum = together(split, gate_got_sum)
    gate_part = line_reduce(gate_kept + gate_got_sum.astype(f32), 2)
    inner_all, gate_part, kept, sent = together(inner_all, gate_part, kept, sent)
    inner_partial, branch_all, branch = together(in_weight_partial(inner_all), branch_all, branch)
    out_partial = matmul_tn(branch_all, cot_all).reshape(group, -1, model)

    out_sum = run_product(branch, out_weight, False, 5)
    out_sum = out_sum.reshape(2, length, model)
    layer_out = own_tokens.astype(f32) + (at(out_sum, core) + swap(at(out_sum, 1 - core)))
    layer_out = layer_out.astype(bf16)[None]

    d_normed = kept + swap(sent)
    gain_term = jnp.sum(d_normed * normal, axis=0)
    gain_term = gain_term.reshape(2, -1)
    gain_term = at(gain_term, core) + swap(at(gain_term, 1 - core))
    d_normal = d_normed * gain_full
    token_grad = inverse * (
        d_normal - normal * jnp.mean(normal * d_normal, axis=1, keepdims=True)
    ) + own_cot.astype(f32)

    vectors = [
        jnp.sum(d_conv * extended[:, tap : tap + length].astype(f32), axis=(0, 1))
        for tap in range(taps)
    ]
    owned = half // count
    vectors += [
        jnp.sum(d_conv, axis=(0, 1)),
        jnp.sum(bias_term, axis=(0, 1)),
        jnp.sum(skip_term, axis=(0, 1)),
        jnp.pad(gain_term.reshape(count, -1), ((0, 0), (0, owned - model // 2 // count))).reshape(-1),
    ]
    vectors = jnp.stack(vectors)
    vectors = jnp.pad(vectors, ((0, -vectors.shape[0] % 16), (0, 0)))
    pack = run_pack(
        d_selected.T, low_rank.T, inner_act, d_logits, vectors, outer_count // 2, owner_rows, 1
    )

    inner_mid = line_step(inner_partial, 1)
    out_kept, out_got = line_trade(out_partial, 1, "member")
    pack, out_got = together(pack, out_got)
    out_mid = out_kept + out_got.astype(f32)
    pack_all = lax.all_to_all(pack, "member", 0, 0)
    inner_part = line_reduce(inner_mid, 2)
    out_total = line_reduce(out_mid, 2, "member")
    inner_part, pack_all = together(inner_part, pack_all)
    pack_own = owner_part(owner_sum(jnp.sum(pack_all.astype(f32), axis=0)), 1).T
    out_grad = to_owner(out_total)
    in_grad = in_weight_rows(inner_part.astype(bf16), gate_part.astype(bf16))
    edge = select_weight.shape[1]
    select_grad = pack_own[:, :edge]
    beta_weight_grad = pack_own[:, edge : edge + rank]
    edge += rank
    conv_weight_grad = pack_own[:, edge : edge + taps]
    conv_bias_grad = pack_own[:, edge + taps]
    beta_bias_grad = pack_own[:, edge + taps + 1]
    skip_grad = pack_own[:, edge + taps + 2]
    gain_grad = pack_own[: model // 2 // count, edge + taps + 3]

    return (
        layer_out,
        token_grad[None],
        gain_grad,
        in_grad,
        conv_weight_grad,
        conv_bias_grad,
        select_grad,
        beta_weight_grad,
        beta_bias_grad,
        skip_grad,
        out_grad,
    )


def solution(mesh):
    devices = mesh.devices
    parts = jax.sharding.Mesh(
        devices.reshape(devices.shape[0] // group, group, devices.shape[1]),
        ("outer", "member", "fsdp"),
    )
    everything = ("outer", "member", "fsdp")
    tokens = P("fsdp", seq, None)
    vector, matrix = P("fsdp"), P("fsdp", None)
    owned, owned_rows = P(everything), P(everything, None)
    in_specs = (
        tokens,
        tokens,
        vector,
        matrix,
        matrix,
        vector,
        matrix,
        matrix,
        vector,
        vector,
        matrix,
    )
    out_specs = (
        tokens,
        tokens,
        owned,
        owned_rows,
        owned_rows,
        owned,
        owned_rows,
        owned_rows,
        owned,
        owned,
        owned_rows,
    )
    return jax.shard_map(
        local, mesh=parts, in_specs=in_specs, out_specs=out_specs, check_vma=False
    )
```
